32 devices in a mesh: batch: 4 (over x, core), seq: 8 (over z, y).
Axes of the slice: x: 2, y: 2, z: 4, core: 2. Of those that a mesh axis runs over, the one named last changes fastest.
Arguments:
- tokens: bfloat16 [4, 2560, 512], P('batch', 'seq'), may hold values from -6 to 6
- norm_gains: float32 [2, 2, 512], replicated, may hold values from 0.25 to 1.75
- qkv_weight: bfloat16 [2, 512, 1536], replicated, may hold values from -0.25 to 0.25
- out_weight: bfloat16 [2, 512, 512], replicated, may hold values from -3.5 to 3.5
- up_weight: bfloat16 [2, 512, 2048], replicated, may hold values from -0.25 to 0.25
- down_weight: bfloat16 [2, 2048, 512], replicated, may hold values from -0.125 to 0.125
- gen_cotangent: bfloat16 [4, 2560, 512], P('batch', 'seq'), may hold values from -6 to 6
- disc_cotangent: bfloat16 [4, 2560, 512], P('batch', 'seq'), may hold values from -6 to 6
- seg_lengths: int32 [4, 4], P('batch'), may hold values from 0 to 2558, as said below
Outputs:
- gen_out: bfloat16 [4, 2560, 512], P('batch', 'seq')
- disc_out: bfloat16 [4, 2560, 512], P('batch', 'seq')
- gen_in_grad: bfloat16 [4, 2560, 512], P('batch', 'seq')
- disc_in_grad: bfloat16 [4, 2560, 512], P('batch', 'seq')
- gain_grad: float32 [2, 2, 512], replicated
- qkv_grad: float32 [2, 512, 1536], replicated
- out_grad: float32 [2, 512, 512], replicated
- up_grad: float32 [2, 512, 2048], replicated
- down_grad: float32 [2, 2048, 512], replicated
The draws below stay inside these ranges and needn't reach their ends.
Inputs may be any that keep to these rules, and one draw needn't show every extreme that they name: `seg_lengths`: each row holds, for one pack, the lengths of a leading thumbnail (1 to min(256, 160) tokens), of one image, of a trailing thumbnail (1 to half of that) and of the padding (0 to a quarter of it), in this order; they sum to 2560. The image starts in the first band of seq and ends in the last. In one pack of each draw both thumbnails have one token and there is no padding.
All inputs are finite; a program needn't handle non-finite values.
Results may differ from the reference program's by a relative error of at most 0.015.
Values may be sent and summed in bfloat16 or wider, within the bound.
A program may use at most 320 MiB of HBM per device.

```python
import functools
import math
import jax
import jax.numpy as jnp
from jax import lax

D = 512
HEADS = 8
FF = 2048
HEAD = 64
TOK_DEV = 320
THUMB = 256
PACK = 2560
PACKS = 4


def draw_seg_lengths(key, part):
    key = jax.random.fold_in(key, 11)
    head_key, tail_key, fill_key, pick_key = jax.random.split(key, 4)
    limit = min(THUMB, TOK_DEV // 2)
    leading = jax.random.randint(head_key, (PACKS,), 1, limit + 1)
    trailing = jax.random.randint(tail_key, (PACKS,), 1, limit // 2 + 1)
    padding = jax.random.randint(fill_key, (PACKS,), 0, limit // 4 + 1)
    chosen = jax.random.randint(pick_key, (), 0, PACKS)
    picked = jnp.arange(PACKS, dtype=jnp.int32) == chosen
    leading = jnp.where(picked, 1, leading)
    trailing = jnp.where(picked, 1, trailing)
    padding = jnp.where(picked, 0, padding)
    image = PACK - leading - trailing - padding
    return jnp.stack([leading, image, trailing, padding], axis=-1).astype(jnp.int32)


def block_levels(stream_key, shape, cuts, least, top_value):
    def one(axis_at, blocks):
        draws = jax.random.uniform(jax.random.fold_in(jax.random.fold_in(stream_key, 6), axis_at), (blocks,), jnp.float32, least / len(cuts), top_value / len(cuts))
        return jnp.repeat(jnp.exp(draws), shape[axis_at] // blocks).reshape((-1,) + (1,) * (len(shape) - axis_at - 1))

    loudness = one(*cuts[0])
    for cut in cuts[1:]:
        loudness = loudness * one(*cut)
    return loudness


def noise(key, shape, deviation, most, shards=(), held_as=jnp.bfloat16):
    array = deviation * jax.random.normal(key, shape, jnp.float32)
    if shards:
        array = array * block_levels(key, shape, shards, -0.22, 0.18)
    return jnp.clip(array, -most, most).astype(held_as)


def setup_inputs(seed: int = 0) -> dict:
    key_of = jax.random.split(jax.random.key(seed), 10)
    return {
        "tokens": noise(key_of[0], (PACKS, PACK, D), 1.0, 6.0, ((0, 4), (1, 8))),
        "norm_gains": jnp.clip(1.0 + 0.15 * jax.random.normal(key_of[1], (2, 2, D), jnp.float32), 0.25, 1.75),
        "qkv_weight": noise(key_of[2], (2, D, 3 * D), D ** -0.5, 0.25),
        "out_weight": noise(key_of[3], (2, D, D), (max(1, D * 16 // PACK)) ** -0.5, 3.5),
        "up_weight": noise(key_of[4], (2, D, FF), D ** -0.5, 0.25),
        "down_weight": noise(key_of[5], (2, FF, D), FF ** -0.5, 0.125),
        "gen_cotangent": noise(key_of[6], (PACKS, PACK, D), 1.0, 6.0, ((0, 4), (1, 8))),
        "disc_cotangent": noise(key_of[7], (PACKS, PACK, D), 1.0, 6.0, ((0, 4), (1, 8))),
        "seg_lengths": draw_seg_lengths(jax.random.fold_in(key_of[9], 71), 0),
    }


@jax.custom_vjp
def low(v):
    return lax.optimization_barrier(v.astype(jnp.bfloat16)).astype(jnp.float32)

@jax.custom_vjp
def low_back(v):
    return v

def low_keep(v):
    return (low(v), None)

def low_pass(kept, grad):
    return (grad,)

def back_keep(v):
    return (v, None)

def back_low(kept, grad):
    return (low(grad),)
low.defvjp(low_keep, low_pass)
low_back.defvjp(back_keep, back_low)
highest = lax.Precision.HIGHEST
epsilon = 1e-05
masked_score = -1e+30

def layer_norm(inputs, gain_row):
    average = lax.optimization_barrier(jnp.mean(inputs, axis=-1, keepdims=True))
    centred = inputs - average
    variance = lax.optimization_barrier(jnp.mean(centred * centred, axis=-1, keepdims=True))
    return centred * lax.rsqrt(variance + epsilon) * gain_row

def gelu_tanh(inputs):
    return 0.5 * inputs * (1.0 + jnp.tanh(0.7978845608028654 * (inputs + 0.044715 * inputs * inputs * inputs)))

def segment_of(lengths, positions):
    first = lengths[0]
    second = first + lengths[1]
    third = second + lengths[2]
    return (positions >= first).astype(jnp.int32) + (positions >= second).astype(jnp.int32) + (positions >= third).astype(jnp.int32)

def attend_block(key_heads, value_heads, key_segment, query_part):
    query_heads, query_segment = query_part
    scores = jnp.einsum('qhe,khe->hqk', query_heads, key_heads, precision=highest) * HEAD ** (-0.5)
    allowed = query_segment[:, None] == key_segment[None, :]
    scores = low_back(jnp.where(allowed[None], scores, masked_score))
    row_max = lax.optimization_barrier(jnp.max(scores, axis=-1, keepdims=True))
    log_total = row_max + jnp.log(lax.optimization_barrier(jnp.sum(jnp.exp(scores - row_max), axis=-1, keepdims=True)))
    weights = low(jnp.exp(scores - log_total))
    return jnp.einsum('hqk,khe->qhe', weights, value_heads, precision=highest)

def block_pack(inputs, gains, qkv_matrix, out_matrix, up_matrix, down_matrix, lengths):
    positions = jnp.arange(PACK, dtype=jnp.int32)
    segment = segment_of(lengths, positions)
    keep_rows = (segment < 3).astype(inputs.dtype)[:, None]
    normed = low(layer_norm(inputs, gains[0]))
    qkv_rows = low_back(low(jnp.dot(normed, qkv_matrix, precision=highest, preferred_element_type=jnp.float32)))
    query_heads = qkv_rows[:, :D].reshape(PACK, HEADS, HEAD)
    key_heads = qkv_rows[:, D:2 * D].reshape(PACK, HEADS, HEAD)
    value_heads = qkv_rows[:, 2 * D:].reshape(PACK, HEADS, HEAD)
    block_rows = math.gcd(PACK, 512)
    attended = lax.map(jax.checkpoint(functools.partial(attend_block, key_heads, value_heads, segment)), (query_heads.reshape(PACK // block_rows, block_rows, HEADS, HEAD), segment.reshape(PACK // block_rows, block_rows)))
    attended = low_back(low(attended.reshape(PACK, D) * keep_rows))
    middle = inputs + low_back(jnp.dot(attended, out_matrix, precision=highest, preferred_element_type=jnp.float32))
    second_norm = low(layer_norm(middle, gains[1]))
    up_rows = low_back(jnp.dot(second_norm, up_matrix, precision=highest, preferred_element_type=jnp.float32))
    hidden = low_back(low(gelu_tanh(up_rows)))
    return middle + low_back(jnp.dot(hidden, down_matrix, precision=highest, preferred_element_type=jnp.float32))

def forward(inputs, gains, qkv_matrix, out_matrix, up_matrix, down_matrix, seg_lengths):
    return jnp.stack([block_pack(inputs[number], gains, qkv_matrix, out_matrix, up_matrix, down_matrix, seg_lengths[number]) for number in range(PACKS)])

def reference(tokens, norm_gains, qkv_weight, out_weight, up_weight, down_weight, gen_cotangent, disc_cotangent, seg_lengths):
    params = [norm_gains.astype(jnp.float32), qkv_weight.astype(jnp.float32), out_weight.astype(jnp.float32), up_weight.astype(jnp.float32), down_weight.astype(jnp.float32)]
    runner = functools.partial(forward, seg_lengths=seg_lengths)
    gen_rows, gen_back = jax.vjp(runner, tokens.astype(jnp.float32), *[param[0] for param in params])
    gen_out = gen_rows.astype(jnp.bfloat16)
    disc_rows, disc_back = jax.vjp(runner, gen_out.astype(jnp.float32), *[param[1] for param in params])
    gen_grads = gen_back(gen_cotangent.astype(jnp.float32))
    disc_grads = disc_back(disc_cotangent.astype(jnp.float32))
    stacked = [jnp.stack([gen_grads[number + 1], disc_grads[number + 1]]) for number in range(5)]
    return (gen_out, disc_rows.astype(jnp.bfloat16), gen_grads[0].astype(jnp.bfloat16), disc_grads[0].astype(jnp.bfloat16), stacked[0], stacked[1], stacked[2], stacked[3], stacked[4])
```

```python
import functools
import math

import jax
import jax.numpy as jnp
from jax import lax
from jax.experimental import pallas as pl
from jax.experimental.pallas import tpu as pltpu
from jax.sharding import PartitionSpec as P

HEADS = 8


epsilon = 1e-05
masked_score = -1e30
key_block = 2048


def layer_norm(inputs, gain_row):
    average = jnp.mean(inputs, axis=-1, keepdims=True)
    centred = inputs - average
    variance = jnp.mean(centred * centred, axis=-1, keepdims=True)
    return centred * lax.rsqrt(variance + epsilon) * gain_row


def gelu_tanh(inputs):
    return (
        0.5
        * inputs
        * (1.0 + jnp.tanh(0.7978845608028654 * (inputs + 0.044715 * inputs * inputs * inputs)))
    )


def segment_of(lengths, positions):
    first = lengths[0]
    second = first + lengths[1]
    third = second + lengths[2]
    return (
        (positions >= first).astype(jnp.int32)
        + (positions >= second).astype(jnp.int32)
        + (positions >= third).astype(jnp.int32)
    )


def block_scores(query_heads, key_heads, query_segment, key_segment, scale):
    scores = (
        jnp.einsum("qhe,khe->hqk", query_heads, key_heads, preferred_element_type=jnp.float32)
        * scale
    )
    allowed = query_segment[:, None] == key_segment[None, :]
    return jnp.where(allowed[None], scores, masked_score)


def split_blocks(array_rows, width):
    return array_rows.reshape((array_rows.shape[0] // width, width) + array_rows.shape[1:])


def attend(query_heads, key_heads, value_heads, query_segment, key_segment, scale):
    width = math.gcd(key_heads.shape[0], key_block)
    blocks = (
        split_blocks(key_heads, width),
        split_blocks(value_heads, width),
        split_blocks(key_segment, width),
    )
    heads = query_heads.shape[1]
    row_count = query_heads.shape[0]

    def statistics(carry, item):
        row_max, totals = carry
        scores = block_scores(query_heads, item[0], query_segment, item[2], scale)
        new_max = jnp.maximum(row_max, jnp.max(scores, axis=-1))
        totals = totals * jnp.exp(row_max - new_max) + jnp.sum(
            jnp.exp(scores - new_max[..., None]), axis=-1
        )
        return ((new_max, totals), None)

    start_max = jnp.full((heads, row_count), masked_score, jnp.float32)
    (row_max, totals), unused = lax.scan(
        statistics, (start_max, jnp.zeros((heads, row_count), jnp.float32)), blocks
    )
    log_total = row_max + jnp.log(totals)

    def weighted(running, item):
        scores = block_scores(query_heads, item[0], query_segment, item[2], scale)
        weights_low = jnp.exp(scores - log_total[..., None]).astype(jnp.bfloat16)
        return (
            running
            + jnp.einsum("hqk,khe->qhe", weights_low, item[1], preferred_element_type=jnp.float32),
            None,
        )

    attended, unused = lax.scan(weighted, jnp.zeros(query_heads.shape, jnp.float32), blocks)
    return (attended, log_total)


def query_side(
    query_heads,
    key_heads,
    value_heads,
    query_segment,
    key_segment,
    grad_heads,
    log_total,
    delta,
    scale,
):
    width = math.gcd(key_heads.shape[0], key_block)
    blocks = (
        split_blocks(key_heads, width),
        split_blocks(value_heads, width),
        split_blocks(key_segment, width),
    )

    def step(running, item):
        scores = block_scores(query_heads, item[0], query_segment, item[2], scale)
        weights = jnp.exp(scores - log_total[..., None])
        dprobs = jnp.einsum("qhe,khe->hqk", grad_heads, item[1], preferred_element_type=jnp.float32)
        dscores = (weights * (dprobs - delta[..., None])).astype(jnp.bfloat16)
        running = running + jnp.einsum(
            "hqk,khe->qhe", dscores, item[0], preferred_element_type=jnp.float32
        )
        key_part = (
            jnp.einsum("hqk,qhe->khe", dscores, query_heads, preferred_element_type=jnp.float32)
            * scale
        )
        value_part = jnp.einsum(
            "hqk,qhe->khe",
            weights.astype(jnp.bfloat16),
            grad_heads,
            preferred_element_type=jnp.float32,
        )
        return (running, (key_part, value_part))

    grad_query, key_parts = lax.scan(step, jnp.zeros(query_heads.shape, jnp.float32), blocks)
    return (grad_query * scale, key_parts)


def block_forward(inputs, gains, qkv_matrix, out_matrix, up_matrix, down_matrix, lengths):
    row_count, width = inputs.shape
    heads = HEADS
    head_size = width // heads
    scale = head_size ** (-0.5)
    band_index = lax.axis_index("seq")
    positions = band_index * row_count + jnp.arange(row_count, dtype=jnp.int32)
    query_segment = segment_of(lengths, positions)
    key_segment = segment_of(lengths, jnp.arange(row_count * lax.axis_size("seq"), dtype=jnp.int32))
    keep_rows = (query_segment < 3).astype(jnp.float32)[:, None]
    normed = layer_norm(inputs, gains[0]).astype(jnp.bfloat16)
    qkv_rows = jnp.dot(normed, qkv_matrix, preferred_element_type=jnp.float32).astype(jnp.bfloat16)
    all_keys, all_values = (
        lax.all_gather(qkv_rows[:, width : 2 * width], "seq", axis=0, tiled=True),
        lax.all_gather(qkv_rows[:, 2 * width :], "seq", axis=0, tiled=True),
    )
    attended, log_total = attend(
        qkv_rows[:, :width].reshape(row_count, heads, head_size),
        all_keys.reshape(-1, heads, head_size),
        all_values.reshape(-1, heads, head_size),
        query_segment,
        key_segment,
        scale,
    )
    attended = attended.reshape(row_count, width)
    attended_low = (attended * keep_rows).astype(jnp.bfloat16)
    middle = inputs + jnp.dot(attended_low, out_matrix, preferred_element_type=jnp.float32)
    second_norm = layer_norm(middle, gains[1]).astype(jnp.bfloat16)
    up_rows = jnp.dot(second_norm, up_matrix, preferred_element_type=jnp.float32)
    hidden = gelu_tanh(up_rows).astype(jnp.bfloat16)
    outputs = middle + jnp.dot(hidden, down_matrix, preferred_element_type=jnp.float32)
    kept = (
        inputs,
        normed,
        qkv_rows,
        None,
        attended,
        log_total,
        attended_low,
        middle,
        second_norm,
        up_rows,
        hidden,
        query_segment,
        key_segment,
        keep_rows,
        lengths,
    )
    return (outputs, kept)


def block_backward(kept, grad_out, gains, qkv_matrix, out_matrix, up_matrix, down_matrix):
    (
        inputs,
        normed,
        qkv_rows,
        gathered,
        attended,
        log_total,
        attended_low,
        middle,
        second_norm,
        up_rows,
        hidden,
        query_segment,
        key_segment,
        keep_rows,
        lengths,
    ) = kept
    row_count, width = inputs.shape
    heads = HEADS
    head_size = width // heads
    scale = head_size ** (-0.5)
    grad_down = jnp.einsum("tf,td->fd", hidden, grad_out, preferred_element_type=jnp.float32)
    grad_hidden = jnp.einsum("td,fd->tf", grad_out, down_matrix, preferred_element_type=jnp.float32)
    unused, gelu_back = jax.vjp(gelu_tanh, up_rows)
    grad_up_rows = gelu_back(grad_hidden)[0].astype(jnp.bfloat16)
    grad_up = jnp.einsum("td,tf->df", second_norm, grad_up_rows, preferred_element_type=jnp.float32)
    grad_second = jnp.einsum(
        "tf,df->td", grad_up_rows, up_matrix, preferred_element_type=jnp.float32
    )
    unused, second_back = jax.vjp(layer_norm, middle, gains[1])
    middle_part, gain_second = second_back(grad_second)
    grad_middle = grad_out.astype(jnp.float32) + middle_part
    grad_branch = grad_middle.astype(jnp.bfloat16)
    grad_outw = jnp.einsum(
        "td,te->de", attended_low, grad_branch, preferred_element_type=jnp.float32
    )
    grad_attended = jnp.einsum(
        "te,de->td", grad_branch, out_matrix, preferred_element_type=jnp.float32
    ).astype(jnp.bfloat16) * keep_rows.astype(jnp.bfloat16)
    grad_heads = grad_attended.reshape(row_count, heads, head_size)
    delta = jnp.sum(
        grad_heads.astype(jnp.float32) * attended.reshape(row_count, heads, head_size), axis=-1
    ).T
    query_heads = qkv_rows[:, :width].reshape(row_count, heads, head_size)
    all_keys, all_values = (
        lax.all_gather(qkv_rows[:, width : 2 * width], "seq", axis=0, tiled=True),
        lax.all_gather(qkv_rows[:, 2 * width :], "seq", axis=0, tiled=True),
    )
    key_heads = all_keys.reshape(-1, heads, head_size)
    value_heads = all_values.reshape(-1, heads, head_size)
    grad_query, key_parts = query_side(
        query_heads,
        key_heads,
        value_heads,
        query_segment,
        key_segment,
        grad_heads,
        log_total,
        delta,
        scale,
    )
    grad_keys, grad_values = (
        lax.psum_scatter(
            key_parts[0].reshape(-1, width).astype(jnp.bfloat16),
            "seq",
            scatter_dimension=0,
            tiled=True,
        ).astype(jnp.float32),
        lax.psum_scatter(
            key_parts[1].reshape(-1, width).astype(jnp.bfloat16),
            "seq",
            scatter_dimension=0,
            tiled=True,
        ).astype(jnp.float32),
    )
    grad_qkv_rows = jnp.concatenate(
        [grad_query.reshape(row_count, width), grad_keys, grad_values], axis=1
    ).astype(jnp.bfloat16)
    grad_qkv = jnp.einsum("td,tf->df", normed, grad_qkv_rows, preferred_element_type=jnp.float32)
    grad_first = jnp.einsum(
        "tf,df->td", grad_qkv_rows, qkv_matrix, preferred_element_type=jnp.float32
    )
    unused, first_back = jax.vjp(layer_norm, inputs, gains[0])
    input_part, gain_first = first_back(grad_first)
    grad_inputs = grad_middle + input_part
    return (
        grad_inputs,
        (jnp.stack([gain_first, gain_second]), grad_qkv, grad_outw, grad_up, grad_down),
    )


def local_scan(
    tokens,
    norm_gains,
    qkv_weight,
    out_weight,
    up_weight,
    down_weight,
    gen_cotangent,
    disc_cotangent,
    seg_lengths,
):
    gen_weights = (norm_gains[0], qkv_weight[0], out_weight[0], up_weight[0], down_weight[0])
    disc_weights = (norm_gains[1], qkv_weight[1], out_weight[1], up_weight[1], down_weight[1])
    gen_outs, disc_outs, gen_ins, disc_ins = ([], [], [], [])
    number = 0
    lengths = seg_lengths[number]
    gen_rows, gen_kept = block_forward(tokens[number].astype(jnp.float32), *gen_weights, lengths)
    gen_low = gen_rows.astype(jnp.bfloat16)
    disc_rows, disc_kept = block_forward(gen_low.astype(jnp.float32), *disc_weights, lengths)
    disc_grad_in, disc_terms = block_backward(disc_kept, disc_cotangent[number], *disc_weights)
    gen_grad_in, gen_terms = block_backward(gen_kept, gen_cotangent[number], *gen_weights)
    gen_outs.append(gen_low)
    disc_outs.append(disc_rows.astype(jnp.bfloat16))
    gen_ins.append(gen_grad_in.astype(jnp.bfloat16))
    disc_ins.append(disc_grad_in.astype(jnp.bfloat16))
    stacked = [jnp.stack([gen_terms[number], disc_terms[number]]) for number in range(5)]
    summed = lax.psum(
        (stacked[0], stacked[1], stacked[2], stacked[3], stacked[4]), ("batch", "seq")
    )
    return (
        jnp.stack(gen_outs),
        jnp.stack(disc_outs),
        jnp.stack(gen_ins),
        jnp.stack(disc_ins),
        summed[0],
        summed[1],
        summed[2],
        summed[3],
        summed[4],
    )


NN = (((1,), (0,)), ((), ()))
NT = (((1,), (1,)), ((), ()))
TN = (((0,), (0,)), ((), ()))
LOW = jnp.bfloat16
WIDE = jnp.float32
GROUP = 4
vmem_bytes = 62 << 20


def product(left, right, form):
    return lax.dot_general(left, right, form, preferred_element_type=WIDE)


def normalise(inputs):
    average = jnp.mean(inputs, axis=-1, keepdims=True)
    centred = inputs - average
    variance = jnp.mean(centred * centred, axis=-1, keepdims=True)
    inverse = lax.rsqrt(variance + epsilon)
    return (centred * inverse, inverse)


def normalise_back(hat, inverse, gain_row, grad):
    scaled = grad * gain_row
    first = jnp.mean(scaled, axis=-1, keepdims=True)
    second = jnp.mean(scaled * hat, axis=-1, keepdims=True)
    return inverse * (scaled - first - hat * second)


def segments(lengths, positions):
    first = lengths[0, 0]
    second = first + lengths[0, 1]
    third = second + lengths[0, 2]
    return (
        (positions >= first).astype(jnp.int32)
        + (positions >= second).astype(jnp.int32)
        + (positions >= third).astype(jnp.int32)
    )


def stacked_positions(band, rows):
    lanes = lax.broadcasted_iota(jnp.int32, (1, GROUP * rows), 1)
    for unused in range(1, GROUP):
        lanes = lanes - jnp.where(lanes >= rows, rows, 0)
    return lanes + band * rows


def head_lanes(rows, head_size):
    return lax.broadcasted_iota(jnp.int32, (rows, GROUP * head_size), 1) // head_size


def stack_heads(rows_group, lane_head):
    zero = jnp.zeros_like(rows_group)
    return jnp.concatenate(
        [jnp.where(lane_head == head, rows_group, zero) for head in range(GROUP)], axis=0
    )


def unstack_heads(stacked, lane_head, rows):
    total = jnp.where(lane_head == 0, stacked[:rows], 0.0)
    for head in range(1, GROUP):
        total = jnp.where(lane_head == head, stacked[head * rows : (head + 1) * rows], total)
    return total


def key_chunks(bands, rows):
    step = 2 if (bands - 2) % 2 == 0 else 1
    chunks = [(0, rows)]
    for at in range(1, bands - 1, step):
        chunks.append((at * rows, step * rows))
    chunks.append(((bands - 1) * rows, rows))
    return chunks


def forward_kernel(
    block,
    lengths,
    normed_all,
    inputs_ref,
    gains_ref,
    qkv_hbm,
    out_hbm,
    up_hbm,
    down_hbm,
    output_ref,
    next_ref,
    kv_ref,
    query_ref,
    weights_hbm,
    low_ref,
    attended_ref,
    inverse_ref,
    middle_ref,
    second_ref,
    hidden_ref,
    slope_ref,
    qkv_matrix,
    out_matrix,
    up_matrix,
    down_matrix,
    query_stack,
    scores_ref,
    weights_ref,
    load_sems,
    store_sems,
):
    loads = [
        pltpu.make_async_copy(source.at[block], target, load_sems.at[number])
        for number, (source, target) in enumerate(
            [
                (qkv_hbm, qkv_matrix),
                (out_hbm, out_matrix),
                (up_hbm, up_matrix),
                (down_hbm, down_matrix),
            ]
        )
    ]
    for load in loads:
        load.start()
    rows, width = inputs_ref.shape
    total = normed_all.shape[0]
    head_size = width // HEADS
    group_width = GROUP * head_size
    groups = width // group_width
    band = lax.axis_index("seq")
    lane_head = head_lanes(rows, head_size)
    chunks = key_chunks(total // rows, rows)
    image_query = segments(lengths, stacked_positions(band, rows))
    loads[0].wait()
    own = normed_all[pl.ds(pl.multiple_of(band * rows, rows), rows), :]
    query = product(own, qkv_matrix[:, :width], NN).astype(LOW)
    query = query * jnp.asarray(head_size ** (-0.5), LOW)
    query_ref[...] = query
    for group in range(groups):
        lanes = slice(group * group_width, (group + 1) * group_width)
        query_stack[group] = stack_heads(query[:, lanes], lane_head)
    kv_ref[...] = product(normed_all[...], qkv_matrix[:, width:], NN).astype(LOW)
    stores = []
    for group in range(groups):
        lanes = slice(group * group_width, (group + 1) * group_width)
        value_lanes = slice(width + group * group_width, width + (group + 1) * group_width)
        stack = query_stack[group]
        edge_max = None
        middle_max = None
        for number, (start, size) in enumerate(chunks):
            scores = product(kv_ref[start : start + size, lanes], stack, NT)
            edge = number in (0, len(chunks) - 1)
            if edge:
                positions = start + lax.broadcasted_iota(jnp.int32, (size, 1), 0)
                allowed = segments(lengths, positions) == image_query
                scores = jnp.where(allowed, scores, masked_score)
            scores_ref[start : start + size] = scores
            top = jnp.max(scores, axis=0, keepdims=True)
            if edge:
                edge_max = top if edge_max is None else jnp.maximum(edge_max, top)
            else:
                middle_max = top if middle_max is None else jnp.maximum(middle_max, top)
        is_image = image_query == 1
        row_max = jnp.maximum(edge_max, jnp.where(is_image, middle_max, masked_score))
        inner_max = jnp.where(is_image, row_max, -masked_score)
        totals = None
        gathered = None
        for number, (start, size) in enumerate(chunks):
            edge = number in (0, len(chunks) - 1)
            weights = jnp.exp(scores_ref[start : start + size] - (row_max if edge else inner_max))
            part = jnp.sum(weights, axis=0, keepdims=True)
            totals = part if totals is None else totals + part
            low = weights.astype(LOW)
            weights_ref[group, start : start + size] = low
            piece = product(low, kv_ref[start : start + size, value_lanes], TN)
            gathered = piece if gathered is None else gathered + piece
        store = pltpu.make_async_copy(
            weights_ref.at[group], weights_hbm.at[group], store_sems.at[group]
        )
        store.start()
        stores.append(store)
        columns = jnp.transpose(jnp.broadcast_to(1.0 / totals, (128, GROUP * rows)))
        inverse = jnp.concatenate([columns] * (group_width // 128), axis=1)
        attended_ref[:, lanes] = unstack_heads(gathered * inverse, lane_head, rows)
        inverse_ref[:, lanes] = unstack_heads(inverse, lane_head, rows)
    positions = band * rows + lax.broadcasted_iota(jnp.int32, (rows, 1), 0)
    keep_rows = (segments(lengths, positions) < 3).astype(WIDE)
    low = (attended_ref[...] * keep_rows).astype(LOW)
    low_ref[...] = low
    loads[1].wait()
    middle = inputs_ref[...].astype(WIDE) + product(low, out_matrix[...], NN)
    middle_ref[...] = middle
    hat, unused = normalise(middle)
    second = (hat * gains_ref[block, 1:2, :]).astype(LOW)
    second_ref[...] = second
    loads[2].wait()
    up_rows = product(second, up_matrix[...], NN)
    square = up_rows * up_rows
    bend = jnp.tanh(0.7978845608028654 * (up_rows + 0.044715 * square * up_rows))
    half = 0.5 * (1.0 + bend)
    hidden = (up_rows * half).astype(LOW)
    hidden_ref[...] = hidden
    slope_ref[...] = (
        half
        + 0.5
        * up_rows
        * (1.0 - bend * bend)
        * (0.7978845608028654 * (1.0 + (3 * 0.044715) * square))
    ).astype(LOW)
    loads[3].wait()
    output = (middle + product(hidden, down_matrix[...], NN)).astype(LOW)
    output_ref[...] = output
    if next_ref is not None:
        hat, unused = normalise(output.astype(WIDE))
        next_ref[...] = (hat * gains_ref[block + 1, 0:1, :]).astype(LOW)
    for store in stores:
        store.wait()


def backward_kernel(
    block,
    lengths,
    normed_all,
    grad_ref,
    gains_ref,
    kv_ref,
    query_ref,
    weights_hbm,
    low_ref,
    attended_ref,
    inverse_ref,
    middle_ref,
    second_ref,
    hidden_ref,
    slope_ref,
    qkv_hbm,
    out_hbm,
    up_hbm,
    down_hbm,
    terms_ref,
    gain_terms_ref,
    normed_grad_ref,
    query_grad_ref,
    middle_grad_ref,
    qkv_matrix,
    out_matrix,
    up_matrix,
    down_matrix,
    weights_ref,
    query_stack,
    grad_stack,
    kv_grad_ref,
    load_sems,
):
    loads = [
        pltpu.make_async_copy(source, target, load_sems.at[number])
        for number, (source, target) in enumerate(
            [
                (down_hbm.at[block], down_matrix),
                (up_hbm.at[block], up_matrix),
                (out_hbm.at[block], out_matrix),
                (weights_hbm, weights_ref),
                (qkv_hbm.at[block], qkv_matrix),
            ]
        )
    ]
    for load in loads:
        load.start()
    rows, width = grad_ref.shape
    total = normed_all.shape[0]
    head_size = width // HEADS
    group_width = GROUP * head_size
    groups = width // group_width
    band = lax.axis_index("seq")
    lane_head = head_lanes(rows, head_size)
    chunks = key_chunks(total // rows, rows)
    fan = hidden_ref.shape[1]
    qkv_at, out_at, up_at, down_at = 0, 3 * width, 4 * width, 4 * width + fan

    def put(at, value):
        for number in range(value.shape[1] // width):
            terms_ref[at + number * width : at + (number + 1) * width] = value[
                :, number * width : (number + 1) * width
            ].astype(LOW)

    grad = grad_ref[...]
    loads[0].wait()
    grad_hidden = product(grad, down_matrix[...], NT)
    grad_up = (grad_hidden * slope_ref[...].astype(WIDE)).astype(LOW)
    terms_ref[down_at : down_at + fan] = product(hidden_ref[...], grad, TN).astype(LOW)
    put(up_at, product(second_ref[...], grad_up, TN))
    loads[1].wait()
    grad_second = product(grad_up, up_matrix[...], NT)
    hat, inverse = normalise(middle_ref[...])
    gain_terms_ref[1:2, :] = jnp.sum(grad_second * hat, axis=0, keepdims=True)
    grad_middle = grad.astype(WIDE) + normalise_back(
        hat, inverse, gains_ref[block, 1:2, :], grad_second
    )
    middle_grad_ref[...] = grad_middle
    grad_branch = grad_middle.astype(LOW)
    put(out_at, product(low_ref[...], grad_branch, TN))
    positions = band * rows + lax.broadcasted_iota(jnp.int32, (rows, 1), 0)
    keep_rows = (segments(lengths, positions) < 3).astype(WIDE)
    loads[2].wait()
    grad_attended = product(grad_branch, out_matrix[...], NT) * keep_rows
    scaled = (grad_attended * inverse_ref[...]).astype(LOW)
    ones = jnp.ones((8, group_width), LOW)
    deltas = []
    for group in range(groups):
        lanes = slice(group * group_width, (group + 1) * group_width)
        query_stack[group] = stack_heads(query_ref[:, lanes], lane_head)
        stack = stack_heads(scaled[:, lanes], lane_head)
        grad_stack[group] = stack
        attended = attended_ref[:, lanes]
        dots = stack.astype(WIDE) * jnp.concatenate([attended] * GROUP, axis=0)
        high = dots.astype(LOW)
        rest = (dots - high.astype(WIDE)).astype(LOW)
        deltas.append((product(ones, high, NT) + product(ones, rest, NT))[0:1])
    loads[3].wait()
    query_grads = []
    for group in range(groups):
        lanes = slice(group * group_width, (group + 1) * group_width)
        value_lanes = slice(width + group * group_width, width + (group + 1) * group_width)
        collected = None
        for start, size in chunks:
            at = slice(start, start + size)
            low = weights_ref[group, at]
            grad_weights = product(kv_ref[at, value_lanes], grad_stack[group], NT)
            grad_scores = (low.astype(WIDE) * (grad_weights - deltas[group])).astype(LOW)
            kv_grad_ref[at, value_lanes] = product(low, grad_stack[group], NN).astype(LOW)
            kv_grad_ref[at, lanes] = product(grad_scores, query_stack[group], NN).astype(LOW)
            piece = product(grad_scores, kv_ref[at, lanes], TN)
            collected = piece if collected is None else collected + piece
        query_grads.append(unstack_heads(collected, lane_head, rows))
    query_grad = (jnp.concatenate(query_grads, axis=1) * head_size ** (-0.5)).astype(LOW)
    loads[4].wait()
    own = normed_all[pl.ds(pl.multiple_of(band * rows, rows), rows), :]
    normed_grad = product(kv_grad_ref[...], qkv_matrix[:, width:], NT)
    normed_grad_ref[...] = normed_grad.astype(LOW)
    query_part = product(query_grad, qkv_matrix[:, :width], NT)
    query_grad_ref[...] = query_part
    gain_terms_ref[0:1, :] = (
        jnp.sum(normed_grad * normed_all[...].astype(WIDE), axis=0, keepdims=True)
        + jnp.sum(query_part * own.astype(WIDE), axis=0, keepdims=True)
    ) / gains_ref[block, 0:1, :]
    put(qkv_at, product(own, query_grad, TN))
    put(qkv_at + width, product(normed_all[...], kv_grad_ref[...], TN))


def input_kernel(block, inputs_ref, gains_ref, summed_ref, query_grad_ref, middle_grad_ref, out_ref):
    hat, inverse = normalise(inputs_ref[...].astype(WIDE))
    grad = summed_ref[...].astype(WIDE) + query_grad_ref[...]
    out_ref[...] = (
        middle_grad_ref[...] + normalise_back(hat, inverse, gains_ref[block, 0:1, :], grad)
    ).astype(LOW)


whole = pl.BlockSpec(memory_space=pltpu.VMEM)
scalars = pl.BlockSpec(memory_space=pltpu.SMEM)
apart = pl.BlockSpec(memory_space=pl.ANY)


def weight_scratch(width, fan):
    return {
        "qkv": pltpu.VMEM((width, 3 * width), LOW),
        "out": pltpu.VMEM((width, width), LOW),
        "up": pltpu.VMEM((width, fan), LOW),
        "down": pltpu.VMEM((fan, width), LOW),
    }


def run_forward(block, lengths, normed_all, inputs, gains, matrices, last):
    rows, width = inputs.shape
    total = normed_all.shape[0]
    fan = matrices[2].shape[2]
    group_width = GROUP * width // HEADS
    groups = width // group_width
    shape = jax.ShapeDtypeStruct
    outs = [
        (shape((rows, width), LOW), whole),
        (shape((rows, width), LOW), whole),
        (shape((total, 2 * width), LOW), whole),
        (shape((rows, width), LOW), whole),
        (shape((groups, total, GROUP * rows), LOW), apart),
        (shape((rows, width), LOW), whole),
        (shape((rows, width), WIDE), whole),
        (shape((rows, width), WIDE), whole),
        (shape((rows, width), WIDE), whole),
        (shape((rows, width), LOW), whole),
        (shape((rows, fan), LOW), whole),
        (shape((rows, fan), LOW), whole),
    ]
    kernel = functools.partial(forward_kernel, block)
    if last:
        outs.pop(1)

        def kernel(*refs):
            forward_kernel(block, *refs[:9], None, *refs[9:])

    held = weight_scratch(width, fan)
    results = pl.pallas_call(
        kernel,
        out_shape=[out[0] for out in outs],
        in_specs=[scalars, whole, whole, whole, apart, apart, apart, apart],
        out_specs=[out[1] for out in outs],
        scratch_shapes=[
            held["qkv"],
            held["out"],
            held["up"],
            held["down"],
            pltpu.VMEM((groups, GROUP * rows, group_width), LOW),
            pltpu.VMEM((total, GROUP * rows), WIDE),
            pltpu.VMEM((groups, total, GROUP * rows), LOW),
            pltpu.SemaphoreType.DMA((4,)),
            pltpu.SemaphoreType.DMA((groups,)),
        ],
        compiler_params=pltpu.CompilerParams(vmem_limit_bytes=vmem_bytes),
        cost_estimate=pl.CostEstimate(flops=14 << 30, bytes_accessed=40 << 20, transcendentals=0),
        name="forward_part",
    )(lengths, normed_all, inputs, gains, *matrices)
    results = list(results)
    if last:
        results.insert(1, None)
    return results


def run_backward(block, lengths, normed_all, grad, gains, kept, matrices):
    rows, width = grad.shape
    total = normed_all.shape[0]
    fan = matrices[2].shape[2]
    group_width = GROUP * width // HEADS
    groups = width // group_width
    shape = jax.ShapeDtypeStruct
    terms = 4 * width + 2 * fan
    held = weight_scratch(width, fan)
    return pl.pallas_call(
        functools.partial(backward_kernel, block),
        out_shape=[
            shape((terms, width), LOW),
            shape((2, width), WIDE),
            shape((total, width), LOW),
            shape((rows, width), WIDE),
            shape((rows, width), WIDE),
        ],
        in_specs=[scalars, whole, whole, whole, whole, whole, apart] + [whole] * 7 + [apart] * 4,
        out_specs=[whole] * 5,
        scratch_shapes=[
            held["qkv"],
            held["out"],
            held["up"],
            held["down"],
            pltpu.VMEM((groups, total, GROUP * rows), LOW),
            pltpu.VMEM((groups, GROUP * rows, group_width), LOW),
            pltpu.VMEM((groups, GROUP * rows, group_width), LOW),
            pltpu.VMEM((total, 2 * width), LOW),
            pltpu.SemaphoreType.DMA((5,)),
        ],
        compiler_params=pltpu.CompilerParams(vmem_limit_bytes=vmem_bytes),
        cost_estimate=pl.CostEstimate(flops=28 << 30, bytes_accessed=40 << 20, transcendentals=0),
        name="backward_part",
    )(lengths, normed_all, grad, gains, *kept, *matrices)


def run_input(block, inputs, gains, summed, query_grad, middle_grad):
    return pl.pallas_call(
        functools.partial(input_kernel, block),
        out_shape=jax.ShapeDtypeStruct(inputs.shape, LOW),
        in_specs=[whole] * 5,
        out_specs=whole,
        compiler_params=pltpu.CompilerParams(vmem_limit_bytes=vmem_bytes),
        name="input_part",
    )(inputs, gains, summed, query_grad, middle_grad)


def local_kernels(
    tokens,
    norm_gains,
    qkv_weight,
    out_weight,
    up_weight,
    down_weight,
    gen_cotangent,
    disc_cotangent,
    seg_lengths,
):
    matrices = (qkv_weight, out_weight, up_weight, down_weight)
    inputs = tokens[0]
    normed = layer_norm(inputs.astype(WIDE), norm_gains[0, 0]).astype(LOW)
    terms, gain_terms, outs, ins = ([], [], [], [])
    for block, grad in enumerate((gen_cotangent[0], disc_cotangent[0])):
        normed_all = lax.all_gather(normed, "seq", axis=0, tiled=True)
        output, normed, *kept = run_forward(
            block, seg_lengths, normed_all, inputs, norm_gains, matrices, block == 1
        )
        part, gain_part, normed_grad, query_grad, middle_grad = run_backward(
            block, seg_lengths, normed_all, grad, norm_gains, kept, matrices
        )
        summed = lax.psum_scatter(normed_grad, "seq", scatter_dimension=0, tiled=True)
        ins.append(run_input(block, inputs, norm_gains, summed, query_grad, middle_grad))
        outs.append(output)
        terms.append(lax.psum(part, ("batch", "seq")))
        gain_terms.append(gain_part)
        inputs = output
    width, fan = up_weight.shape[1:]

    def columns(at, count):
        return jnp.stack(
            [
                jnp.concatenate(
                    [term[at + n * width : at + (n + 1) * width] for n in range(count)], axis=1
                ).astype(WIDE)
                for term in terms
            ]
        )

    down_at = 4 * width + fan
    return (
        outs[0][None],
        outs[1][None],
        ins[0][None],
        ins[1][None],
        lax.psum(jnp.stack(gain_terms), ("batch", "seq")),
        columns(0, 3),
        columns(3 * width, 1),
        columns(4 * width, fan // width),
        jnp.stack([term[down_at : down_at + fan] for term in terms]).astype(WIDE),
    )


def solution(mesh):
    placed = (
        P("batch", "seq", None),
        P(),
        P(),
        P(),
        P(),
        P(),
        P("batch", "seq", None),
        P("batch", "seq", None),
        P("batch", None),
    )
    small = mesh.shape["seq"] <= 8
    return jax.shard_map(
        local_kernels if small else local_scan,
        mesh=mesh,
        in_specs=placed,
        out_specs=(
            P("batch", "seq", None),
            P("batch", "seq", None),
            P("batch", "seq", None),
            P("batch", "seq", None),
            P(),
            P(),
            P(),
            P(),
            P(),
        ),
        check_vma=False,
    )
```

```python
import functools
import math

import jax
import jax.numpy as jnp
from jax import lax
from jax.experimental import pallas as pl
from jax.experimental.pallas import tpu as pltpu
from jax.sharding import PartitionSpec as P

HEADS = 8


epsilon = 1e-05
masked_score = -1e30
key_block = 2048


def layer_norm(inputs, gain_row):
    average = jnp.mean(inputs, axis=-1, keepdims=True)
    centred = inputs - average
    variance = jnp.mean(centred * centred, axis=-1, keepdims=True)
    return centred * lax.rsqrt(variance + epsilon) * gain_row


def gelu_tanh(inputs):
    return (
        0.5
        * inputs
        * (1.0 + jnp.tanh(0.7978845608028654 * (inputs + 0.044715 * inputs * inputs * inputs)))
    )


def segment_of(lengths, positions):
    first = lengths[0]
    second = first + lengths[1]
    third = second + lengths[2]
    return (
        (positions >= first).astype(jnp.int32)
        + (positions >= second).astype(jnp.int32)
        + (positions >= third).astype(jnp.int32)
    )


def block_scores(query_heads, key_heads, query_segment, key_segment, scale):
    scores = (
        jnp.einsum("qhe,khe->hqk", query_heads, key_heads, preferred_element_type=jnp.float32)
        * scale
    )
    allowed = query_segment[:, None] == key_segment[None, :]
    return jnp.where(allowed[None], scores, masked_score)


def split_blocks(array_rows, width):
    return array_rows.reshape((array_rows.shape[0] // width, width) + array_rows.shape[1:])


def attend(query_heads, key_heads, value_heads, query_segment, key_segment, scale):
    width = math.gcd(key_heads.shape[0], key_block)
    blocks = (
        split_blocks(key_heads, width),
        split_blocks(value_heads, width),
        split_blocks(key_segment, width),
    )
    heads = query_heads.shape[1]
    row_count = query_heads.shape[0]

    def statistics(carry, item):
        row_max, totals = carry
        scores = block_scores(query_heads, item[0], query_segment, item[2], scale)
        new_max = jnp.maximum(row_max, jnp.max(scores, axis=-1))
        totals = totals * jnp.exp(row_max - new_max) + jnp.sum(
            jnp.exp(scores - new_max[..., None]), axis=-1
        )
        return ((new_max, totals), None)

    start_max = jnp.full((heads, row_count), masked_score, jnp.float32)
    (row_max, totals), unused = lax.scan(
        statistics, (start_max, jnp.zeros((heads, row_count), jnp.float32)), blocks
    )
    log_total = row_max + jnp.log(totals)

    def weighted(running, item):
        scores = block_scores(query_heads, item[0], query_segment, item[2], scale)
        weights_low = jnp.exp(scores - log_total[..., None]).astype(jnp.bfloat16)
        return (
            running
            + jnp.einsum("hqk,khe->qhe", weights_low, item[1], preferred_element_type=jnp.float32),
            None,
        )

    attended, unused = lax.scan(weighted, jnp.zeros(query_heads.shape, jnp.float32), blocks)
    return (attended, log_total)


def query_side(
    query_heads,
    key_heads,
    value_heads,
    query_segment,
    key_segment,
    grad_heads,
    log_total,
    delta,
    scale,
):
    width = math.gcd(key_heads.shape[0], key_block)
    blocks = (
        split_blocks(key_heads, width),
        split_blocks(value_heads, width),
        split_blocks(key_segment, width),
    )

    def step(running, item):
        scores = block_scores(query_heads, item[0], query_segment, item[2], scale)
        weights = jnp.exp(scores - log_total[..., None])
        dprobs = jnp.einsum("qhe,khe->hqk", grad_heads, item[1], preferred_element_type=jnp.float32)
        dscores = (weights * (dprobs - delta[..., None])).astype(jnp.bfloat16)
        running = running + jnp.einsum(
            "hqk,khe->qhe", dscores, item[0], preferred_element_type=jnp.float32
        )
        key_part = (
            jnp.einsum("hqk,qhe->khe", dscores, query_heads, preferred_element_type=jnp.float32)
            * scale
        )
        value_part = jnp.einsum(
            "hqk,qhe->khe",
            weights.astype(jnp.bfloat16),
            grad_heads,
            preferred_element_type=jnp.float32,
        )
        return (running, (key_part, value_part))

    grad_query, key_parts = lax.scan(step, jnp.zeros(query_heads.shape, jnp.float32), blocks)
    return (grad_query * scale, key_parts)


def block_forward(inputs, gains, qkv_matrix, out_matrix, up_matrix, down_matrix, lengths):
    row_count, width = inputs.shape
    heads = HEADS
    head_size = width // heads
    scale = head_size ** (-0.5)
    band_index = lax.axis_index("seq")
    positions = band_index * row_count + jnp.arange(row_count, dtype=jnp.int32)
    query_segment = segment_of(lengths, positions)
    key_segment = segment_of(lengths, jnp.arange(row_count * lax.axis_size("seq"), dtype=jnp.int32))
    keep_rows = (query_segment < 3).astype(jnp.float32)[:, None]
    normed = layer_norm(inputs, gains[0]).astype(jnp.bfloat16)
    qkv_rows = jnp.dot(normed, qkv_matrix, preferred_element_type=jnp.float32).astype(jnp.bfloat16)
    all_keys, all_values = (
        lax.all_gather(qkv_rows[:, width : 2 * width], "seq", axis=0, tiled=True),
        lax.all_gather(qkv_rows[:, 2 * width :], "seq", axis=0, tiled=True),
    )
    attended, log_total = attend(
        qkv_rows[:, :width].reshape(row_count, heads, head_size),
        all_keys.reshape(-1, heads, head_size),
        all_values.reshape(-1, heads, head_size),
        query_segment,
        key_segment,
        scale,
    )
    attended = attended.reshape(row_count, width)
    attended_low = (attended * keep_rows).astype(jnp.bfloat16)
    middle = inputs + jnp.dot(attended_low, out_matrix, preferred_element_type=jnp.float32)
    second_norm = layer_norm(middle, gains[1]).astype(jnp.bfloat16)
    up_rows = jnp.dot(second_norm, up_matrix, preferred_element_type=jnp.float32)
    hidden = gelu_tanh(up_rows).astype(jnp.bfloat16)
    outputs = middle + jnp.dot(hidden, down_matrix, preferred_element_type=jnp.float32)
    kept = (
        inputs,
        normed,
        qkv_rows,
        None,
        attended,
        log_total,
        attended_low,
        middle,
        second_norm,
        up_rows,
        hidden,
        query_segment,
        key_segment,
        keep_rows,
        lengths,
    )
    return (outputs, kept)


def block_backward(kept, grad_out, gains, qkv_matrix, out_matrix, up_matrix, down_matrix):
    (
        inputs,
        normed,
        qkv_rows,
        gathered,
        attended,
        log_total,
        attended_low,
        middle,
        second_norm,
        up_rows,
        hidden,
        query_segment,
        key_segment,
        keep_rows,
        lengths,
    ) = kept
    row_count, width = inputs.shape
    heads = HEADS
    head_size = width // heads
    scale = head_size ** (-0.5)
    grad_down = jnp.einsum("tf,td->fd", hidden, grad_out, preferred_element_type=jnp.float32)
    grad_hidden = jnp.einsum("td,fd->tf", grad_out, down_matrix, preferred_element_type=jnp.float32)
    unused, gelu_back = jax.vjp(gelu_tanh, up_rows)
    grad_up_rows = gelu_back(grad_hidden)[0].astype(jnp.bfloat16)
    grad_up = jnp.einsum("td,tf->df", second_norm, grad_up_rows, preferred_element_type=jnp.float32)
    grad_second = jnp.einsum(
        "tf,df->td", grad_up_rows, up_matrix, preferred_element_type=jnp.float32
    )
    unused, second_back = jax.vjp(layer_norm, middle, gains[1])
    middle_part, gain_second = second_back(grad_second)
    grad_middle = grad_out.astype(jnp.float32) + middle_part
    grad_branch = grad_middle.astype(jnp.bfloat16)
    grad_outw = jnp.einsum(
        "td,te->de", attended_low, grad_branch, preferred_element_type=jnp.float32
    )
    grad_attended = jnp.einsum(
        "te,de->td", grad_branch, out_matrix, preferred_element_type=jnp.float32
    ).astype(jnp.bfloat16) * keep_rows.astype(jnp.bfloat16)
    grad_heads = grad_attended.reshape(row_count, heads, head_size)
    delta = jnp.sum(
        grad_heads.astype(jnp.float32) * attended.reshape(row_count, heads, head_size), axis=-1
    ).T
    query_heads = qkv_rows[:, :width].reshape(row_count, heads, head_size)
    all_keys, all_values = (
        lax.all_gather(qkv_rows[:, width : 2 * width], "seq", axis=0, tiled=True),
        lax.all_gather(qkv_rows[:, 2 * width :], "seq", axis=0, tiled=True),
    )
    key_heads = all_keys.reshape(-1, heads, head_size)
    value_heads = all_values.reshape(-1, heads, head_size)
    grad_query, key_parts = query_side(
        query_heads,
        key_heads,
        value_heads,
        query_segment,
        key_segment,
        grad_heads,
        log_total,
        delta,
        scale,
    )
    grad_keys, grad_values = (
        lax.psum_scatter(
            key_parts[0].reshape(-1, width).astype(jnp.bfloat16),
            "seq",
            scatter_dimension=0,
            tiled=True,
        ).astype(jnp.float32),
        lax.psum_scatter(
            key_parts[1].reshape(-1, width).astype(jnp.bfloat16),
            "seq",
            scatter_dimension=0,
            tiled=True,
        ).astype(jnp.float32),
    )
    grad_qkv_rows = jnp.concatenate(
        [grad_query.reshape(row_count, width), grad_keys, grad_values], axis=1
    ).astype(jnp.bfloat16)
    grad_qkv = jnp.einsum("td,tf->df", normed, grad_qkv_rows, preferred_element_type=jnp.float32)
    grad_first = jnp.einsum(
        "tf,df->td", grad_qkv_rows, qkv_matrix, preferred_element_type=jnp.float32
    )
    unused, first_back = jax.vjp(layer_norm, inputs, gains[0])
    input_part, gain_first = first_back(grad_first)
    grad_inputs = grad_middle + input_part
    return (
        grad_inputs,
        (jnp.stack([gain_first, gain_second]), grad_qkv, grad_outw, grad_up, grad_down),
    )


def local_scan(
    tokens,
    norm_gains,
    qkv_weight,
    out_weight,
    up_weight,
    down_weight,
    gen_cotangent,
    disc_cotangent,
    seg_lengths,
):
    gen_weights = (norm_gains[0], qkv_weight[0], out_weight[0], up_weight[0], down_weight[0])
    disc_weights = (norm_gains[1], qkv_weight[1], out_weight[1], up_weight[1], down_weight[1])
    gen_outs, disc_outs, gen_ins, disc_ins = ([], [], [], [])
    number = 0
    lengths = seg_lengths[number]
    gen_rows, gen_kept = block_forward(tokens[number].astype(jnp.float32), *gen_weights, lengths)
    gen_low = gen_rows.astype(jnp.bfloat16)
    disc_rows, disc_kept = block_forward(gen_low.astype(jnp.float32), *disc_weights, lengths)
    disc_grad_in, disc_terms = block_backward(disc_kept, disc_cotangent[number], *disc_weights)
    gen_grad_in, gen_terms = block_backward(gen_kept, gen_cotangent[number], *gen_weights)
    gen_outs.append(gen_low)
    disc_outs.append(disc_rows.astype(jnp.bfloat16))
    gen_ins.append(gen_grad_in.astype(jnp.bfloat16))
    disc_ins.append(disc_grad_in.astype(jnp.bfloat16))
    stacked = [jnp.stack([gen_terms[number], disc_terms[number]]) for number in range(5)]
    summed = lax.psum(
        (stacked[0], stacked[1], stacked[2], stacked[3], stacked[4]), ("batch", "seq")
    )
    return (
        jnp.stack(gen_outs),
        jnp.stack(disc_outs),
        jnp.stack(gen_ins),
        jnp.stack(disc_ins),
        summed[0],
        summed[1],
        summed[2],
        summed[3],
        summed[4],
    )


NN = (((1,), (0,)), ((), ()))
NT = (((1,), (1,)), ((), ()))
TN = (((0,), (0,)), ((), ()))
LOW = jnp.bfloat16
WIDE = jnp.float32
GROUP = 4
vmem_bytes = 63 << 20


def product(left, right, form):
    return lax.dot_general(left, right, form, preferred_element_type=WIDE)


def normalise(inputs):
    average = jnp.mean(inputs, axis=-1, keepdims=True)
    centred = inputs - average
    variance = jnp.mean(centred * centred, axis=-1, keepdims=True)
    inverse = lax.rsqrt(variance + epsilon)
    return (centred * inverse, inverse)


def normalise_back(hat, inverse, gain_row, grad):
    scaled = grad * gain_row
    first = jnp.mean(scaled, axis=-1, keepdims=True)
    second = jnp.mean(scaled * hat, axis=-1, keepdims=True)
    return inverse * (scaled - first - hat * second)


def segments(lengths, positions):
    first = lengths[0, 0]
    second = first + lengths[0, 1]
    third = second + lengths[0, 2]
    return (
        (positions >= first).astype(jnp.int32)
        + (positions >= second).astype(jnp.int32)
        + (positions >= third).astype(jnp.int32)
    )


def stacked_positions(band, rows):
    lanes = lax.broadcasted_iota(jnp.int32, (1, GROUP * rows), 1)
    for unused in range(1, GROUP):
        lanes = lanes - jnp.where(lanes >= rows, rows, 0)
    return lanes + band * rows


def head_lanes(rows, head_size):
    return lax.broadcasted_iota(jnp.int32, (rows, GROUP * head_size), 1) // head_size


def stack_heads(rows_group, lane_head):
    zero = jnp.zeros_like(rows_group)
    return jnp.concatenate(
        [jnp.where(lane_head == head, rows_group, zero) for head in range(GROUP)], axis=0
    )


def unstack_heads(stacked, lane_head, rows):
    total = jnp.where(lane_head == 0, stacked[:rows], 0.0)
    for head in range(1, GROUP):
        total = jnp.where(lane_head == head, stacked[head * rows : (head + 1) * rows], total)
    return total


def key_chunks(bands, rows):
    step = 2 if (bands - 2) % 2 == 0 else 1
    chunks = [(0, rows)]
    for at in range(1, bands - 1, step):
        chunks.append((at * rows, step * rows))
    chunks.append(((bands - 1) * rows, rows))
    return chunks


class Moves:
    def __init__(self, sems):
        self.sems = sems
        self.pending = {}
        self.count = 0

    def start(self, key, source, target):
        copy = pltpu.make_async_copy(source, target, self.sems.at[self.count])
        copy.start()
        self.count += 1
        self.pending[key] = copy

    def wait(self, key):
        self.pending.pop(key).wait()


GRID = pl.DeviceIdType.MESH
CORE, EDGE_X, EDGE_Y, NEAR_Z, FAR_Z = (
    ("batch", 0),
    ("batch", 1),
    ("seq", 0),
    ("seq", 1),
    ("seq", 2),
)
ORDERS = (
    (CORE, EDGE_X, EDGE_Y, NEAR_Z, FAR_Z),
    (CORE, EDGE_Y, NEAR_Z, EDGE_X, FAR_Z),
    (CORE, NEAR_Z, EDGE_X, EDGE_Y, FAR_Z),
)
STEPS = 5
DEVICES = 1 << STEPS


def place():
    return (lax.axis_index("batch"), lax.axis_index("seq"))


def swapped(number):
    return 2 * lax.rem(number, 2) + number // 2


def band_here():
    batch, seq = place()
    return 2 * swapped(batch) + lax.rem(seq, 2)


def home():
    batch, seq = place()
    return (swapped(seq // 2), 2 * swapped(batch) + lax.rem(seq, 2))


def bit_of(axis, number):
    return lax.rem(lax.axis_index(axis) // (1 << number), 2)


def across(axis, number):
    batch, seq = place()
    step = (1 - 2 * bit_of(axis, number)) * (1 << number)
    return (batch + step, seq) if axis == "batch" else (batch, seq + step)


def announce(partners):
    for partner in partners:
        pl.semaphore_signal(
            pltpu.get_barrier_semaphore(), inc=1, device_id=partner, device_id_type=GRID
        )


def meet(count):
    pl.semaphore_wait(pltpu.get_barrier_semaphore(), count)


def aligned(at, size):
    return pl.ds(pl.multiple_of(at, 16), size)


class Copies:
    def __init__(self, sems):
        self.sems = sems
        self.known = {}
        self.count = 0

    def send(self, key, source, target, partner):
        number = self.count
        self.count += 1
        copy = pltpu.make_async_remote_copy(
            src_ref=source,
            dst_ref=target,
            send_sem=self.sems.at[0, number],
            recv_sem=self.sems.at[1, number],
            device_id=partner,
            device_id_type=GRID,
        )
        copy.start()
        self.known[key] = copy

    def arrive(self, key):
        self.known[key].wait_recv()

    def sent(self, keys):
        for key in keys:
            self.known.pop(key).wait_send()

    def close(self):
        for copy in self.known.values():
            copy.wait_send()


class Layout:
    def __init__(self, sizes):
        self.sizes = sizes
        self.starts = [sum(sizes[:number]) for number in range(len(sizes))]

    def base(self, number, step):
        at, size = (self.starts[number] // 2, self.sizes[number] // 2)
        for axis in ORDERS[number][1:step]:
            size = size // 2
            at = at + bit_of(*axis) * size
        return (at, size)

    def whole_base(self, number, step):
        at, size = self.base(number, step)
        start, half = self.starts[number], self.sizes[number] // 2
        return (at - start // 2 + start + bit_of(*CORE) * half, size)

    def part(self, number):
        return pl.ds(self.starts[number] // DEVICES, self.sizes[number] // DEVICES)


class Reduction:
    def __init__(self, sizes, source, part, held, landing, local_sems, sems, apart_first=False):
        self.layout = Layout(sizes)
        self.sizes = sizes
        self.source, self.part, self.held, self.landing = (source, part, held, landing)
        self.copies = Copies(sems)
        self.moves = Moves(local_sems)
        self.apart_first = apart_first

    def pieces(self, number, part):
        next_bit = bit_of(*ORDERS[number][1])
        piece = (1 - next_bit) if part == 0 else next_bit
        return (piece, self.sizes[number] // 4)

    def begin(self):
        for part in range(2):
            for number, size in enumerate(self.sizes):
                piece, quarter = self.pieces(number, part)
                at = self.layout.starts[number] + (1 - bit_of(*CORE)) * (size // 2)
                landing = self.layout.starts[number] // 2 + part * quarter
                self.copies.send(
                    (number, part),
                    self.source.at[aligned(at + piece * quarter, quarter)],
                    self.landing.at[pl.ds(landing, quarter)],
                    across(*CORE),
                )
        for number, size in enumerate(self.sizes):
            start = self.layout.starts[number]
            self.moves.start(
                number,
                self.source.at[aligned(start + bit_of(*CORE) * (size // 2), size // 2)],
                self.held.at[pl.ds(start // 2, size // 2)],
            )

    def first(self, number, part):
        piece, quarter = self.pieces(number, part)
        if part == 0:
            self.moves.wait(number)
        self.copies.arrive((number, part))
        start = self.layout.starts[number] // 2
        here = aligned(start + piece * quarter, quarter)
        self.held[here, :] = (
            self.held[here, :].astype(WIDE)
            + self.landing[pl.ds(start + part * quarter, quarter), :].astype(WIDE)
        ).astype(LOW)
        if part == 0:
            self.send(number, 1)

    def release(self):
        self.copies.sent([(number, part) for number in range(len(self.sizes)) for part in range(2)])

    def landed(self, number, step):
        start = sum(self.sizes) // 2
        for earlier in range(1, STEPS if self.apart_first and step == 1 else step):
            start += sum(self.sizes) >> (earlier + 1)
        return pl.ds(start + (self.layout.starts[number] >> (step + 1)), self.sizes[number] >> (step + 1))

    def send(self, number, step):
        axis = ORDERS[number][step]
        at, size = self.layout.base(number, step)
        size = size // 2
        self.copies.send(
            (number, "at", step),
            self.held.at[aligned(at + (1 - bit_of(*axis)) * size, size)],
            self.landing.at[self.landed(number, step)],
            across(*axis),
        )

    def add(self, number, step):
        at, size = self.layout.base(number, step + 1)
        self.copies.arrive((number, "at", step))
        summed = (
            self.held[aligned(at, size), :].astype(WIDE)
            + self.landing[self.landed(number, step), :].astype(WIDE)
        ).astype(LOW)
        if step + 1 < STEPS:
            self.held[aligned(at, size), :] = summed
            self.send(number, step + 1)
        else:
            self.part[self.layout.part(number), :] = summed
            if number == len(self.sizes) - 1:
                self.copies.close()

    def tasks(self):
        numbers = range(len(self.sizes))
        steps = [self.begin]
        steps += [functools.partial(self.first, number, part) for part in range(2) for number in numbers]
        steps += [
            functools.partial(self.add, number, step) for step in range(1, STEPS) for number in numbers
        ]
        return steps

    @staticmethod
    def scratch(sizes, apart_first):
        rows = sum(sizes)
        landing = sum(rows >> step for step in range(1, STEPS + 1))
        if apart_first:
            landing += rows >> 2
        return [
            pltpu.VMEM((rows // 2, 512), LOW),
            pltpu.VMEM((landing, 512), LOW),
            pltpu.SemaphoreType.DMA((len(sizes),)),
            pltpu.SemaphoreType.DMA((2, 6 * len(sizes))),
        ]


class Sharing:
    def __init__(self, sizes, part, total, local_sems, sems):
        self.layout = Layout(sizes)
        self.sizes = sizes
        self.part, self.total, self.local = (part, total, local_sems)
        self.met = False
        self.copies = Copies(sems)

    def rows(self, number, step):
        return aligned(*self.layout.whole_base(number, step))

    def stay(self, number):
        return pltpu.make_async_copy(
            self.part.at[self.layout.part(number)],
            self.total.at[self.rows(number, STEPS)],
            self.local.at[number],
        )

    def begin(self):
        for number in range(len(self.sizes)):
            self.stay(number).start()
        for number in range(len(self.sizes)):
            self.stay(number).wait()
            self.share(number, STEPS - 1)
            self.pass_on(number, STEPS)

    def share(self, number, step):
        rows = self.rows(number, step + 1)
        self.copies.send(
            (number, step),
            self.total.at[rows],
            self.total.at[rows],
            across(*ORDERS[number][step]),
        )

    def pass_on(self, number, step):
        if step == STEPS:
            rows = self.rows(number, STEPS)
        else:
            at, size = self.layout.whole_base(number, step)
            size = size // 2
            rows = aligned(at + (1 - bit_of(*ORDERS[number][step])) * size, size)
        self.copies.send(
            (number, "pass", step), self.total.at[rows], self.total.at[rows], across(*CORE)
        )

    def gather(self, number, step):
        self.copies.arrive((number, step))
        if step > 1:
            self.share(number, step - 1)
        self.pass_on(number, step)

    def core_began(self):
        if not self.met:
            self.met = True
            for number in range(len(self.sizes)):
                self.copies.arrive((number, "pass", STEPS))

    def end(self):
        self.core_began()
        for step in range(STEPS - 1, 0, -1):
            for number in range(len(self.sizes)):
                self.copies.arrive((number, "pass", step))
        self.copies.close()

    def tasks(self):
        steps = [self.begin]
        steps += [
            functools.partial(self.gather, number, step)
            for step in range(STEPS - 1, 0, -1)
            for number in range(len(self.sizes))
        ]
        return steps + [self.end]

    @staticmethod
    def scratch(sizes):
        return [
            pltpu.SemaphoreType.DMA((len(sizes),)),
            pltpu.SemaphoreType.DMA((2, 9 * len(sizes))),
        ]


class SmallSum:
    def __init__(self, total, landing, sems):
        self.total, self.landing = (total, landing)
        self.copies = Copies(sems)

    def send(self, step):
        self.copies.send(
            step, self.landing.at[STEPS + step], self.landing.at[step], across(*ORDERS[0][step])
        )

    def add(self, step):
        self.copies.arrive(step)
        summed = self.landing[STEPS + step] + self.landing[step]
        if step + 1 < STEPS:
            self.landing[STEPS + step + 1] = summed
            self.send(step + 1)
        else:
            self.total[...] = summed
            self.copies.close()

    def tasks(self):
        return [functools.partial(self.send, 0)] + [
            functools.partial(self.add, step) for step in range(STEPS)
        ]

    @staticmethod
    def scratch():
        return [
            pltpu.VMEM((2 * STEPS, 8, 512), WIDE),
            pltpu.SemaphoreType.DMA((2, STEPS)),
        ]


class Gathering:
    def __init__(self, whole_ref, rows, sems):
        self.whole, self.rows = (whole_ref, rows)
        self.copies = Copies(sems)
        self.band = band_here()
        self.x = self.band + 2 * (1 - 2 * bit_of(*EDGE_X))
        self.y = self.band + 1 - 2 * bit_of(*EDGE_Y)
        self.corner = self.x + self.y - self.band

    def send(self, key, band, axis, half=None):
        start, size = (band * self.rows, self.rows)
        if half is not None:
            size = size // 2
            start = start + half * size
        ref = self.whole.at[aligned(start, size)]
        self.copies.send(key, ref, ref, across(*axis))

    def begin(self):
        self.send("x", self.band, EDGE_X)
        self.send("y", self.band, EDGE_Y)
        self.send("core", self.band, CORE)

    def from_x(self):
        self.copies.arrive("x")
        self.send("corner 0", self.x, EDGE_Y, 0)
        self.send("core x", self.x, CORE)

    def from_y(self):
        self.copies.arrive("y")
        self.send("corner 1", self.y, EDGE_X, 1)
        self.send("core y", self.y, CORE)

    def from_corner(self, half):
        self.copies.arrive("corner %d" % half)
        self.send("core corner %d" % half, self.corner, CORE, half)

    def end(self):
        for key in ("core", "core x", "core y", "core corner 0", "core corner 1"):
            self.copies.arrive(key)
        self.copies.close()

    def tasks(self):
        corners = [functools.partial(self.from_corner, half) for half in range(2)]
        return [self.begin, self.from_x, self.from_y, *corners, self.end]

    @staticmethod
    def scratch():
        return [pltpu.SemaphoreType.DMA((2, 9))]


class Scattering:
    def __init__(self, source, held, landing, local_sems, sems, rows, finish):
        self.source, self.held, self.landing, self.rows, self.finish = (
            source,
            held,
            landing,
            rows,
            finish,
        )
        self.copies = Copies(sems)
        self.moves = Moves(local_sems)
        half = source.shape[1] // 2
        self.lanes = (slice(0, half), slice(half, 2 * half))

    def begin(self):
        size = 4 * self.rows
        self.copies.send(
            "core",
            self.source.at[aligned((1 - bit_of(*CORE)) * size, size)],
            self.landing.at[pl.ds(0, size)],
            across(*CORE),
        )
        self.moves.start("core", self.source.at[aligned(bit_of(*CORE) * size, size)], self.held)

    def first(self):
        rows = self.rows
        self.moves.wait("core")
        self.copies.arrive("core")
        self.held[...] = (
            self.held[...].astype(WIDE) + self.landing[pl.ds(0, 4 * rows), :].astype(WIDE)
        ).astype(LOW)
        x, y = (bit_of(*EDGE_X), bit_of(*EDGE_Y))
        self.copies.send(
            "x",
            self.held.at[aligned(2 * (1 - x) * rows, 2 * rows), self.lanes[0]],
            self.landing.at[pl.ds(4 * rows, 2 * rows), self.lanes[0]],
            across(*EDGE_X),
        )
        for other in range(2):
            self.copies.send(
                ("y", other),
                self.held.at[aligned((2 * other + 1 - y) * rows, rows), self.lanes[1]],
                self.landing.at[pl.ds((4 + other) * rows, rows), self.lanes[1]],
                across(*EDGE_Y),
            )

    def second(self):
        rows = self.rows
        x, y = (bit_of(*EDGE_X), bit_of(*EDGE_Y))
        self.copies.arrive("x")
        here = aligned(2 * x * rows, 2 * rows)
        self.held[here, self.lanes[0]] = (
            self.held[here, self.lanes[0]].astype(WIDE)
            + self.landing[pl.ds(4 * rows, 2 * rows), self.lanes[0]].astype(WIDE)
        ).astype(LOW)
        self.copies.send(
            "then y",
            self.held.at[aligned((2 * x + 1 - y) * rows, rows), self.lanes[0]],
            self.landing.at[pl.ds(6 * rows, rows), self.lanes[0]],
            across(*EDGE_Y),
        )
        for other in range(2):
            self.copies.arrive(("y", other))
            here = aligned((2 * other + y) * rows, rows)
            self.held[here, self.lanes[1]] = (
                self.held[here, self.lanes[1]].astype(WIDE)
                + self.landing[pl.ds((4 + other) * rows, rows), self.lanes[1]].astype(WIDE)
            ).astype(LOW)
        self.copies.send(
            "then x",
            self.held.at[aligned((2 * (1 - x) + y) * rows, rows), self.lanes[1]],
            self.landing.at[pl.ds(6 * rows, rows), self.lanes[1]],
            across(*EDGE_X),
        )

    def third(self):
        rows = self.rows
        self.copies.arrive("then y")
        self.copies.arrive("then x")
        here = aligned((2 * bit_of(*EDGE_X) + bit_of(*EDGE_Y)) * rows, rows)
        self.finish(
            self.held[here, :].astype(WIDE) + self.landing[pl.ds(6 * rows, rows), :].astype(WIDE)
        )
        self.copies.close()

    def tasks(self):
        return [self.begin, self.first, self.second, self.third]

    @staticmethod
    def scratch(rows):
        return [
            pltpu.VMEM((4 * rows, 512), LOW),
            pltpu.VMEM((7 * rows, 512), LOW),
            pltpu.SemaphoreType.DMA((2,)),
            pltpu.SemaphoreType.DMA((2, 7)),
        ]


class Homing:
    def __init__(self, source, target, sems):
        batch, seq = place()
        partner = home()
        self.here = (partner[0] == batch) & (partner[1] == seq)
        self.stay = pltpu.make_async_copy(source, target, sems.at[0])
        self.go = pltpu.make_async_remote_copy(
            src_ref=source,
            dst_ref=target,
            send_sem=sems.at[0],
            recv_sem=sems.at[1],
            device_id=partner,
            device_id_type=GRID,
        )

    def start(self):
        @pl.when(self.here)
        def _():
            self.stay.start()

        @pl.when(jnp.logical_not(self.here))
        def _():
            self.go.start()

    def wait(self):
        @pl.when(self.here)
        def _():
            self.stay.wait()

        @pl.when(jnp.logical_not(self.here))
        def _():
            self.go.wait()

    def tasks(self):
        return [self.start, self.wait]


def announce_home():
    batch, seq = place()
    partner = home()

    @pl.when((partner[0] != batch) | (partner[1] != seq))
    def _():
        announce([partner])


def meet_with_home(count):
    batch, seq = place()
    partner = home()
    here = (partner[0] == batch) & (partner[1] == seq)

    @pl.when(jnp.logical_not(here))
    def _():
        meet(count + 1)

    if count:

        @pl.when(here)
        def _():
            meet(count)


HOMING = [pltpu.SemaphoreType.DMA((2,))]


whole = pl.BlockSpec(memory_space=pltpu.VMEM)
scalars = pl.BlockSpec(memory_space=pltpu.SMEM)
apart = pl.BlockSpec(memory_space=pl.ANY)

def settings(number, limit=vmem_bytes):
    if number is None:
        return pltpu.CompilerParams(vmem_limit_bytes=limit)
    return pltpu.CompilerParams(
        vmem_limit_bytes=limit, collective_id=number, has_side_effects=True
    )


def cost(flops):
    return pl.CostEstimate(flops=int(flops), bytes_accessed=40 << 20, transcendentals=0)


class Names:
    def __init__(self, refs):
        self.refs = list(refs)

    def take(self, count):
        taken, self.refs = (self.refs[:count], self.refs[count:])
        return taken

    def share(self, lists):
        return [self.take(len(item)) for item in lists]


def flat(lists):
    return [item for items in lists for item in items]


GATHER_DUE = (
    (8.99000, 8.99002, 8.99004, 8.99006, 8.99008, 8.99010),
    (48.99022, 63.39036, 63.39038, 76.49050, 79.99056, 82.99078),
)
SCATTER_DUE = (
    (82.99064, 87.39090, 96.54154, 103.49134),
    (138.99190, 138.99802, 139.00418, 139.01038),
)
EARLY_REDUCE_DUE = (
    (54.49024, 58.69026, 60.69028, 62.69032, 63.39034, 64.69040, 66.69042, 73.39046, 72.69044, 74.69048, 82.99058, 79.99052, 82.99060, 83.99080, 82.99072, 83.99082, 88.49094, 87.39092, 89.54138),
    (110.49152, 115.39156, 116.69158, 118.69162, 119.39168, 121.39170, 122.69174, 138.99188, 128.69180, 138.99394, 138.99700, 138.99904, 139.00006, 139.00212, 139.00930, 139.00932, 139.00934, 139.01144, 139.01246),
)
EARLY_SHARE_DUE = (
    (89.54140, 94.39108, 96.54150, 98.69198, 98.69200, 99.79204, 103.49132, 108.99148, 106.99140, 110.49150, 128.69178, 118.69160, 132.49184, 138.99186),
    (139.01248, 139.01660, 139.01766, 139.01970, 139.02174, 139.02480, 139.02686, 139.02788, 139.02890, 139.03298, 139.03502, 139.03604, 139.03910, 139.04318),
)
LATE_REDUCE_DUE = (
    (79.99054, 82.99062, 82.99066, 82.99068, 82.99070, 82.99074, 82.99076, 84.89084, 87.39086, 87.39088, 88.49096, 90.64142, 90.64144, 90.64146, 97.64156, 96.54152, 98.69202, 99.79206, 99.79208),
    (139.00316, 139.00420, 139.00522, 139.00624, 139.00826, 139.00928, 139.00936, 139.01250, 139.01252, 139.01040, 139.01456, 139.01762, 139.01354, 139.01868, 139.02072, 139.01764, 139.02378, 139.02582, 139.02276),
)
LATE_SHARE_DUE = (
    (99.79210, 106.99142, 106.99144, 106.99146, 122.69176, 118.69164, 118.69166, 130.69182, 138.99596, 138.99292, 138.99598, 139.00008, 139.00110, 139.00314),
    (139.02584, 139.02992, 139.03094, 139.03196, 139.03400, 139.03706, 139.03808, 139.04012, 139.04114, 139.04216, 139.04420, 139.04522, 139.04624, 139.04726),
)
HOME_DUE = (
    (48.99020, 60.69030),
    (104.99138, 122.69172),
    (103.49136, 114.69154),
    (139.01042, 139.01558),
)


QUERY_LANES = 512


class Schedule:
    def __init__(self):
        self.waiting = []
        self.now = 0.0
        self.base = 0.0

    def add(self, due, tasks):
        self.waiting += zip(due, tasks, strict=True)
        self.waiting.sort(key=lambda task: task[0])

    def stage(self, base):
        self.base = base
        self.tick(0.0)

    def tick(self, now):
        self.now = self.base + now
        while self.waiting and self.waiting[0][0] <= self.now:
            self.waiting.pop(0)[1]()

    def require(self, last):
        while any(task == last for unused, task in self.waiting):
            self.waiting.pop(0)[1]()

    def drain(self):
        while self.waiting:
            self.waiting.pop(0)[1]()


def load_early(moves, block, hbm, target):
    unused, out_hbm, up_hbm, down_hbm = hbm
    width = target.shape[1]
    fan = up_hbm.shape[2]
    for number in range(fan // width):
        moves.start(
            ("up", block, number),
            up_hbm.at[block, :, pl.ds(number * width, width)],
            target.at[pl.ds(number * width, width)],
        )
    moves.start(("down", block), down_hbm.at[block], target.at[pl.ds(fan, fan)])
    moves.start(("out", block), out_hbm.at[block], target.at[pl.ds(2 * fan, width)])


def load_late(moves, block, hbm, target):
    width = target.shape[2]
    for number in range(3):
        moves.start(
            ("qkv", block, number),
            hbm[0].at[block, :, pl.ds(number * width, width)],
            target.at[block, pl.ds(number * width, width)],
        )


def forward_pass(block, schedule, moves, lengths, gains_ref, spill, r):
    tick = schedule.tick
    rows, width = r.moved.shape
    total = r.kv.shape[0]
    fan = r.hidden.shape[1]
    head_size = width // HEADS
    group_width = GROUP * head_size
    groups = width // group_width
    stacked = GROUP * rows
    band = band_here()
    lane_head = head_lanes(rows, head_size)
    chunks = key_chunks(total // rows, rows)
    image_query = segments(lengths, stacked_positions(band, rows))
    is_image = image_query == 1
    inputs_ref = r.moved if block == 0 else r.outputs.at[0]
    normed_all = r.normed.at[block]
    matrices = r.late_matrices.at[block]
    for number in range(3):
        moves.wait(("qkv", block, number))
    own = normed_all[aligned(band * rows, rows), :]
    query = product(own, matrices[:width], NN).astype(LOW)
    query = query * jnp.asarray(head_size ** (-0.5), LOW)
    for group in range(groups):
        lanes = slice(group * group_width, (group + 1) * group_width)
        r.query_stack[group] = stack_heads(query[:, lanes], lane_head)
    tick(1.0)
    for number, (start, size) in enumerate(chunks):
        at = slice(start, start + size)
        rows_here = normed_all[at]
        for part in range(2):
            r.kv[at, part * width : (part + 1) * width] = product(
                rows_here, matrices[(part + 1) * width : (part + 2) * width], NN
            ).astype(LOW)
        tick(1.5 + 0.4 * number)
    for group in range(groups):
        base = 3.5 + 7.0 * group
        lanes = slice(group * group_width, (group + 1) * group_width)
        value_lanes = slice(width + group * group_width, width + (group + 1) * group_width)
        if group > 0:
            moves.wait(("spill", block, group - 1))
        attended, inverses = ([], [])
        for lane in range(0, stacked, QUERY_LANES):
            size_lanes = min(QUERY_LANES, stacked - lane)
            here = slice(lane, lane + size_lanes)
            stack = r.query_stack[group, here]
            edge_max = None
            middle_max = None
            for number, (start, size) in enumerate(chunks):
                scores = product(r.kv[start : start + size, lanes], stack, NT)
                edge = number in (0, len(chunks) - 1)
                if edge:
                    positions = start + lax.broadcasted_iota(jnp.int32, (size, 1), 0)
                    allowed = segments(lengths, positions) == image_query[:, here]
                    scores = jnp.where(allowed, scores, masked_score)
                r.scores[start : start + size, :size_lanes] = scores
                top = jnp.max(scores, axis=0, keepdims=True)
                if edge:
                    edge_max = top if edge_max is None else jnp.maximum(edge_max, top)
                else:
                    middle_max = top if middle_max is None else jnp.maximum(middle_max, top)
            tick(base + lane * 0.0042 + 0.9)
            image = is_image[:, here]
            row_max = jnp.maximum(edge_max, jnp.where(image, middle_max, masked_score))
            inner_max = jnp.where(image, row_max, -masked_score)
            totals = None
            gathered = None
            for number, (start, size) in enumerate(chunks):
                edge = number in (0, len(chunks) - 1)
                weights = jnp.exp(
                    r.scores[start : start + size, :size_lanes] - (row_max if edge else inner_max)
                )
                part = jnp.sum(weights, axis=0, keepdims=True)
                totals = part if totals is None else totals + part
                low = weights.astype(LOW)
                r.weights[start : start + size, here] = low
                piece = product(low, r.kv[start : start + size, value_lanes], TN)
                gathered = piece if gathered is None else gathered + piece
            attended.append(gathered)
            inverses.append(1.0 / totals)
            tick(base + lane * 0.0042 + 2.0)
        if group + 1 < groups:
            moves.start(("spill", block, group), r.weights, spill.at[group])
        columns = jnp.transpose(
            jnp.broadcast_to(jnp.concatenate(inverses, axis=1), (128, stacked))
        )
        inverse = unstack_heads(
            jnp.concatenate([columns] * (group_width // 128), axis=1), lane_head, rows
        )
        r.inverse[:, lanes] = inverse
        r.attended[:, lanes] = (
            unstack_heads(jnp.concatenate(attended, axis=0), lane_head, rows) * inverse
        )
        tick(base + 6.9)
    positions = band * rows + lax.broadcasted_iota(jnp.int32, (rows, 1), 0)
    keep_rows = (segments(lengths, positions) < 3).astype(WIDE)
    low = (r.attended[...] * keep_rows).astype(LOW)
    moves.wait(("out", block))
    middle = inputs_ref[...].astype(WIDE) + product(low, r.early_matrices[2 * fan :], NN)
    r.middle[...] = middle
    hat, unused = normalise(middle)
    second = (hat * gains_ref[block, 1:2, :]).astype(LOW)
    tick(18.5)
    for number in range(fan // width):
        moves.wait(("up", block, number))
        here = slice(number * width, (number + 1) * width)
        up_rows = product(second, r.early_matrices[here], NN)
        square = up_rows * up_rows
        bend = jnp.tanh(0.7978845608028654 * (up_rows + 0.044715 * square * up_rows))
        half = 0.5 * (1.0 + bend)
        r.hidden[:, here] = (up_rows * half).astype(LOW)
        r.slope[:, here] = (
            half
            + 0.5
            * up_rows
            * (1.0 - bend * bend)
            * (0.7978845608028654 * (1.0 + (3 * 0.044715) * square))
        ).astype(LOW)
    moves.wait(("down", block))
    tick(20.5)
    output = (middle + product(r.hidden[...], r.early_matrices[fan : 2 * fan], NN)).astype(LOW)
    r.outputs[block] = output
    if block == 0:
        hat, unused = normalise(output.astype(WIDE))
        r.normed[1, aligned(band * rows, rows), :] = (hat * gains_ref[1, 0:1, :]).astype(LOW)


def backward_pass(block, schedule, moves, lengths, gains_ref, spill, r, begin_early, begin_late):
    tick = schedule.tick
    rows, width = r.moved.shape
    total = r.kv.shape[0]
    fan = r.hidden.shape[1]
    head_size = width // HEADS
    group_width = GROUP * head_size
    groups = width // group_width
    band = band_here()
    lane_head = head_lanes(rows, head_size)
    chunks = key_chunks(total // rows, rows)
    normed_all = r.normed.at[block]
    matrices = r.late_matrices.at[block]
    early = r.early_matrices
    gain_terms = r.small.at[STEPS]

    def reload(group, number):
        at = pl.ds(*chunks[number])
        moves.start(("reload", block, group, number), spill.at[group, at], r.weights.at[at])

    order = tuple(reversed(range(groups)))
    grad = r.grads[block]
    grad_hidden = product(grad, early[fan : 2 * fan], NT)
    grad_up = (grad_hidden * r.slope[...].astype(WIDE)).astype(LOW)
    early[fan : 2 * fan] = product(r.hidden[...], grad, TN).astype(LOW)
    tick(2.0)
    hat, inverse = normalise(r.middle[...])
    second = (hat * gains_ref[block, 1:2, :]).astype(LOW)
    grad_second = None
    for number in range(fan // width):
        here = slice(number * width, (number + 1) * width)
        piece = product(grad_up[:, here], early[here], NT)
        grad_second = piece if grad_second is None else grad_second + piece
    for number in range(fan // width):
        here = slice(number * width, (number + 1) * width)
        early[here] = product(second, grad_up[:, here], TN).astype(LOW)
    tick(4.0)
    gain_terms[2 * block + 1 : 2 * block + 2, :] = jnp.sum(grad_second * hat, axis=0, keepdims=True)
    grad_middle = grad.astype(WIDE) + normalise_back(
        hat, inverse, gains_ref[block, 1:2, :], grad_second
    )
    r.middle_grad[...] = grad_middle
    grad_branch = grad_middle.astype(LOW)
    positions = band * rows + lax.broadcasted_iota(jnp.int32, (rows, 1), 0)
    keep_rows = (segments(lengths, positions) < 3).astype(WIDE)
    grad_attended = product(grad_branch, early[2 * fan :], NT) * keep_rows
    low = (r.attended[...] * keep_rows).astype(LOW)
    early[2 * fan :] = product(low, grad_branch, TN).astype(LOW)
    begin_early()
    tick(5.5)
    scaled = (grad_attended * r.inverse[...]).astype(LOW)
    ones = jnp.ones((8, group_width), LOW)
    deltas = []
    for group in range(groups):
        lanes = slice(group * group_width, (group + 1) * group_width)
        stack = stack_heads(scaled[:, lanes], lane_head)
        r.grad_stack[group] = stack
        dots = stack.astype(WIDE) * jnp.concatenate([r.attended[:, lanes]] * GROUP, axis=0)
        high = dots.astype(LOW)
        rest = (dots - high.astype(WIDE)).astype(LOW)
        deltas.append((product(ones, high, NT) + product(ones, rest, NT))[0:1])
    tick(7.0)
    query_grads = [None] * groups
    for turn, group in enumerate(order):
        lanes = slice(group * group_width, (group + 1) * group_width)
        value_lanes = slice(width + group * group_width, width + (group + 1) * group_width)
        collected = None
        for number, (start, size) in enumerate(chunks):
            base = 7.0 + 10.0 * turn + 2.0 * number
            at = slice(start, start + size)
            if turn > 0:
                moves.wait(("reload", block, group, number))
            low = r.weights[at]
            grad_weights = product(r.kv[at, value_lanes], r.grad_stack[group], NT)
            grad_scores = (low.astype(WIDE) * (grad_weights - deltas[group])).astype(LOW)
            tick(base + 0.7)
            r.kv[at, value_lanes] = product(low, r.grad_stack[group], NN).astype(LOW)
            piece = product(grad_scores, r.kv[at, lanes], TN)
            collected = piece if collected is None else collected + piece
            tick(base + 1.4)
            r.kv[at, lanes] = product(grad_scores, r.query_stack[group], NN).astype(LOW)
            if turn + 1 < groups:
                reload(order[turn + 1], number)
        query_grads[group] = unstack_heads(collected, lane_head, rows)
    query_grad = (jnp.concatenate(query_grads, axis=1) * head_size ** (-0.5)).astype(LOW)
    tick(27.5)
    here = aligned(band * rows, rows)
    own = normed_all[here, :]
    r.late_terms[:width] = product(own, query_grad, TN).astype(LOW)
    for part in range(2):
        r.late_terms[(part + 1) * width : (part + 2) * width] = product(
            normed_all[...], r.kv[:, part * width : (part + 1) * width], TN
        ).astype(LOW)
    begin_late()
    tick(31.0)
    query_part = product(query_grad, matrices[:width], NT)
    r.query_grad[...] = query_part
    gain_row = jnp.sum(query_part * own.astype(WIDE), axis=0, keepdims=True)
    for start, size in chunks:
        at = slice(start, start + size)
        normed_grad = product(r.kv[at, :width], matrices[width : 2 * width], NT) + product(
            r.kv[at, width:], matrices[2 * width :], NT
        )
        piece = normed_all[at].astype(WIDE)
        gain_row = gain_row + jnp.sum(normed_grad * piece, axis=0, keepdims=True)
        normed_all[at] = normed_grad.astype(LOW)
    gain_terms[2 * block : 2 * block + 1, :] = gain_row / gains_ref[block, 0:1, :]


def inputs_back(block, inputs_ref, gains_ref, r, summed):
    hat, inverse = normalise(inputs_ref[...].astype(WIDE))
    return (
        r.middle_grad[...]
        + normalise_back(hat, inverse, gains_ref[block, 0:1, :], summed + r.query_grad[...])
    ).astype(LOW)


LATE = (512, 512, 512)
EARLY = (1536, 1536, 1536)


class Holder:
    pass


def scratch_plan(rows, width, total, fan):
    groups = HEADS // GROUP
    gw = width // groups
    stacked = GROUP * rows
    plan = {
        "moved": pltpu.VMEM((rows, width), LOW),
        "grads": pltpu.VMEM((2, rows, width), LOW),
        "normed": pltpu.VMEM((2, total, width), LOW),
        "late_matrices": pltpu.VMEM((2, 3 * width, width), LOW),
        "early_matrices": pltpu.VMEM((2 * fan + width, width), LOW),
        "late_terms": pltpu.VMEM((3 * width, width), LOW),
        "query_stack": pltpu.VMEM((groups, stacked, gw), LOW),
        "grad_stack": pltpu.VMEM((groups, stacked, gw), LOW),
        "scores": pltpu.VMEM((total, QUERY_LANES), WIDE),
        "weights": pltpu.VMEM((total, stacked), LOW),
        "kv": pltpu.VMEM((total, 2 * width), LOW),
        "attended": pltpu.VMEM((rows, width), WIDE),
        "inverse": pltpu.VMEM((rows, width), WIDE),
        "middle": pltpu.VMEM((rows, width), WIDE),
        "hidden": pltpu.VMEM((rows, fan), LOW),
        "slope": pltpu.VMEM((rows, fan), LOW),
        "outputs": pltpu.VMEM((2, rows, width), LOW),
        "middle_grad": pltpu.VMEM((rows, width), WIDE),
        "query_grad": pltpu.VMEM((rows, width), WIDE),
        "inputs_grad": pltpu.VMEM((2, rows, width), LOW),
        "late_part": pltpu.VMEM((2, sum(LATE) // DEVICES, width), LOW),
        "early_part": pltpu.VMEM((2, sum(EARLY) // DEVICES, width), LOW),
        "small": pltpu.VMEM((2 * STEPS, 8, width), WIDE),
        "small_sems": pltpu.SemaphoreType.DMA((2, STEPS)),
        "home_sems": pltpu.SemaphoreType.DMA((7, 2)),
        "sems": pltpu.SemaphoreType.DMA((64,)),
    }
    return plan


def buffers(rows):
    return [
        Scattering.scratch(rows)[:2],
        Reduction.scratch(LATE, False)[:2],
        Reduction.scratch(EARLY, True)[:2],
    ]


def block_scratch(rows):
    return [
        Gathering.scratch(),
        Reduction.scratch(LATE, False)[2:],
        Reduction.scratch(EARLY, True)[2:],
        Sharing.scratch(LATE),
        Sharing.scratch(EARLY),
        Scattering.scratch(rows)[2:],
    ]


def blocks_kernel(
    lengths, gains_ref, tokens_ref, gen_grad_ref, disc_grad_ref, qkv_hbm, out_hbm, up_hbm, down_hbm,
    gen_out_ref, disc_out_ref, gen_in_ref, disc_in_ref, gen_late_ref, disc_late_ref, gen_early_ref,
    disc_early_ref, gain_total_ref, spill, *refs,
):
    rows, width = tokens_ref.shape
    total = 8 * rows
    fan = up_hbm.shape[2]
    plan = scratch_plan(rows, width, total, fan)
    r = Holder()
    for name, ref in zip(plan, refs):
        setattr(r, name, ref)
    refs = Names(refs[len(plan) :])
    scatter, late, early = refs.share(buffers(rows))
    passes = [refs.share(block_scratch(rows)) for unused in range(2)]
    hbm = (qkv_hbm, out_hbm, up_hbm, down_hbm)
    moves = Moves(r.sems)
    schedule = Schedule()

    announce_home()
    announce([across(*axis) for axis in ORDERS[0]])
    load_late(moves, 0, hbm, r.late_matrices)
    load_early(moves, 0, hbm, r.early_matrices)
    load_late(moves, 1, hbm, r.late_matrices)
    r.small[STEPS] = jnp.zeros((8, width), WIDE)
    meet_with_home(STEPS)
    homes = [
        Homing(source, target, r.home_sems.at[number])
        for number, (source, target) in enumerate(
            [
                (tokens_ref, r.moved),
                (gen_grad_ref, r.grads.at[0]),
                (disc_grad_ref, r.grads.at[1]),
                (r.outputs.at[0], gen_out_ref),
                (r.outputs.at[1], disc_out_ref),
                (r.inputs_grad.at[0], gen_in_ref),
                (r.inputs_grad.at[1], disc_in_ref),
            ]
        )
    ]
    homes[0].start()
    homes[0].wait()
    gatherings = [Gathering(r.normed.at[block], rows, *passes[block][0]) for block in range(2)]
    hat, unused = normalise(r.moved[...].astype(WIDE))
    r.normed[0, aligned(gatherings[0].band * rows, rows), :] = (
        hat * gains_ref[0, 0:1, :]
    ).astype(LOW)
    schedule.stage(9.0)
    schedule.add(GATHER_DUE[0], gatherings[0].tasks())
    homes[1].start()
    homes[2].start()
    schedule.require(gatherings[0].end)
    schedule.stage(27.0)
    forward_pass(0, schedule, moves, lengths, gains_ref, spill, r)

    scatterings = {}
    first_sharing = []

    def begin_after(ready, begin):
        ready()
        begin()

    totals = ((gen_late_ref, gen_early_ref), (disc_late_ref, disc_early_ref))

    def begin_early(block):
        reduction = Reduction(
            EARLY, r.early_matrices, r.early_part.at[block], *early, *passes[block][2], block == 1
        )
        sharing = Sharing(EARLY, r.early_part.at[block], totals[block][1], *passes[block][4])
        steps = reduction.tasks()
        if block == 0:
            first_sharing.append(sharing)
        else:
            steps[0] = functools.partial(begin_after, first_sharing[0].core_began, steps[0])
        schedule.add(EARLY_REDUCE_DUE[block], steps)
        schedule.add(EARLY_SHARE_DUE[block], sharing.tasks())
        if block == 0:

            def refill():
                reduction.release()
                load_early(moves, 1, hbm, r.early_matrices)

            schedule.add(EARLY_REDUCE_DUE[0][7:8], [refill])

    def begin_late(block):
        reduction = Reduction(LATE, r.late_terms, r.late_part.at[block], *late, *passes[block][1])
        sharing = Sharing(LATE, r.late_part.at[block], totals[block][0], *passes[block][3])
        schedule.add(LATE_REDUCE_DUE[block], reduction.tasks())
        schedule.add(LATE_SHARE_DUE[block], sharing.tasks())

    def begin_scatter(block):
        inputs_ref = r.moved if block == 0 else r.outputs.at[0]

        def finish(summed):
            r.inputs_grad[block] = inputs_back(block, inputs_ref, gains_ref, r, summed)

        scatterings[block] = Scattering(
            r.normed.at[block], *scatter, *passes[block][5], rows, finish
        )
        schedule.add(SCATTER_DUE[block], scatterings[block].tasks())
        schedule.add(HOME_DUE[2 + block], homes[5 + block].tasks())

    homes[1].wait()
    homes[2].wait()
    schedule.add(GATHER_DUE[1], gatherings[1].tasks())
    schedule.add(HOME_DUE[0], homes[3].tasks())
    schedule.stage(49.0)
    backward_pass(
        0, schedule, moves, lengths, gains_ref, spill, r,
        functools.partial(begin_early, 0), functools.partial(begin_late, 0),
    )
    begin_scatter(0)
    schedule.stage(83.0)
    schedule.require(gatherings[1].end)
    forward_pass(1, schedule, moves, lengths, gains_ref, spill, r)
    schedule.require(scatterings[0].third)
    schedule.add(HOME_DUE[1], homes[4].tasks())
    schedule.stage(105.0)
    backward_pass(
        1, schedule, moves, lengths, gains_ref, spill, r,
        functools.partial(begin_early, 1), functools.partial(begin_late, 1),
    )
    begin_scatter(1)
    small = SmallSum(gain_total_ref, r.small, r.small_sems)
    schedule.add([139.0 + 0.006 * step for step in range(1 + STEPS)], small.tasks())
    schedule.drain()


def run_blocks(lengths, gains, tokens, gen_grad, disc_grad, matrices):
    rows, width = tokens.shape
    total = 8 * rows
    fan = matrices[2].shape[2]
    shape = jax.ShapeDtypeStruct
    scratch = list(scratch_plan(rows, width, total, fan).values())
    scratch += flat(buffers(rows)) + flat(block_scratch(rows)) * 2
    return pl.pallas_call(
        blocks_kernel,
        out_shape=[shape((rows, width), LOW)] * 4
        + [shape((sum(LATE), width), LOW)] * 2
        + [shape((sum(EARLY), width), LOW)] * 2
        + [
            shape((8, width), WIDE),
            shape((HEADS // GROUP - 1, total, GROUP * rows), LOW),
        ],
        in_specs=[scalars, whole] + [apart] * 7,
        out_specs=[apart] * 8 + [whole, apart],
        scratch_shapes=scratch,
        compiler_params=settings(1),
        cost_estimate=cost(80e9),
        name="blocks",
    )(lengths, gains, tokens, gen_grad, disc_grad, *matrices)[:9]


def emit_kernel(
    late_refs, early_refs, small_refs, out_refs, small_out_refs, read, written, sems, *small_held
):
    width = read.shape[2]
    qkv_ref, out_ref, up_ref, down_ref = out_refs
    items = []
    for block, (late, early) in enumerate(zip(late_refs, early_refs, strict=True)):
        for target, source, at, count in (
            (qkv_ref, late, 0, qkv_ref.shape[2] // width),
            (up_ref, early, 0, up_ref.shape[2] // width),
            (out_ref, early, up_ref.shape[2] + down_ref.shape[1], 1),
        ):
            for number in range(count):
                items.append(
                    (
                        source.at[pl.ds(at + number * width, width)],
                        target.at[block, :, pl.ds(number * width, width)],
                    )
                )
        for number in range(down_ref.shape[1] // width):
            items.append(
                (
                    early.at[pl.ds(up_ref.shape[2] + number * width, width)],
                    down_ref.at[block, pl.ds(number * width, width)],
                )
            )
    slots = read.shape[0]
    small_loads, small_stores = (
        [
            pltpu.make_async_copy(source, target, sems.at[2, number])
            for number, (source, target) in enumerate(zip(sources, targets, strict=True))
        ]
        for sources, targets in ((small_refs, small_held), (small_held, small_out_refs))
    )
    for load in small_loads:
        load.start()
    loads = [
        pltpu.make_async_copy(source, read.at[number % slots], sems.at[0, number % slots])
        for number, (source, unused) in enumerate(items)
    ]
    stores = [
        pltpu.make_async_copy(written.at[number % slots], target, sems.at[1, number % slots])
        for number, (unused, target) in enumerate(items)
    ]
    for number in range(slots):
        loads[number].start()
    for load, store in zip(small_loads, small_stores, strict=True):
        load.wait()
        store.start()
    for number in range(len(items)):
        loads[number].wait()
        if number >= slots:
            stores[number - slots].wait()
        written[number % slots] = read[number % slots].astype(WIDE)
        stores[number].start()
        if number + slots < len(items):
            loads[number + slots].start()
    for store in stores[-slots:]:
        store.wait()
    for store in small_stores:
        store.wait()


def run_emit(lates, earlies, small, width, fan):
    shape = jax.ShapeDtypeStruct
    count = len(small)
    slots = 24

    def kernel(*refs):
        names = Names(refs)
        late_refs, early_refs, small_refs = names.share([lates, earlies, small])
        small_out, out_refs = (names.take(count), names.take(4))
        emit_kernel(late_refs, early_refs, small_refs, out_refs, small_out, *names.refs)

    return pl.pallas_call(
        kernel,
        out_shape=[shape(item.shape, item.dtype) for item in small]
        + [
            shape((2, width, 3 * width), WIDE),
            shape((2, width, width), WIDE),
            shape((2, width, fan), WIDE),
            shape((2, fan, width), WIDE),
        ],
        in_specs=[apart] * (4 + count),
        out_specs=[apart] * (4 + count),
        scratch_shapes=[
            pltpu.VMEM((slots, width, width), LOW),
            pltpu.VMEM((slots, width, width), WIDE),
            pltpu.SemaphoreType.DMA((3, max(slots, count))),
        ]
        + [pltpu.VMEM(item.shape, item.dtype) for item in small],
        compiler_params=settings(None),
        cost_estimate=cost(1e9),
        name="emit_part",
    )(*lates, *earlies, *small)


def local_kernels(
    tokens,
    norm_gains,
    qkv_weight,
    out_weight,
    up_weight,
    down_weight,
    gen_cotangent,
    disc_cotangent,
    seg_lengths,
):
    size = lax.axis_size("seq")
    swap = (0, 2, 1, 3)
    pairs = [
        (batch * size + seq, swap[seq // 2] * size + 2 * swap[batch] + seq % 2)
        for batch in range(lax.axis_size("batch"))
        for seq in range(size)
    ]
    lengths = lax.ppermute(seg_lengths, ("batch", "seq"), pairs)
    *outs, gen_late, disc_late, gen_early, disc_early, gain_sums = run_blocks(
        lengths,
        norm_gains,
        tokens[0],
        gen_cotangent[0],
        disc_cotangent[0],
        (qkv_weight, out_weight, up_weight, down_weight),
    )
    *outs, gain_sums, qkv_grad, out_grad, up_grad, down_grad = run_emit(
        (gen_late, disc_late),
        (gen_early, disc_early),
        (*outs, gain_sums),
        up_weight.shape[1],
        up_weight.shape[2],
    )
    return (
        *(out[None] for out in outs),
        gain_sums[:4].reshape(2, 2, -1),
        qkv_grad,
        out_grad,
        up_grad,
        down_grad,
    )


def solution(mesh):
    placed = (
        P("batch", "seq", None),
        P(),
        P(),
        P(),
        P(),
        P(),
        P("batch", "seq", None),
        P("batch", "seq", None),
        P("batch", None),
    )
    planes = dict(mesh.shape) == {"batch": 4, "seq": 8}
    return jax.shard_map(
        local_kernels if planes else local_scan,
        mesh=mesh,
        in_specs=placed,
        out_specs=(
            P("batch", "seq", None),
            P("batch", "seq", None),
            P("batch", "seq", None),
            P("batch", "seq", None),
            P(),
            P(),
            P(),
            P(),
            P(),
        ),
        check_vma=False,
    )
```

```python
import functools
import math

import jax
import jax.numpy as jnp
from jax import lax
from jax.experimental import pallas as pl
from jax.experimental.pallas import tpu as pltpu
from jax.sharding import PartitionSpec as P

HEADS = 8


epsilon = 1e-05
masked_score = -1e30
key_block = 2048


def layer_norm(inputs, gain_row):
    average = jnp.mean(inputs, axis=-1, keepdims=True)
    centred = inputs - average
    variance = jnp.mean(centred * centred, axis=-1, keepdims=True)
    return centred * lax.rsqrt(variance + epsilon) * gain_row


def gelu_tanh(inputs):
    return (
        0.5
        * inputs
        * (1.0 + jnp.tanh(0.7978845608028654 * (inputs + 0.044715 * inputs * inputs * inputs)))
    )


def segment_of(lengths, positions):
    first = lengths[0]
    second = first + lengths[1]
    third = second + lengths[2]
    return (
        (positions >= first).astype(jnp.int32)
        + (positions >= second).astype(jnp.int32)
        + (positions >= third).astype(jnp.int32)
    )


def block_scores(query_heads, key_heads, query_segment, key_segment, scale):
    scores = (
        jnp.einsum("qhe,khe->hqk", query_heads, key_heads, preferred_element_type=jnp.float32)
        * scale
    )
    allowed = query_segment[:, None] == key_segment[None, :]
    return jnp.where(allowed[None], scores, masked_score)


def split_blocks(array_rows, width):
    return array_rows.reshape((array_rows.shape[0] // width, width) + array_rows.shape[1:])


def attend(query_heads, key_heads, value_heads, query_segment, key_segment, scale):
    width = math.gcd(key_heads.shape[0], key_block)
    blocks = (
        split_blocks(key_heads, width),
        split_blocks(value_heads, width),
        split_blocks(key_segment, width),
    )
    heads = query_heads.shape[1]
    row_count = query_heads.shape[0]

    def statistics(carry, item):
        row_max, totals = carry
        scores = block_scores(query_heads, item[0], query_segment, item[2], scale)
        new_max = jnp.maximum(row_max, jnp.max(scores, axis=-1))
        totals = totals * jnp.exp(row_max - new_max) + jnp.sum(
            jnp.exp(scores - new_max[..., None]), axis=-1
        )
        return ((new_max, totals), None)

    start_max = jnp.full((heads, row_count), masked_score, jnp.float32)
    (row_max, totals), unused = lax.scan(
        statistics, (start_max, jnp.zeros((heads, row_count), jnp.float32)), blocks
    )
    log_total = row_max + jnp.log(totals)

    def weighted(running, item):
        scores = block_scores(query_heads, item[0], query_segment, item[2], scale)
        weights_low = jnp.exp(scores - log_total[..., None]).astype(jnp.bfloat16)
        return (
            running
            + jnp.einsum("hqk,khe->qhe", weights_low, item[1], preferred_element_type=jnp.float32),
            None,
        )

    attended, unused = lax.scan(weighted, jnp.zeros(query_heads.shape, jnp.float32), blocks)
    return (attended, log_total)


def query_side(
    query_heads,
    key_heads,
    value_heads,
    query_segment,
    key_segment,
    grad_heads,
    log_total,
    delta,
    scale,
):
    width = math.gcd(key_heads.shape[0], key_block)
    blocks = (
        split_blocks(key_heads, width),
        split_blocks(value_heads, width),
        split_blocks(key_segment, width),
    )

    def step(running, item):
        scores = block_scores(query_heads, item[0], query_segment, item[2], scale)
        weights = jnp.exp(scores - log_total[..., None])
        dprobs = jnp.einsum("qhe,khe->hqk", grad_heads, item[1], preferred_element_type=jnp.float32)
        dscores = (weights * (dprobs - delta[..., None])).astype(jnp.bfloat16)
        running = running + jnp.einsum(
            "hqk,khe->qhe", dscores, item[0], preferred_element_type=jnp.float32
        )
        key_part = (
            jnp.einsum("hqk,qhe->khe", dscores, query_heads, preferred_element_type=jnp.float32)
            * scale
        )
        value_part = jnp.einsum(
            "hqk,qhe->khe",
            weights.astype(jnp.bfloat16),
            grad_heads,
            preferred_element_type=jnp.float32,
        )
        return (running, (key_part, value_part))

    grad_query, key_parts = lax.scan(step, jnp.zeros(query_heads.shape, jnp.float32), blocks)
    return (grad_query * scale, key_parts)


def block_forward(inputs, gains, qkv_matrix, out_matrix, up_matrix, down_matrix, lengths):
    row_count, width = inputs.shape
    heads = HEADS
    head_size = width // heads
    scale = head_size ** (-0.5)
    band_index = lax.axis_index("seq")
    positions = band_index * row_count + jnp.arange(row_count, dtype=jnp.int32)
    query_segment = segment_of(lengths, positions)
    key_segment = segment_of(lengths, jnp.arange(row_count * lax.axis_size("seq"), dtype=jnp.int32))
    keep_rows = (query_segment < 3).astype(jnp.float32)[:, None]
    normed = layer_norm(inputs, gains[0]).astype(jnp.bfloat16)
    qkv_rows = jnp.dot(normed, qkv_matrix, preferred_element_type=jnp.float32).astype(jnp.bfloat16)
    all_keys, all_values = (
        lax.all_gather(qkv_rows[:, width : 2 * width], "seq", axis=0, tiled=True),
        lax.all_gather(qkv_rows[:, 2 * width :], "seq", axis=0, tiled=True),
    )
    attended, log_total = attend(
        qkv_rows[:, :width].reshape(row_count, heads, head_size),
        all_keys.reshape(-1, heads, head_size),
        all_values.reshape(-1, heads, head_size),
        query_segment,
        key_segment,
        scale,
    )
    attended = attended.reshape(row_count, width)
    attended_low = (attended * keep_rows).astype(jnp.bfloat16)
    middle = inputs + jnp.dot(attended_low, out_matrix, preferred_element_type=jnp.float32)
    second_norm = layer_norm(middle, gains[1]).astype(jnp.bfloat16)
    up_rows = jnp.dot(second_norm, up_matrix, preferred_element_type=jnp.float32)
    hidden = gelu_tanh(up_rows).astype(jnp.bfloat16)
    outputs = middle + jnp.dot(hidden, down_matrix, preferred_element_type=jnp.float32)
    kept = (
        inputs,
        normed,
        qkv_rows,
        None,
        attended,
        log_total,
        attended_low,
        middle,
        second_norm,
        up_rows,
        hidden,
        query_segment,
        key_segment,
        keep_rows,
        lengths,
    )
    return (outputs, kept)


def block_backward(kept, grad_out, gains, qkv_matrix, out_matrix, up_matrix, down_matrix):
    (
        inputs,
        normed,
        qkv_rows,
        gathered,
        attended,
        log_total,
        attended_low,
        middle,
        second_norm,
        up_rows,
        hidden,
        query_segment,
        key_segment,
        keep_rows,
        lengths,
    ) = kept
    row_count, width = inputs.shape
    heads = HEADS
    head_size = width // heads
    scale = head_size ** (-0.5)
    grad_down = jnp.einsum("tf,td->fd", hidden, grad_out, preferred_element_type=jnp.float32)
    grad_hidden = jnp.einsum("td,fd->tf", grad_out, down_matrix, preferred_element_type=jnp.float32)
    unused, gelu_back = jax.vjp(gelu_tanh, up_rows)
    grad_up_rows = gelu_back(grad_hidden)[0].astype(jnp.bfloat16)
    grad_up = jnp.einsum("td,tf->df", second_norm, grad_up_rows, preferred_element_type=jnp.float32)
    grad_second = jnp.einsum(
        "tf,df->td", grad_up_rows, up_matrix, preferred_element_type=jnp.float32
    )
    unused, second_back = jax.vjp(layer_norm, middle, gains[1])
    middle_part, gain_second = second_back(grad_second)
    grad_middle = grad_out.astype(jnp.float32) + middle_part
    grad_branch = grad_middle.astype(jnp.bfloat16)
    grad_outw = jnp.einsum(
        "td,te->de", attended_low, grad_branch, preferred_element_type=jnp.float32
    )
    grad_attended = jnp.einsum(
        "te,de->td", grad_branch, out_matrix, preferred_element_type=jnp.float32
    ).astype(jnp.bfloat16) * keep_rows.astype(jnp.bfloat16)
    grad_heads = grad_attended.reshape(row_count, heads, head_size)
    delta = jnp.sum(
        grad_heads.astype(jnp.float32) * attended.reshape(row_count, heads, head_size), axis=-1
    ).T
    query_heads = qkv_rows[:, :width].reshape(row_count, heads, head_size)
    all_keys, all_values = (
        lax.all_gather(qkv_rows[:, width : 2 * width], "seq", axis=0, tiled=True),
        lax.all_gather(qkv_rows[:, 2 * width :], "seq", axis=0, tiled=True),
    )
    key_heads = all_keys.reshape(-1, heads, head_size)
    value_heads = all_values.reshape(-1, heads, head_size)
    grad_query, key_parts = query_side(
        query_heads,
        key_heads,
        value_heads,
        query_segment,
        key_segment,
        grad_heads,
        log_total,
        delta,
        scale,
    )
    grad_keys, grad_values = (
        lax.psum_scatter(
            key_parts[0].reshape(-1, width).astype(jnp.bfloat16),
            "seq",
            scatter_dimension=0,
            tiled=True,
        ).astype(jnp.float32),
        lax.psum_scatter(
            key_parts[1].reshape(-1, width).astype(jnp.bfloat16),
            "seq",
            scatter_dimension=0,
            tiled=True,
        ).astype(jnp.float32),
    )
    grad_qkv_rows = jnp.concatenate(
        [grad_query.reshape(row_count, width), grad_keys, grad_values], axis=1
    ).astype(jnp.bfloat16)
    grad_qkv = jnp.einsum("td,tf->df", normed, grad_qkv_rows, preferred_element_type=jnp.float32)
    grad_first = jnp.einsum(
        "tf,df->td", grad_qkv_rows, qkv_matrix, preferred_element_type=jnp.float32
    )
    unused, first_back = jax.vjp(layer_norm, inputs, gains[0])
    input_part, gain_first = first_back(grad_first)
    grad_inputs = grad_middle + input_part
    return (
        grad_inputs,
        (jnp.stack([gain_first, gain_second]), grad_qkv, grad_outw, grad_up, grad_down),
    )


def local_scan(
    tokens,
    norm_gains,
    qkv_weight,
    out_weight,
    up_weight,
    down_weight,
    gen_cotangent,
    disc_cotangent,
    seg_lengths,
):
    gen_weights = (norm_gains[0], qkv_weight[0], out_weight[0], up_weight[0], down_weight[0])
    disc_weights = (norm_gains[1], qkv_weight[1], out_weight[1], up_weight[1], down_weight[1])
    gen_outs, disc_outs, gen_ins, disc_ins = ([], [], [], [])
    number = 0
    lengths = seg_lengths[number]
    gen_rows, gen_kept = block_forward(tokens[number].astype(jnp.float32), *gen_weights, lengths)
    gen_low = gen_rows.astype(jnp.bfloat16)
    disc_rows, disc_kept = block_forward(gen_low.astype(jnp.float32), *disc_weights, lengths)
    disc_grad_in, disc_terms = block_backward(disc_kept, disc_cotangent[number], *disc_weights)
    gen_grad_in, gen_terms = block_backward(gen_kept, gen_cotangent[number], *gen_weights)
    gen_outs.append(gen_low)
    disc_outs.append(disc_rows.astype(jnp.bfloat16))
    gen_ins.append(gen_grad_in.astype(jnp.bfloat16))
    disc_ins.append(disc_grad_in.astype(jnp.bfloat16))
    stacked = [jnp.stack([gen_terms[number], disc_terms[number]]) for number in range(5)]
    summed = lax.psum(
        (stacked[0], stacked[1], stacked[2], stacked[3], stacked[4]), ("batch", "seq")
    )
    return (
        jnp.stack(gen_outs),
        jnp.stack(disc_outs),
        jnp.stack(gen_ins),
        jnp.stack(disc_ins),
        summed[0],
        summed[1],
        summed[2],
        summed[3],
        summed[4],
    )


NN = (((1,), (0,)), ((), ()))
NT = (((1,), (1,)), ((), ()))
TN = (((0,), (0,)), ((), ()))
LOW = jnp.bfloat16
WIDE = jnp.float32
GROUP = 4
vmem_bytes = 63 << 20


def product(left, right, form):
    return lax.dot_general(left, right, form, preferred_element_type=WIDE)


def normalise(inputs):
    average = jnp.mean(inputs, axis=-1, keepdims=True)
    centred = inputs - average
    variance = jnp.mean(centred * centred, axis=-1, keepdims=True)
    inverse = lax.rsqrt(variance + epsilon)
    return (centred * inverse, inverse)


def normalise_back(hat, inverse, gain_row, grad):
    scaled = grad * gain_row
    first = jnp.mean(scaled, axis=-1, keepdims=True)
    second = jnp.mean(scaled * hat, axis=-1, keepdims=True)
    return inverse * (scaled - first - hat * second)


def segments(lengths, positions):
    first = lengths[0, 0]
    second = first + lengths[0, 1]
    third = second + lengths[0, 2]
    return (
        (positions >= first).astype(jnp.int32)
        + (positions >= second).astype(jnp.int32)
        + (positions >= third).astype(jnp.int32)
    )


def stacked_positions(band, rows):
    lanes = lax.broadcasted_iota(jnp.int32, (1, GROUP * rows), 1)
    for unused in range(1, GROUP):
        lanes = lanes - jnp.where(lanes >= rows, rows, 0)
    return lanes + band * rows


def head_lanes(rows, head_size):
    return lax.broadcasted_iota(jnp.int32, (rows, GROUP * head_size), 1) // head_size


def stack_heads(rows_group, lane_head):
    zero = jnp.zeros_like(rows_group)
    return jnp.concatenate(
        [jnp.where(lane_head == head, rows_group, zero) for head in range(GROUP)], axis=0
    )


def unstack_heads(stacked, lane_head, rows):
    total = jnp.where(lane_head == 0, stacked[:rows], 0.0)
    for head in range(1, GROUP):
        total = jnp.where(lane_head == head, stacked[head * rows : (head + 1) * rows], total)
    return total


def key_chunks(bands, rows):
    step = 2 if (bands - 2) % 2 == 0 else 1
    chunks = [(0, rows)]
    for at in range(1, bands - 1, step):
        chunks.append((at * rows, step * rows))
    chunks.append(((bands - 1) * rows, rows))
    return chunks


class Moves:
    def __init__(self, sems):
        self.sems = sems
        self.pending = {}
        self.count = 0

    def start(self, key, source, target):
        copy = pltpu.make_async_copy(source, target, self.sems.at[self.count])
        copy.start()
        self.count += 1
        self.pending[key] = copy

    def wait(self, key):
        self.pending.pop(key).wait()


GRID = pl.DeviceIdType.MESH
CORE, EDGE_X, EDGE_Y, NEAR_Z, FAR_Z = (
    ("batch", 0),
    ("batch", 1),
    ("seq", 0),
    ("seq", 1),
    ("seq", 2),
)
ORDERS = (
    (CORE, EDGE_X, EDGE_Y, NEAR_Z, FAR_Z),
    (CORE, EDGE_Y, NEAR_Z, EDGE_X, FAR_Z),
    (CORE, NEAR_Z, EDGE_X, EDGE_Y, FAR_Z),
)
STEPS = 5
DEVICES = 1 << STEPS


def place():
    return (lax.axis_index("batch"), lax.axis_index("seq"))


def swapped(number):
    return 2 * lax.rem(number, 2) + number // 2


def band_here():
    batch, seq = place()
    return 2 * swapped(batch) + lax.rem(seq, 2)


def home():
    batch, seq = place()
    return (swapped(seq // 2), 2 * swapped(batch) + lax.rem(seq, 2))


def bit_of(axis, number):
    return lax.rem(lax.axis_index(axis) // (1 << number), 2)


def across(axis, number):
    batch, seq = place()
    step = (1 - 2 * bit_of(axis, number)) * (1 << number)
    return (batch + step, seq) if axis == "batch" else (batch, seq + step)


def announce(partners):
    for partner in partners:
        pl.semaphore_signal(
            pltpu.get_barrier_semaphore(), inc=1, device_id=partner, device_id_type=GRID
        )


def meet(count):
    pl.semaphore_wait(pltpu.get_barrier_semaphore(), count)


def aligned(at, size):
    return pl.ds(pl.multiple_of(at, 16), size)


class Copies:
    def __init__(self, sems):
        self.sems = sems
        self.known = {}
        self.count = 0

    def send(self, key, source, target, partner):
        number = self.count
        self.count += 1
        copy = pltpu.make_async_remote_copy(
            src_ref=source,
            dst_ref=target,
            send_sem=self.sems.at[0, number],
            recv_sem=self.sems.at[1, number],
            device_id=partner,
            device_id_type=GRID,
        )
        copy.start()
        self.known[key] = copy

    def arrive(self, key):
        self.known[key].wait_recv()

    def sent(self, keys):
        for key in keys:
            self.known.pop(key).wait_send()

    def close(self):
        for copy in self.known.values():
            copy.wait_send()


class Layout:
    def __init__(self, sizes):
        self.sizes = sizes
        self.starts = [sum(sizes[:number]) for number in range(len(sizes))]

    def base(self, number, step):
        at, size = (self.starts[number] // 2, self.sizes[number] // 2)
        for axis in ORDERS[number][1:step]:
            size = size // 2
            at = at + bit_of(*axis) * size
        return (at, size)

    def whole_base(self, number, step):
        at, size = self.base(number, step)
        start, half = self.starts[number], self.sizes[number] // 2
        return (at - start // 2 + start + bit_of(*CORE) * half, size)

    def part(self, number):
        return pl.ds(self.starts[number] // DEVICES, self.sizes[number] // DEVICES)


class Reduction:
    def __init__(self, sizes, source, part, held, landing, local_sems, sems, apart_first=False):
        self.layout = Layout(sizes)
        self.sizes = sizes
        self.source, self.part, self.held, self.landing = (source, part, held, landing)
        self.copies = Copies(sems)
        self.moves = Moves(local_sems)
        self.apart_first = apart_first

    def pieces(self, number, part):
        next_bit = bit_of(*ORDERS[number][1])
        piece = (1 - next_bit) if part == 0 else next_bit
        return (piece, self.sizes[number] // 4)

    def begin(self):
        for part in range(2):
            for number, size in enumerate(self.sizes):
                piece, quarter = self.pieces(number, part)
                at = self.layout.starts[number] + (1 - bit_of(*CORE)) * (size // 2)
                landing = self.layout.starts[number] // 2 + part * quarter
                self.copies.send(
                    (number, part),
                    self.source.at[aligned(at + piece * quarter, quarter)],
                    self.landing.at[pl.ds(landing, quarter)],
                    across(*CORE),
                )
        for number, size in enumerate(self.sizes):
            start = self.layout.starts[number]
            self.moves.start(
                number,
                self.source.at[aligned(start + bit_of(*CORE) * (size // 2), size // 2)],
                self.held.at[pl.ds(start // 2, size // 2)],
            )

    def first(self, number, part):
        piece, quarter = self.pieces(number, part)
        if part == 0:
            self.moves.wait(number)
        self.copies.arrive((number, part))
        start = self.layout.starts[number] // 2
        here = aligned(start + piece * quarter, quarter)
        self.held[here, :] = (
            self.held[here, :].astype(WIDE)
            + self.landing[pl.ds(start + part * quarter, quarter), :].astype(WIDE)
        ).astype(LOW)
        if part == 0:
            self.send(number, 1)

    def release(self):
        self.copies.sent([(number, part) for number in range(len(self.sizes)) for part in range(2)])

    def landed(self, number, step):
        start = sum(self.sizes) // 2
        for earlier in range(1, STEPS if self.apart_first and step == 1 else step):
            start += sum(self.sizes) >> (earlier + 1)
        return pl.ds(start + (self.layout.starts[number] >> (step + 1)), self.sizes[number] >> (step + 1))

    def send(self, number, step):
        axis = ORDERS[number][step]
        at, size = self.layout.base(number, step)
        size = size // 2
        self.copies.send(
            (number, "at", step),
            self.held.at[aligned(at + (1 - bit_of(*axis)) * size, size)],
            self.landing.at[self.landed(number, step)],
            across(*axis),
        )

    def add(self, number, step):
        at, size = self.layout.base(number, step + 1)
        self.copies.arrive((number, "at", step))
        summed = (
            self.held[aligned(at, size), :].astype(WIDE)
            + self.landing[self.landed(number, step), :].astype(WIDE)
        ).astype(LOW)
        if step + 1 < STEPS:
            self.held[aligned(at, size), :] = summed
            self.send(number, step + 1)
        else:
            self.part[self.layout.part(number), :] = summed
            if number == len(self.sizes) - 1:
                self.copies.close()

    def tasks(self):
        numbers = range(len(self.sizes))
        steps = [self.begin]
        steps += [functools.partial(self.first, number, part) for part in range(2) for number in numbers]
        steps += [
            functools.partial(self.add, number, step) for step in range(1, STEPS) for number in numbers
        ]
        return steps

    @staticmethod
    def scratch(sizes, apart_first):
        rows = sum(sizes)
        landing = sum(rows >> step for step in range(1, STEPS + 1))
        if apart_first:
            landing += rows >> 2
        return [
            pltpu.VMEM((rows // 2, 512), LOW),
            pltpu.VMEM((landing, 512), LOW),
            pltpu.SemaphoreType.DMA((len(sizes),)),
            pltpu.SemaphoreType.DMA((2, 6 * len(sizes))),
        ]


class Sharing:
    def __init__(self, sizes, part, total, local_sems, sems):
        self.layout = Layout(sizes)
        self.sizes = sizes
        self.part, self.total, self.local = (part, total, local_sems)
        self.met = False
        self.copies = Copies(sems)

    def rows(self, number, step):
        return aligned(*self.layout.whole_base(number, step))

    def stay(self, number):
        return pltpu.make_async_copy(
            self.part.at[self.layout.part(number)],
            self.total.at[self.rows(number, STEPS)],
            self.local.at[number],
        )

    def begin(self):
        for number in range(len(self.sizes)):
            self.stay(number).start()
        for number in range(len(self.sizes)):
            self.stay(number).wait()
            self.share(number, STEPS - 1)
            self.pass_on(number, STEPS)

    def share(self, number, step):
        rows = self.rows(number, step + 1)
        self.copies.send(
            (number, step),
            self.total.at[rows],
            self.total.at[rows],
            across(*ORDERS[number][step]),
        )

    def pass_on(self, number, step):
        if step == STEPS:
            rows = self.rows(number, STEPS)
        else:
            at, size = self.layout.whole_base(number, step)
            size = size // 2
            rows = aligned(at + (1 - bit_of(*ORDERS[number][step])) * size, size)
        self.copies.send(
            (number, "pass", step), self.total.at[rows], self.total.at[rows], across(*CORE)
        )

    def gather(self, number, step):
        self.copies.arrive((number, step))
        if step > 1:
            self.share(number, step - 1)
        self.pass_on(number, step)

    def core_began(self):
        if not self.met:
            self.met = True
            for number in range(len(self.sizes)):
                self.copies.arrive((number, "pass", STEPS))

    def end(self):
        self.core_began()
        for step in range(STEPS - 1, 0, -1):
            for number in range(len(self.sizes)):
                self.copies.arrive((number, "pass", step))
        self.copies.close()

    def tasks(self):
        steps = [self.begin]
        steps += [
            functools.partial(self.gather, number, step)
            for step in range(STEPS - 1, 0, -1)
            for number in range(len(self.sizes))
        ]
        return steps + [self.end]

    @staticmethod
    def scratch(sizes):
        return [
            pltpu.SemaphoreType.DMA((len(sizes),)),
            pltpu.SemaphoreType.DMA((2, 9 * len(sizes))),
        ]


class SmallSum:
    def __init__(self, total, landing, sems):
        self.total, self.landing = (total, landing)
        self.copies = Copies(sems)

    def send(self, step):
        self.copies.send(
            step, self.landing.at[STEPS + step], self.landing.at[step], across(*ORDERS[0][step])
        )

    def add(self, step):
        self.copies.arrive(step)
        summed = self.landing[STEPS + step] + self.landing[step]
        if step + 1 < STEPS:
            self.landing[STEPS + step + 1] = summed
            self.send(step + 1)
        else:
            self.total[...] = summed
            self.copies.close()

    def tasks(self):
        return [functools.partial(self.send, 0)] + [
            functools.partial(self.add, step) for step in range(STEPS)
        ]

    @staticmethod
    def scratch():
        return [
            pltpu.VMEM((2 * STEPS, 8, 512), WIDE),
            pltpu.SemaphoreType.DMA((2, STEPS)),
        ]


class Gathering:
    def __init__(self, whole_ref, rows, sems):
        self.whole, self.rows = (whole_ref, rows)
        self.copies = Copies(sems)
        self.band = band_here()
        self.x = self.band + 2 * (1 - 2 * bit_of(*EDGE_X))
        self.y = self.band + 1 - 2 * bit_of(*EDGE_Y)
        self.corner = self.x + self.y - self.band

    def send(self, key, band, axis, half=None):
        start, size = (band * self.rows, self.rows)
        if half is not None:
            size = size // 2
            start = start + half * size
        ref = self.whole.at[aligned(start, size)]
        self.copies.send(key, ref, ref, across(*axis))

    def begin(self):
        self.send("x", self.band, EDGE_X)
        self.send("y", self.band, EDGE_Y)
        self.send("core", self.band, CORE)

    def from_x(self):
        self.copies.arrive("x")
        self.send("corner 0", self.x, EDGE_Y, 0)
        self.send("core x", self.x, CORE)

    def from_y(self):
        self.copies.arrive("y")
        self.send("corner 1", self.y, EDGE_X, 1)
        self.send("core y", self.y, CORE)

    def from_corner(self, half):
        self.copies.arrive("corner %d" % half)
        self.send("core corner %d" % half, self.corner, CORE, half)

    def end(self):
        for key in ("core", "core x", "core y", "core corner 0", "core corner 1"):
            self.copies.arrive(key)
        self.copies.close()

    def tasks(self):
        corners = [functools.partial(self.from_corner, half) for half in range(2)]
        return [self.begin, self.from_x, self.from_y, *corners, self.end]

    @staticmethod
    def scratch():
        return [pltpu.SemaphoreType.DMA((2, 9))]


class Scattering:
    def __init__(self, source, held, landing, local_sems, sems, rows, finish):
        self.source, self.held, self.landing, self.rows, self.finish = (
            source,
            held,
            landing,
            rows,
            finish,
        )
        self.copies = Copies(sems)
        self.moves = Moves(local_sems)
        half = source.shape[1] // 2
        self.lanes = (slice(0, half), slice(half, 2 * half))

    def begin(self):
        size = 4 * self.rows
        self.copies.send(
            "core",
            self.source.at[aligned((1 - bit_of(*CORE)) * size, size)],
            self.landing.at[pl.ds(0, size)],
            across(*CORE),
        )
        self.moves.start("core", self.source.at[aligned(bit_of(*CORE) * size, size)], self.held)

    def first(self):
        rows = self.rows
        self.moves.wait("core")
        self.copies.arrive("core")
        self.held[...] = (
            self.held[...].astype(WIDE) + self.landing[pl.ds(0, 4 * rows), :].astype(WIDE)
        ).astype(LOW)
        x, y = (bit_of(*EDGE_X), bit_of(*EDGE_Y))
        self.copies.send(
            "x",
            self.held.at[aligned(2 * (1 - x) * rows, 2 * rows), self.lanes[0]],
            self.landing.at[pl.ds(4 * rows, 2 * rows), self.lanes[0]],
            across(*EDGE_X),
        )
        for other in range(2):
            self.copies.send(
                ("y", other),
                self.held.at[aligned((2 * other + 1 - y) * rows, rows), self.lanes[1]],
                self.landing.at[pl.ds((4 + other) * rows, rows), self.lanes[1]],
                across(*EDGE_Y),
            )

    def second(self):
        rows = self.rows
        x, y = (bit_of(*EDGE_X), bit_of(*EDGE_Y))
        self.copies.arrive("x")
        here = aligned(2 * x * rows, 2 * rows)
        self.held[here, self.lanes[0]] = (
            self.held[here, self.lanes[0]].astype(WIDE)
            + self.landing[pl.ds(4 * rows, 2 * rows), self.lanes[0]].astype(WIDE)
        ).astype(LOW)
        self.copies.send(
            "then y",
            self.held.at[aligned((2 * x + 1 - y) * rows, rows), self.lanes[0]],
            self.landing.at[pl.ds(6 * rows, rows), self.lanes[0]],
            across(*EDGE_Y),
        )
        for other in range(2):
            self.copies.arrive(("y", other))
            here = aligned((2 * other + y) * rows, rows)
            self.held[here, self.lanes[1]] = (
                self.held[here, self.lanes[1]].astype(WIDE)
                + self.landing[pl.ds((4 + other) * rows, rows), self.lanes[1]].astype(WIDE)
            ).astype(LOW)
        self.copies.send(
            "then x",
            self.held.at[aligned((2 * (1 - x) + y) * rows, rows), self.lanes[1]],
            self.landing.at[pl.ds(6 * rows, rows), self.lanes[1]],
            across(*EDGE_X),
        )

    def third(self):
        rows = self.rows
        self.copies.arrive("then y")
        self.copies.arrive("then x")
        here = aligned((2 * bit_of(*EDGE_X) + bit_of(*EDGE_Y)) * rows, rows)
        self.finish(
            self.held[here, :].astype(WIDE) + self.landing[pl.ds(6 * rows, rows), :].astype(WIDE)
        )
        self.copies.close()

    def tasks(self):
        return [self.begin, self.first, self.second, self.third]

    @staticmethod
    def scratch(rows):
        return [
            pltpu.VMEM((4 * rows, 512), LOW),
            pltpu.VMEM((7 * rows, 512), LOW),
            pltpu.SemaphoreType.DMA((2,)),
            pltpu.SemaphoreType.DMA((2, 7)),
        ]


class Homing:
    def __init__(self, source, target, sems):
        batch, seq = place()
        partner = home()
        self.here = (partner[0] == batch) & (partner[1] == seq)
        self.stay = pltpu.make_async_copy(source, target, sems.at[0])
        self.go = pltpu.make_async_remote_copy(
            src_ref=source,
            dst_ref=target,
            send_sem=sems.at[0],
            recv_sem=sems.at[1],
            device_id=partner,
            device_id_type=GRID,
        )

    def start(self):
        @pl.when(self.here)
        def _():
            self.stay.start()

        @pl.when(jnp.logical_not(self.here))
        def _():
            self.go.start()

    def wait(self):
        @pl.when(self.here)
        def _():
            self.stay.wait()

        @pl.when(jnp.logical_not(self.here))
        def _():
            self.go.wait()

    def tasks(self):
        return [self.start, self.wait]


def announce_home():
    batch, seq = place()
    partner = home()

    @pl.when((partner[0] != batch) | (partner[1] != seq))
    def _():
        announce([partner])


def meet_with_home(count):
    batch, seq = place()
    partner = home()
    here = (partner[0] == batch) & (partner[1] == seq)

    @pl.when(jnp.logical_not(here))
    def _():
        meet(count + 1)

    if count:

        @pl.when(here)
        def _():
            meet(count)


HOMING = [pltpu.SemaphoreType.DMA((2,))]


whole = pl.BlockSpec(memory_space=pltpu.VMEM)
scalars = pl.BlockSpec(memory_space=pltpu.SMEM)
apart = pl.BlockSpec(memory_space=pl.ANY)

def settings(number, limit=vmem_bytes):
    if number is None:
        return pltpu.CompilerParams(vmem_limit_bytes=limit)
    return pltpu.CompilerParams(
        vmem_limit_bytes=limit, collective_id=number, has_side_effects=True
    )


def cost(flops):
    return pl.CostEstimate(flops=int(flops), bytes_accessed=40 << 20, transcendentals=0)


class Names:
    def __init__(self, refs):
        self.refs = list(refs)

    def take(self, count):
        taken, self.refs = (self.refs[:count], self.refs[count:])
        return taken

    def share(self, lists):
        return [self.take(len(item)) for item in lists]


def flat(lists):
    return [item for items in lists for item in items]


GATHER_DUE = (
    (8.99000, 8.99002, 8.99004, 8.99006, 8.99008, 8.99010),
    (48.99022, 63.89040, 63.89042, 73.89050, 75.89052, 79.99062),
)
SCATTER_DUE = (
    (82.99078, 88.49090, 99.79192, 103.49130),
    (138.99192, 138.99398, 139.00136, 139.00552),
)
EARLY_REDUCE_DUE = (
    (54.49024, 57.89026, 57.89028, 57.89030, 59.89032, 59.89034, 59.89036, 71.89048, 69.89044, 69.89046, 79.99058, 76.49054, 79.99060, 86.09080, 82.99076, 86.09082, 92.79180, 90.64132, 92.79182),
    (110.49148, 113.89152, 113.89154, 113.89156, 115.89158, 115.89160, 115.89162, 138.99190, 125.89174, 135.99182, 138.99504, 138.99606, 138.99396, 139.00020, 139.00132, 138.99708, 139.00344, 139.00446, 139.00134),
)
EARLY_SHARE_DUE = (
    (92.79184, 99.79194, 101.49116, 103.49120, 103.49128, 103.49134, 106.99138, 108.99146, 117.89168, 117.89170, 127.89180, 135.99184, 138.99502, 138.99710),
    (139.00448, 139.00760, 139.00966, 139.01070, 139.01276, 139.01172, 139.01274, 139.01692, 139.01588, 139.01690, 139.02306, 139.02100, 139.02304, 139.02512),
)
LATE_REDUCE_DUE = (
    (79.99056, 82.99064, 82.99066, 82.99068, 82.99070, 82.99072, 82.99074, 88.49084, 88.49086, 88.49088, 92.79174, 92.79176, 92.79178, 97.64146, 99.79188, 99.79190, 103.49118, 103.49122, 103.49124),
    (138.99916, 139.00018, 139.00022, 139.00124, 139.00126, 139.00128, 139.00130, 139.00238, 139.00340, 139.00342, 139.00550, 139.00656, 139.00658, 139.00862, 139.01068, 139.00864, 139.01380, 139.01482, 139.01484),
)
LATE_SHARE_DUE = (
    (103.49126, 108.99140, 108.99142, 108.99144, 125.89172, 117.89166, 113.89150, 138.99188, 135.99186, 127.89178, 138.99500, 138.99294, 138.99812, 138.99914),
    (139.01486, 139.01794, 139.01896, 139.01998, 139.02408, 139.02410, 139.02202, 139.02614, 139.02616, 139.02618, 139.02720, 139.02722, 139.02724, 139.02826),
)
HOME_DUE = (
    (48.99020, 61.89038),
    (104.99136, 127.89176),
    (103.49132, 115.89164),
    (139.00554, 139.01378),
)


QUERY_LANES = 512


class Schedule:
    def __init__(self):
        self.waiting = []
        self.now = 0.0
        self.base = 0.0

    def add(self, due, tasks):
        self.waiting += zip(due, tasks, strict=True)
        self.waiting.sort(key=lambda task: task[0])

    def stage(self, base):
        self.base = base
        self.tick(0.0)

    def tick(self, now):
        self.now = self.base + now
        while self.waiting and self.waiting[0][0] <= self.now:
            self.waiting.pop(0)[1]()

    def require(self, last):
        while any(task == last for unused, task in self.waiting):
            self.waiting.pop(0)[1]()

    def drain(self):
        while self.waiting:
            self.waiting.pop(0)[1]()


def load_early(moves, block, hbm, target):
    unused, out_hbm, up_hbm, down_hbm = hbm
    width = target.shape[1]
    fan = up_hbm.shape[2]
    for number in range(fan // width):
        moves.start(
            ("up", block, number),
            up_hbm.at[block, :, pl.ds(number * width, width)],
            target.at[pl.ds(number * width, width)],
        )
    moves.start(("down", block), down_hbm.at[block], target.at[pl.ds(fan, fan)])
    moves.start(("out", block), out_hbm.at[block], target.at[pl.ds(2 * fan, width)])


def load_late(moves, block, hbm, target):
    width = target.shape[2]
    for number in range(3):
        moves.start(
            ("qkv", block, number),
            hbm[0].at[block, :, pl.ds(number * width, width)],
            target.at[block, pl.ds(number * width, width)],
        )


def forward_pass(block, schedule, moves, lengths, gains_ref, spill, r):
    tick = schedule.tick
    rows, width = r.moved.shape
    total = r.kv.shape[0]
    fan = r.hidden.shape[1]
    head_size = width // HEADS
    group_width = GROUP * head_size
    groups = width // group_width
    stacked = GROUP * rows
    band = band_here()
    lane_head = head_lanes(rows, head_size)
    chunks = key_chunks(total // rows, rows)
    image_query = segments(lengths, stacked_positions(band, rows))
    is_image = image_query == 1
    inputs_ref = r.moved if block == 0 else r.outputs.at[0]
    normed_all = r.normed.at[block]
    matrices = r.late_matrices.at[block]
    for number in range(3):
        moves.wait(("qkv", block, number))
    own = normed_all[aligned(band * rows, rows), :]
    query = product(own, matrices[:width], NN).astype(LOW)
    query = query * jnp.asarray(head_size ** (-0.5), LOW)
    for group in range(groups):
        lanes = slice(group * group_width, (group + 1) * group_width)
        r.query_stack[group] = stack_heads(query[:, lanes], lane_head)
    tick(1.0)
    for number, (start, size) in enumerate(chunks):
        at = slice(start, start + size)
        rows_here = normed_all[at]
        for part in range(2):
            r.kv[at, part * width : (part + 1) * width] = product(
                rows_here, matrices[(part + 1) * width : (part + 2) * width], NN
            ).astype(LOW)
    tick(3.1)
    for group in range(groups):
        base = 3.5 + 7.0 * group
        lanes = slice(group * group_width, (group + 1) * group_width)
        value_lanes = slice(width + group * group_width, width + (group + 1) * group_width)
        if group > 0:
            moves.wait(("spill", block, group - 1))
        attended, inverses = ([], [])
        for lane in range(0, stacked, QUERY_LANES):
            size_lanes = min(QUERY_LANES, stacked - lane)
            here = slice(lane, lane + size_lanes)
            stack = r.query_stack[group, here]
            edge_max = None
            middle_max = None
            for number, (start, size) in enumerate(chunks):
                scores = product(r.kv[start : start + size, lanes], stack, NT)
                edge = number in (0, len(chunks) - 1)
                if edge:
                    positions = start + lax.broadcasted_iota(jnp.int32, (size, 1), 0)
                    allowed = segments(lengths, positions) == image_query[:, here]
                    scores = jnp.where(allowed, scores, masked_score)
                r.scores[start : start + size, :size_lanes] = scores
                top = jnp.max(scores, axis=0, keepdims=True)
                if edge:
                    edge_max = top if edge_max is None else jnp.maximum(edge_max, top)
                else:
                    middle_max = top if middle_max is None else jnp.maximum(middle_max, top)
            image = is_image[:, here]
            row_max = jnp.maximum(edge_max, jnp.where(image, middle_max, masked_score))
            inner_max = jnp.where(image, row_max, -masked_score)
            totals = None
            gathered = None
            for number, (start, size) in enumerate(chunks):
                edge = number in (0, len(chunks) - 1)
                weights = jnp.exp(
                    r.scores[start : start + size, :size_lanes] - (row_max if edge else inner_max)
                )
                part = jnp.sum(weights, axis=0, keepdims=True)
                totals = part if totals is None else totals + part
                low = weights.astype(LOW)
                r.weights[start : start + size, here] = low
                piece = product(low, r.kv[start : start + size, value_lanes], TN)
                gathered = piece if gathered is None else gathered + piece
            attended.append(gathered)
            inverses.append(1.0 / totals)
            tick(base + lane * 0.0042 + 2.0)
        if group + 1 < groups:
            moves.start(("spill", block, group), r.weights, spill.at[group])
        columns = jnp.transpose(
            jnp.broadcast_to(jnp.concatenate(inverses, axis=1), (128, stacked))
        )
        inverse = unstack_heads(
            jnp.concatenate([columns] * (group_width // 128), axis=1), lane_head, rows
        )
        r.inverse[:, lanes] = inverse
        r.attended[:, lanes] = (
            unstack_heads(jnp.concatenate(attended, axis=0), lane_head, rows) * inverse
        )
    positions = band * rows + lax.broadcasted_iota(jnp.int32, (rows, 1), 0)
    keep_rows = (segments(lengths, positions) < 3).astype(WIDE)
    low = (r.attended[...] * keep_rows).astype(LOW)
    moves.wait(("out", block))
    middle = inputs_ref[...].astype(WIDE) + product(low, r.early_matrices[2 * fan :], NN)
    r.middle[...] = middle
    hat, unused = normalise(middle)
    second = (hat * gains_ref[block, 1:2, :]).astype(LOW)
    tick(18.5)
    for number in range(fan // width):
        moves.wait(("up", block, number))
        here = slice(number * width, (number + 1) * width)
        up_rows = product(second, r.early_matrices[here], NN)
        square = up_rows * up_rows
        bend = jnp.tanh(0.7978845608028654 * (up_rows + 0.044715 * square * up_rows))
        half = 0.5 * (1.0 + bend)
        r.hidden[:, here] = (up_rows * half).astype(LOW)
        r.slope[:, here] = (
            half
            + 0.5
            * up_rows
            * (1.0 - bend * bend)
            * (0.7978845608028654 * (1.0 + (3 * 0.044715) * square))
        ).astype(LOW)
    moves.wait(("down", block))
    tick(20.5)
    output = (middle + product(r.hidden[...], r.early_matrices[fan : 2 * fan], NN)).astype(LOW)
    r.outputs[block] = output
    if block == 0:
        hat, unused = normalise(output.astype(WIDE))
        r.normed[1, aligned(band * rows, rows), :] = (hat * gains_ref[1, 0:1, :]).astype(LOW)


def backward_pass(block, schedule, moves, lengths, gains_ref, spill, r, begin_early, begin_late):
    tick = schedule.tick
    rows, width = r.moved.shape
    total = r.kv.shape[0]
    fan = r.hidden.shape[1]
    head_size = width // HEADS
    group_width = GROUP * head_size
    groups = width // group_width
    band = band_here()
    lane_head = head_lanes(rows, head_size)
    chunks = key_chunks(total // rows, rows)
    normed_all = r.normed.at[block]
    matrices = r.late_matrices.at[block]
    early = r.early_matrices
    gain_terms = r.small.at[STEPS]

    def reload(group, number):
        at = pl.ds(*chunks[number])
        moves.start(("reload", block, group, number), spill.at[group, at], r.weights.at[at])

    order = tuple(reversed(range(groups)))
    grad = r.grads[block]
    grad_hidden = product(grad, early[fan : 2 * fan], NT)
    grad_up = (grad_hidden * r.slope[...].astype(WIDE)).astype(LOW)
    early[fan : 2 * fan] = product(r.hidden[...], grad, TN).astype(LOW)
    tick(2.0)
    hat, inverse = normalise(r.middle[...])
    second = (hat * gains_ref[block, 1:2, :]).astype(LOW)
    grad_second = None
    for number in range(fan // width):
        here = slice(number * width, (number + 1) * width)
        piece = product(grad_up[:, here], early[here], NT)
        grad_second = piece if grad_second is None else grad_second + piece
    for number in range(fan // width):
        here = slice(number * width, (number + 1) * width)
        early[here] = product(second, grad_up[:, here], TN).astype(LOW)
    tick(4.0)
    gain_terms[2 * block + 1 : 2 * block + 2, :] = jnp.sum(grad_second * hat, axis=0, keepdims=True)
    grad_middle = grad.astype(WIDE) + normalise_back(
        hat, inverse, gains_ref[block, 1:2, :], grad_second
    )
    r.middle_grad[...] = grad_middle
    grad_branch = grad_middle.astype(LOW)
    positions = band * rows + lax.broadcasted_iota(jnp.int32, (rows, 1), 0)
    keep_rows = (segments(lengths, positions) < 3).astype(WIDE)
    grad_attended = product(grad_branch, early[2 * fan :], NT) * keep_rows
    low = (r.attended[...] * keep_rows).astype(LOW)
    early[2 * fan :] = product(low, grad_branch, TN).astype(LOW)
    begin_early()
    tick(5.5)
    scaled = (grad_attended * r.inverse[...]).astype(LOW)
    ones = jnp.ones((8, group_width), LOW)
    deltas = []
    for group in range(groups):
        lanes = slice(group * group_width, (group + 1) * group_width)
        stack = stack_heads(scaled[:, lanes], lane_head)
        r.grad_stack[group] = stack
        dots = stack.astype(WIDE) * jnp.concatenate([r.attended[:, lanes]] * GROUP, axis=0)
        high = dots.astype(LOW)
        rest = (dots - high.astype(WIDE)).astype(LOW)
        deltas.append((product(ones, high, NT) + product(ones, rest, NT))[0:1])
    tick(7.0)
    query_grads = [None] * groups
    for turn, group in enumerate(order):
        lanes = slice(group * group_width, (group + 1) * group_width)
        value_lanes = slice(width + group * group_width, width + (group + 1) * group_width)
        collected = None
        for number, (start, size) in enumerate(chunks):
            base = 7.0 + 10.0 * turn + 2.0 * number
            at = slice(start, start + size)
            if turn > 0:
                moves.wait(("reload", block, group, number))
            low = r.weights[at]
            grad_weights = product(r.kv[at, value_lanes], r.grad_stack[group], NT)
            grad_scores = (low.astype(WIDE) * (grad_weights - deltas[group])).astype(LOW)
            r.kv[at, value_lanes] = product(low, r.grad_stack[group], NN).astype(LOW)
            piece = product(grad_scores, r.kv[at, lanes], TN)
            collected = piece if collected is None else collected + piece
            r.kv[at, lanes] = product(grad_scores, r.query_stack[group], NN).astype(LOW)
            if turn + 1 < groups:
                reload(order[turn + 1], number)
            tick(base + 1.9)
        query_grads[group] = unstack_heads(collected, lane_head, rows)
    query_grad = (jnp.concatenate(query_grads, axis=1) * head_size ** (-0.5)).astype(LOW)
    tick(27.5)
    here = aligned(band * rows, rows)
    own = normed_all[here, :]
    r.late_terms[:width] = product(own, query_grad, TN).astype(LOW)
    for part in range(2):
        r.late_terms[(part + 1) * width : (part + 2) * width] = product(
            normed_all[...], r.kv[:, part * width : (part + 1) * width], TN
        ).astype(LOW)
    begin_late()
    tick(31.0)
    query_part = product(query_grad, matrices[:width], NT)
    r.query_grad[...] = query_part
    gain_row = jnp.sum(query_part * own.astype(WIDE), axis=0, keepdims=True)
    for start, size in chunks:
        at = slice(start, start + size)
        normed_grad = product(r.kv[at, :width], matrices[width : 2 * width], NT) + product(
            r.kv[at, width:], matrices[2 * width :], NT
        )
        piece = normed_all[at].astype(WIDE)
        gain_row = gain_row + jnp.sum(normed_grad * piece, axis=0, keepdims=True)
        normed_all[at] = normed_grad.astype(LOW)
    gain_terms[2 * block : 2 * block + 1, :] = gain_row / gains_ref[block, 0:1, :]


def inputs_back(block, inputs_ref, gains_ref, r, summed):
    hat, inverse = normalise(inputs_ref[...].astype(WIDE))
    return (
        r.middle_grad[...]
        + normalise_back(hat, inverse, gains_ref[block, 0:1, :], summed + r.query_grad[...])
    ).astype(LOW)


LATE = (512, 512, 512)
EARLY = (1536, 1536, 1536)


class Holder:
    pass


def scratch_plan(rows, width, total, fan):
    groups = HEADS // GROUP
    gw = width // groups
    stacked = GROUP * rows
    plan = {
        "moved": pltpu.VMEM((rows, width), LOW),
        "grads": pltpu.VMEM((2, rows, width), LOW),
        "normed": pltpu.VMEM((2, total, width), LOW),
        "late_matrices": pltpu.VMEM((2, 3 * width, width), LOW),
        "early_matrices": pltpu.VMEM((2 * fan + width, width), LOW),
        "late_terms": pltpu.VMEM((3 * width, width), LOW),
        "query_stack": pltpu.VMEM((groups, stacked, gw), LOW),
        "grad_stack": pltpu.VMEM((groups, stacked, gw), LOW),
        "scores": pltpu.VMEM((total, QUERY_LANES), WIDE),
        "weights": pltpu.VMEM((total, stacked), LOW),
        "kv": pltpu.VMEM((total, 2 * width), LOW),
        "attended": pltpu.VMEM((rows, width), WIDE),
        "inverse": pltpu.VMEM((rows, width), WIDE),
        "middle": pltpu.VMEM((rows, width), WIDE),
        "hidden": pltpu.VMEM((rows, fan), LOW),
        "slope": pltpu.VMEM((rows, fan), LOW),
        "outputs": pltpu.VMEM((2, rows, width), LOW),
        "middle_grad": pltpu.VMEM((rows, width), WIDE),
        "query_grad": pltpu.VMEM((rows, width), WIDE),
        "inputs_grad": pltpu.VMEM((2, rows, width), LOW),
        "late_part": pltpu.VMEM((2, sum(LATE) // DEVICES, width), LOW),
        "early_part": pltpu.VMEM((2, sum(EARLY) // DEVICES, width), LOW),
        "small": pltpu.VMEM((2 * STEPS, 8, width), WIDE),
        "small_sems": pltpu.SemaphoreType.DMA((2, STEPS)),
        "home_sems": pltpu.SemaphoreType.DMA((7, 2)),
        "sems": pltpu.SemaphoreType.DMA((64,)),
    }
    return plan


def buffers(rows):
    return [
        Scattering.scratch(rows)[:2],
        Reduction.scratch(LATE, False)[:2],
        Reduction.scratch(EARLY, True)[:2],
    ]


def block_scratch(rows):
    return [
        Gathering.scratch(),
        Reduction.scratch(LATE, False)[2:],
        Reduction.scratch(EARLY, True)[2:],
        Sharing.scratch(LATE),
        Sharing.scratch(EARLY),
        Scattering.scratch(rows)[2:],
    ]


def blocks_kernel(
    lengths, gains_ref, tokens_ref, gen_grad_ref, disc_grad_ref, qkv_hbm, out_hbm, up_hbm, down_hbm,
    gen_out_ref, disc_out_ref, gen_in_ref, disc_in_ref, gen_late_ref, disc_late_ref, gen_early_ref,
    disc_early_ref, gain_total_ref, spill, *refs,
):
    rows, width = tokens_ref.shape
    total = 8 * rows
    fan = up_hbm.shape[2]
    plan = scratch_plan(rows, width, total, fan)
    r = Holder()
    for name, ref in zip(plan, refs):
        setattr(r, name, ref)
    refs = Names(refs[len(plan) :])
    scatter, late, early = refs.share(buffers(rows))
    passes = [refs.share(block_scratch(rows)) for unused in range(2)]
    hbm = (qkv_hbm, out_hbm, up_hbm, down_hbm)
    moves = Moves(r.sems)
    schedule = Schedule()

    announce_home()
    announce([across(*axis) for axis in ORDERS[0]])
    load_late(moves, 0, hbm, r.late_matrices)
    load_early(moves, 0, hbm, r.early_matrices)
    load_late(moves, 1, hbm, r.late_matrices)
    r.small[STEPS] = jnp.zeros((8, width), WIDE)
    meet_with_home(STEPS)
    homes = [
        Homing(source, target, r.home_sems.at[number])
        for number, (source, target) in enumerate(
            [
                (tokens_ref, r.moved),
                (gen_grad_ref, r.grads.at[0]),
                (disc_grad_ref, r.grads.at[1]),
                (r.outputs.at[0], gen_out_ref),
                (r.outputs.at[1], disc_out_ref),
                (r.inputs_grad.at[0], gen_in_ref),
                (r.inputs_grad.at[1], disc_in_ref),
            ]
        )
    ]
    homes[0].start()
    homes[0].wait()
    gatherings = [Gathering(r.normed.at[block], rows, *passes[block][0]) for block in range(2)]
    hat, unused = normalise(r.moved[...].astype(WIDE))
    r.normed[0, aligned(gatherings[0].band * rows, rows), :] = (
        hat * gains_ref[0, 0:1, :]
    ).astype(LOW)
    schedule.stage(9.0)
    schedule.add(GATHER_DUE[0], gatherings[0].tasks())
    homes[1].start()
    homes[2].start()
    schedule.require(gatherings[0].end)
    schedule.stage(27.0)
    forward_pass(0, schedule, moves, lengths, gains_ref, spill, r)

    scatterings = {}
    first_sharing = []

    def begin_after(ready, begin):
        ready()
        begin()

    totals = ((gen_late_ref, gen_early_ref), (disc_late_ref, disc_early_ref))

    def begin_early(block):
        reduction = Reduction(
            EARLY, r.early_matrices, r.early_part.at[block], *early, *passes[block][2], block == 1
        )
        sharing = Sharing(EARLY, r.early_part.at[block], totals[block][1], *passes[block][4])
        steps = reduction.tasks()
        if block == 0:
            first_sharing.append(sharing)
        else:
            steps[0] = functools.partial(begin_after, first_sharing[0].core_began, steps[0])
        schedule.add(EARLY_REDUCE_DUE[block], steps)
        schedule.add(EARLY_SHARE_DUE[block], sharing.tasks())
        if block == 0:

            def refill():
                reduction.release()
                load_early(moves, 1, hbm, r.early_matrices)

            schedule.add(EARLY_REDUCE_DUE[0][7:8], [refill])

    def begin_late(block):
        reduction = Reduction(LATE, r.late_terms, r.late_part.at[block], *late, *passes[block][1])
        sharing = Sharing(LATE, r.late_part.at[block], totals[block][0], *passes[block][3])
        schedule.add(LATE_REDUCE_DUE[block], reduction.tasks())
        schedule.add(LATE_SHARE_DUE[block], sharing.tasks())

    def begin_scatter(block):
        inputs_ref = r.moved if block == 0 else r.outputs.at[0]

        def finish(summed):
            r.inputs_grad[block] = inputs_back(block, inputs_ref, gains_ref, r, summed)

        scatterings[block] = Scattering(
            r.normed.at[block], *scatter, *passes[block][5], rows, finish
        )
        schedule.add(SCATTER_DUE[block], scatterings[block].tasks())
        schedule.add(HOME_DUE[2 + block], homes[5 + block].tasks())

    homes[1].wait()
    homes[2].wait()
    schedule.add(GATHER_DUE[1], gatherings[1].tasks())
    schedule.add(HOME_DUE[0], homes[3].tasks())
    schedule.stage(49.0)
    backward_pass(
        0, schedule, moves, lengths, gains_ref, spill, r,
        functools.partial(begin_early, 0), functools.partial(begin_late, 0),
    )
    begin_scatter(0)
    schedule.stage(83.0)
    schedule.require(gatherings[1].end)
    forward_pass(1, schedule, moves, lengths, gains_ref, spill, r)
    schedule.require(scatterings[0].third)
    schedule.add(HOME_DUE[1], homes[4].tasks())
    schedule.stage(105.0)
    backward_pass(
        1, schedule, moves, lengths, gains_ref, spill, r,
        functools.partial(begin_early, 1), functools.partial(begin_late, 1),
    )
    begin_scatter(1)
    small = SmallSum(gain_total_ref, r.small, r.small_sems)
    schedule.add([139.0 + 0.006 * step for step in range(1 + STEPS)], small.tasks())
    schedule.drain()


def run_blocks(lengths, gains, tokens, gen_grad, disc_grad, matrices):
    rows, width = tokens.shape
    total = 8 * rows
    fan = matrices[2].shape[2]
    shape = jax.ShapeDtypeStruct
    scratch = list(scratch_plan(rows, width, total, fan).values())
    scratch += flat(buffers(rows)) + flat(block_scratch(rows)) * 2
    return pl.pallas_call(
        blocks_kernel,
        out_shape=[shape((rows, width), LOW)] * 4
        + [shape((sum(LATE), width), LOW)] * 2
        + [shape((sum(EARLY), width), LOW)] * 2
        + [
            shape((8, width), WIDE),
            shape((HEADS // GROUP - 1, total, GROUP * rows), LOW),
        ],
        in_specs=[scalars, whole] + [apart] * 7,
        out_specs=[apart] * 8 + [whole, apart],
        scratch_shapes=scratch,
        compiler_params=settings(1),
        cost_estimate=cost(80e9),
        name="blocks",
    )(lengths, gains, tokens, gen_grad, disc_grad, *matrices)[:9]


def emit_kernel(
    late_refs, early_refs, small_refs, out_refs, small_out_refs, read, written, sems, *small_held
):
    width = read.shape[2]
    qkv_ref, out_ref, up_ref, down_ref = out_refs
    items = []
    for block, (late, early) in enumerate(zip(late_refs, early_refs, strict=True)):
        for target, source, at, count in (
            (qkv_ref, late, 0, qkv_ref.shape[2] // width),
            (up_ref, early, 0, up_ref.shape[2] // width),
            (out_ref, early, up_ref.shape[2] + down_ref.shape[1], 1),
        ):
            for number in range(count):
                items.append(
                    (
                        source.at[pl.ds(at + number * width, width)],
                        target.at[block, :, pl.ds(number * width, width)],
                    )
                )
        for number in range(down_ref.shape[1] // width):
            items.append(
                (
                    early.at[pl.ds(up_ref.shape[2] + number * width, width)],
                    down_ref.at[block, pl.ds(number * width, width)],
                )
            )
    slots = read.shape[0]
    small_loads, small_stores = (
        [
            pltpu.make_async_copy(source, target, sems.at[2, number])
            for number, (source, target) in enumerate(zip(sources, targets, strict=True))
        ]
        for sources, targets in ((small_refs, small_held), (small_held, small_out_refs))
    )
    for load in small_loads:
        load.start()
    loads = [
        pltpu.make_async_copy(source, read.at[number % slots], sems.at[0, number % slots])
        for number, (source, unused) in enumerate(items)
    ]
    stores = [
        pltpu.make_async_copy(written.at[number % slots], target, sems.at[1, number % slots])
        for number, (unused, target) in enumerate(items)
    ]
    for number in range(slots):
        loads[number].start()
    for load, store in zip(small_loads, small_stores, strict=True):
        load.wait()
        store.start()
    for number in range(len(items)):
        loads[number].wait()
        if number >= slots:
            stores[number - slots].wait()
        written[number % slots] = read[number % slots].astype(WIDE)
        stores[number].start()
        if number + slots < len(items):
            loads[number + slots].start()
    for store in stores[-slots:]:
        store.wait()
    for store in small_stores:
        store.wait()


def run_emit(lates, earlies, small, width, fan):
    shape = jax.ShapeDtypeStruct
    count = len(small)
    slots = 24

    def kernel(*refs):
        names = Names(refs)
        late_refs, early_refs, small_refs = names.share([lates, earlies, small])
        small_out, out_refs = (names.take(count), names.take(4))
        emit_kernel(late_refs, early_refs, small_refs, out_refs, small_out, *names.refs)

    return pl.pallas_call(
        kernel,
        out_shape=[shape(item.shape, item.dtype) for item in small]
        + [
            shape((2, width, 3 * width), WIDE),
            shape((2, width, width), WIDE),
            shape((2, width, fan), WIDE),
            shape((2, fan, width), WIDE),
        ],
        in_specs=[apart] * (4 + count),
        out_specs=[apart] * (4 + count),
        scratch_shapes=[
            pltpu.VMEM((slots, width, width), LOW),
            pltpu.VMEM((slots, width, width), WIDE),
            pltpu.SemaphoreType.DMA((3, max(slots, count))),
        ]
        + [pltpu.VMEM(item.shape, item.dtype) for item in small],
        compiler_params=settings(None),
        cost_estimate=cost(1e9),
        name="emit_part",
    )(*lates, *earlies, *small)


def local_kernels(
    tokens,
    norm_gains,
    qkv_weight,
    out_weight,
    up_weight,
    down_weight,
    gen_cotangent,
    disc_cotangent,
    seg_lengths,
):
    size = lax.axis_size("seq")
    swap = (0, 2, 1, 3)
    pairs = [
        (batch * size + seq, swap[seq // 2] * size + 2 * swap[batch] + seq % 2)
        for batch in range(lax.axis_size("batch"))
        for seq in range(size)
    ]
    lengths = lax.ppermute(seg_lengths, ("batch", "seq"), pairs)
    *outs, gen_late, disc_late, gen_early, disc_early, gain_sums = run_blocks(
        lengths,
        norm_gains,
        tokens[0],
        gen_cotangent[0],
        disc_cotangent[0],
        (qkv_weight, out_weight, up_weight, down_weight),
    )
    *outs, gain_sums, qkv_grad, out_grad, up_grad, down_grad = run_emit(
        (gen_late, disc_late),
        (gen_early, disc_early),
        (*outs, gain_sums),
        up_weight.shape[1],
        up_weight.shape[2],
    )
    return (
        *(out[None] for out in outs),
        gain_sums[:4].reshape(2, 2, -1),
        qkv_grad,
        out_grad,
        up_grad,
        down_grad,
    )


def solution(mesh):
    placed = (
        P("batch", "seq", None),
        P(),
        P(),
        P(),
        P(),
        P(),
        P("batch", "seq", None),
        P("batch", "seq", None),
        P("batch", None),
    )
    planes = dict(mesh.shape) == {"batch": 4, "seq": 8}
    return jax.shard_map(
        local_kernels if planes else local_scan,
        mesh=mesh,
        in_specs=placed,
        out_specs=(
            P("batch", "seq", None),
            P("batch", "seq", None),
            P("batch", "seq", None),
            P("batch", "seq", None),
            P(),
            P(),
            P(),
            P(),
            P(),
        ),
        check_vma=False,
    )
```

```python
import functools
import math

import jax
import jax.numpy as jnp
from jax import lax
from jax.experimental import pallas as pl
from jax.experimental.pallas import tpu as pltpu
from jax.sharding import PartitionSpec as P

HEADS = 8


epsilon = 1e-05
masked_score = -1e30
key_block = 2048


def layer_norm(inputs, gain_row):
    average = jnp.mean(inputs, axis=-1, keepdims=True)
    centred = inputs - average
    variance = jnp.mean(centred * centred, axis=-1, keepdims=True)
    return centred * lax.rsqrt(variance + epsilon) * gain_row


def gelu_tanh(inputs):
    return (
        0.5
        * inputs
        * (1.0 + jnp.tanh(0.7978845608028654 * (inputs + 0.044715 * inputs * inputs * inputs)))
    )


def segment_of(lengths, positions):
    first = lengths[0]
    second = first + lengths[1]
    third = second + lengths[2]
    return (
        (positions >= first).astype(jnp.int32)
        + (positions >= second).astype(jnp.int32)
        + (positions >= third).astype(jnp.int32)
    )


def block_scores(query_heads, key_heads, query_segment, key_segment, scale):
    scores = (
        jnp.einsum("qhe,khe->hqk", query_heads, key_heads, preferred_element_type=jnp.float32)
        * scale
    )
    allowed = query_segment[:, None] == key_segment[None, :]
    return jnp.where(allowed[None], scores, masked_score)


def split_blocks(array_rows, width):
    return array_rows.reshape((array_rows.shape[0] // width, width) + array_rows.shape[1:])


def attend(query_heads, key_heads, value_heads, query_segment, key_segment, scale):
    width = math.gcd(key_heads.shape[0], key_block)
    blocks = (
        split_blocks(key_heads, width),
        split_blocks(value_heads, width),
        split_blocks(key_segment, width),
    )
    heads = query_heads.shape[1]
    row_count = query_heads.shape[0]

    def statistics(carry, item):
        row_max, totals = carry
        scores = block_scores(query_heads, item[0], query_segment, item[2], scale)
        new_max = jnp.maximum(row_max, jnp.max(scores, axis=-1))
        totals = totals * jnp.exp(row_max - new_max) + jnp.sum(
            jnp.exp(scores - new_max[..., None]), axis=-1
        )
        return ((new_max, totals), None)

    start_max = jnp.full((heads, row_count), masked_score, jnp.float32)
    (row_max, totals), unused = lax.scan(
        statistics, (start_max, jnp.zeros((heads, row_count), jnp.float32)), blocks
    )
    log_total = row_max + jnp.log(totals)

    def weighted(running, item):
        scores = block_scores(query_heads, item[0], query_segment, item[2], scale)
        weights_low = jnp.exp(scores - log_total[..., None]).astype(jnp.bfloat16)
        return (
            running
            + jnp.einsum("hqk,khe->qhe", weights_low, item[1], preferred_element_type=jnp.float32),
            None,
        )

    attended, unused = lax.scan(weighted, jnp.zeros(query_heads.shape, jnp.float32), blocks)
    return (attended, log_total)


def query_side(
    query_heads,
    key_heads,
    value_heads,
    query_segment,
    key_segment,
    grad_heads,
    log_total,
    delta,
    scale,
):
    width = math.gcd(key_heads.shape[0], key_block)
    blocks = (
        split_blocks(key_heads, width),
        split_blocks(value_heads, width),
        split_blocks(key_segment, width),
    )

    def step(running, item):
        scores = block_scores(query_heads, item[0], query_segment, item[2], scale)
        weights = jnp.exp(scores - log_total[..., None])
        dprobs = jnp.einsum("qhe,khe->hqk", grad_heads, item[1], preferred_element_type=jnp.float32)
        dscores = (weights * (dprobs - delta[..., None])).astype(jnp.bfloat16)
        running = running + jnp.einsum(
            "hqk,khe->qhe", dscores, item[0], preferred_element_type=jnp.float32
        )
        key_part = (
            jnp.einsum("hqk,qhe->khe", dscores, query_heads, preferred_element_type=jnp.float32)
            * scale
        )
        value_part = jnp.einsum(
            "hqk,qhe->khe",
            weights.astype(jnp.bfloat16),
            grad_heads,
            preferred_element_type=jnp.float32,
        )
        return (running, (key_part, value_part))

    grad_query, key_parts = lax.scan(step, jnp.zeros(query_heads.shape, jnp.float32), blocks)
    return (grad_query * scale, key_parts)


def block_forward(inputs, gains, qkv_matrix, out_matrix, up_matrix, down_matrix, lengths):
    row_count, width = inputs.shape
    heads = HEADS
    head_size = width // heads
    scale = head_size ** (-0.5)
    band_index = lax.axis_index("seq")
    positions = band_index * row_count + jnp.arange(row_count, dtype=jnp.int32)
    query_segment = segment_of(lengths, positions)
    key_segment = segment_of(lengths, jnp.arange(row_count * lax.axis_size("seq"), dtype=jnp.int32))
    keep_rows = (query_segment < 3).astype(jnp.float32)[:, None]
    normed = layer_norm(inputs, gains[0]).astype(jnp.bfloat16)
    qkv_rows = jnp.dot(normed, qkv_matrix, preferred_element_type=jnp.float32).astype(jnp.bfloat16)
    all_keys, all_values = (
        lax.all_gather(qkv_rows[:, width : 2 * width], "seq", axis=0, tiled=True),
        lax.all_gather(qkv_rows[:, 2 * width :], "seq", axis=0, tiled=True),
    )
    attended, log_total = attend(
        qkv_rows[:, :width].reshape(row_count, heads, head_size),
        all_keys.reshape(-1, heads, head_size),
        all_values.reshape(-1, heads, head_size),
        query_segment,
        key_segment,
        scale,
    )
    attended = attended.reshape(row_count, width)
    attended_low = (attended * keep_rows).astype(jnp.bfloat16)
    middle = inputs + jnp.dot(attended_low, out_matrix, preferred_element_type=jnp.float32)
    second_norm = layer_norm(middle, gains[1]).astype(jnp.bfloat16)
    up_rows = jnp.dot(second_norm, up_matrix, preferred_element_type=jnp.float32)
    hidden = gelu_tanh(up_rows).astype(jnp.bfloat16)
    outputs = middle + jnp.dot(hidden, down_matrix, preferred_element_type=jnp.float32)
    kept = (
        inputs,
        normed,
        qkv_rows,
        None,
        attended,
        log_total,
        attended_low,
        middle,
        second_norm,
        up_rows,
        hidden,
        query_segment,
        key_segment,
        keep_rows,
        lengths,
    )
    return (outputs, kept)


def block_backward(kept, grad_out, gains, qkv_matrix, out_matrix, up_matrix, down_matrix):
    (
        inputs,
        normed,
        qkv_rows,
        gathered,
        attended,
        log_total,
        attended_low,
        middle,
        second_norm,
        up_rows,
        hidden,
        query_segment,
        key_segment,
        keep_rows,
        lengths,
    ) = kept
    row_count, width = inputs.shape
    heads = HEADS
    head_size = width // heads
    scale = head_size ** (-0.5)
    grad_down = jnp.einsum("tf,td->fd", hidden, grad_out, preferred_element_type=jnp.float32)
    grad_hidden = jnp.einsum("td,fd->tf", grad_out, down_matrix, preferred_element_type=jnp.float32)
    unused, gelu_back = jax.vjp(gelu_tanh, up_rows)
    grad_up_rows = gelu_back(grad_hidden)[0].astype(jnp.bfloat16)
    grad_up = jnp.einsum("td,tf->df", second_norm, grad_up_rows, preferred_element_type=jnp.float32)
    grad_second = jnp.einsum(
        "tf,df->td", grad_up_rows, up_matrix, preferred_element_type=jnp.float32
    )
    unused, second_back = jax.vjp(layer_norm, middle, gains[1])
    middle_part, gain_second = second_back(grad_second)
    grad_middle = grad_out.astype(jnp.float32) + middle_part
    grad_branch = grad_middle.astype(jnp.bfloat16)
    grad_outw = jnp.einsum(
        "td,te->de", attended_low, grad_branch, preferred_element_type=jnp.float32
    )
    grad_attended = jnp.einsum(
        "te,de->td", grad_branch, out_matrix, preferred_element_type=jnp.float32
    ).astype(jnp.bfloat16) * keep_rows.astype(jnp.bfloat16)
    grad_heads = grad_attended.reshape(row_count, heads, head_size)
    delta = jnp.sum(
        grad_heads.astype(jnp.float32) * attended.reshape(row_count, heads, head_size), axis=-1
    ).T
    query_heads = qkv_rows[:, :width].reshape(row_count, heads, head_size)
    all_keys, all_values = (
        lax.all_gather(qkv_rows[:, width : 2 * width], "seq", axis=0, tiled=True),
        lax.all_gather(qkv_rows[:, 2 * width :], "seq", axis=0, tiled=True),
    )
    key_heads = all_keys.reshape(-1, heads, head_size)
    value_heads = all_values.reshape(-1, heads, head_size)
    grad_query, key_parts = query_side(
        query_heads,
        key_heads,
        value_heads,
        query_segment,
        key_segment,
        grad_heads,
        log_total,
        delta,
        scale,
    )
    grad_keys, grad_values = (
        lax.psum_scatter(
            key_parts[0].reshape(-1, width).astype(jnp.bfloat16),
            "seq",
            scatter_dimension=0,
            tiled=True,
        ).astype(jnp.float32),
        lax.psum_scatter(
            key_parts[1].reshape(-1, width).astype(jnp.bfloat16),
            "seq",
            scatter_dimension=0,
            tiled=True,
        ).astype(jnp.float32),
    )
    grad_qkv_rows = jnp.concatenate(
        [grad_query.reshape(row_count, width), grad_keys, grad_values], axis=1
    ).astype(jnp.bfloat16)
    grad_qkv = jnp.einsum("td,tf->df", normed, grad_qkv_rows, preferred_element_type=jnp.float32)
    grad_first = jnp.einsum(
        "tf,df->td", grad_qkv_rows, qkv_matrix, preferred_element_type=jnp.float32
    )
    unused, first_back = jax.vjp(layer_norm, inputs, gains[0])
    input_part, gain_first = first_back(grad_first)
    grad_inputs = grad_middle + input_part
    return (
        grad_inputs,
        (jnp.stack([gain_first, gain_second]), grad_qkv, grad_outw, grad_up, grad_down),
    )


def local_scan(
    tokens,
    norm_gains,
    qkv_weight,
    out_weight,
    up_weight,
    down_weight,
    gen_cotangent,
    disc_cotangent,
    seg_lengths,
):
    gen_weights = (norm_gains[0], qkv_weight[0], out_weight[0], up_weight[0], down_weight[0])
    disc_weights = (norm_gains[1], qkv_weight[1], out_weight[1], up_weight[1], down_weight[1])
    gen_outs, disc_outs, gen_ins, disc_ins = ([], [], [], [])
    number = 0
    lengths = seg_lengths[number]
    gen_rows, gen_kept = block_forward(tokens[number].astype(jnp.float32), *gen_weights, lengths)
    gen_low = gen_rows.astype(jnp.bfloat16)
    disc_rows, disc_kept = block_forward(gen_low.astype(jnp.float32), *disc_weights, lengths)
    disc_grad_in, disc_terms = block_backward(disc_kept, disc_cotangent[number], *disc_weights)
    gen_grad_in, gen_terms = block_backward(gen_kept, gen_cotangent[number], *gen_weights)
    gen_outs.append(gen_low)
    disc_outs.append(disc_rows.astype(jnp.bfloat16))
    gen_ins.append(gen_grad_in.astype(jnp.bfloat16))
    disc_ins.append(disc_grad_in.astype(jnp.bfloat16))
    stacked = [jnp.stack([gen_terms[number], disc_terms[number]]) for number in range(5)]
    summed = lax.psum(
        (stacked[0], stacked[1], stacked[2], stacked[3], stacked[4]), ("batch", "seq")
    )
    return (
        jnp.stack(gen_outs),
        jnp.stack(disc_outs),
        jnp.stack(gen_ins),
        jnp.stack(disc_ins),
        summed[0],
        summed[1],
        summed[2],
        summed[3],
        summed[4],
    )


NN = (((1,), (0,)), ((), ()))
NT = (((1,), (1,)), ((), ()))
TN = (((0,), (0,)), ((), ()))
LOW = jnp.bfloat16
WIDE = jnp.float32
GROUP = 4
vmem_bytes = 63 << 20


def product(left, right, form):
    return lax.dot_general(left, right, form, preferred_element_type=WIDE)


def normalise(inputs):
    average = jnp.mean(inputs, axis=-1, keepdims=True)
    centred = inputs - average
    variance = jnp.mean(centred * centred, axis=-1, keepdims=True)
    inverse = lax.rsqrt(variance + epsilon)
    return (centred * inverse, inverse)


def normalise_back(hat, inverse, gain_row, grad):
    scaled = grad * gain_row
    first = jnp.mean(scaled, axis=-1, keepdims=True)
    second = jnp.mean(scaled * hat, axis=-1, keepdims=True)
    return inverse * (scaled - first - hat * second)


def segments(lengths, positions):
    first = lengths[0, 0]
    second = first + lengths[0, 1]
    third = second + lengths[0, 2]
    return (
        (positions >= first).astype(jnp.int32)
        + (positions >= second).astype(jnp.int32)
        + (positions >= third).astype(jnp.int32)
    )


def stacked_positions(band, rows):
    lanes = lax.broadcasted_iota(jnp.int32, (1, GROUP * rows), 1)
    for unused in range(1, GROUP):
        lanes = lanes - jnp.where(lanes >= rows, rows, 0)
    return lanes + band * rows


def head_lanes(rows, head_size):
    return lax.broadcasted_iota(jnp.int32, (rows, GROUP * head_size), 1) // head_size


def stack_heads(rows_group, lane_head):
    zero = jnp.zeros_like(rows_group)
    return jnp.concatenate(
        [jnp.where(lane_head == head, rows_group, zero) for head in range(GROUP)], axis=0
    )


def unstack_heads(stacked, lane_head, rows):
    total = jnp.where(lane_head == 0, stacked[:rows], 0.0)
    for head in range(1, GROUP):
        total = jnp.where(lane_head == head, stacked[head * rows : (head + 1) * rows], total)
    return total


def key_chunks(bands, rows):
    step = 2 if (bands - 2) % 2 == 0 else 1
    chunks = [(0, rows)]
    for at in range(1, bands - 1, step):
        chunks.append((at * rows, step * rows))
    chunks.append(((bands - 1) * rows, rows))
    return chunks


class Moves:
    def __init__(self, sems):
        self.sems = sems
        self.pending = {}
        self.count = 0

    def start(self, key, source, target):
        copy = pltpu.make_async_copy(source, target, self.sems.at[self.count])
        copy.start()
        self.count += 1
        self.pending[key] = copy

    def wait(self, key):
        self.pending.pop(key).wait()


GRID = pl.DeviceIdType.MESH
CORE, EDGE_X, EDGE_Y, NEAR_Z, FAR_Z = (
    ("batch", 0),
    ("batch", 1),
    ("seq", 0),
    ("seq", 1),
    ("seq", 2),
)
ORDERS = (
    (CORE, EDGE_X, EDGE_Y, NEAR_Z, FAR_Z),
    (CORE, EDGE_Y, NEAR_Z, EDGE_X, FAR_Z),
    (CORE, NEAR_Z, EDGE_X, EDGE_Y, FAR_Z),
)
STEPS = 5
DEVICES = 1 << STEPS


def place():
    return (lax.axis_index("batch"), lax.axis_index("seq"))


def swapped(number):
    return 2 * lax.rem(number, 2) + number // 2


def band_here():
    batch, seq = place()
    return 2 * swapped(batch) + lax.rem(seq, 2)


def home():
    batch, seq = place()
    return (swapped(seq // 2), 2 * swapped(batch) + lax.rem(seq, 2))


def bit_of(axis, number):
    return lax.rem(lax.axis_index(axis) // (1 << number), 2)


def across(axis, number):
    batch, seq = place()
    step = (1 - 2 * bit_of(axis, number)) * (1 << number)
    return (batch + step, seq) if axis == "batch" else (batch, seq + step)


def announce(partners):
    for partner in partners:
        pl.semaphore_signal(
            pltpu.get_barrier_semaphore(), inc=1, device_id=partner, device_id_type=GRID
        )


def meet(count):
    pl.semaphore_wait(pltpu.get_barrier_semaphore(), count)


def aligned(at, size):
    return pl.ds(pl.multiple_of(at, 16), size)


class Copies:
    def __init__(self, sems):
        self.sems = sems
        self.known = {}
        self.count = 0

    def send(self, key, source, target, partner):
        number = self.count
        self.count += 1
        copy = pltpu.make_async_remote_copy(
            src_ref=source,
            dst_ref=target,
            send_sem=self.sems.at[0, number],
            recv_sem=self.sems.at[1, number],
            device_id=partner,
            device_id_type=GRID,
        )
        copy.start()
        self.known[key] = copy

    def arrive(self, key):
        self.known[key].wait_recv()

    def sent(self, keys):
        for key in keys:
            self.known.pop(key).wait_send()

    def close(self):
        for copy in self.known.values():
            copy.wait_send()


class Layout:
    def __init__(self, sizes):
        self.sizes = sizes
        self.starts = [sum(sizes[:number]) for number in range(len(sizes))]

    def base(self, number, step):
        at, size = (self.starts[number] // 2, self.sizes[number] // 2)
        for axis in ORDERS[number][1:step]:
            size = size // 2
            at = at + bit_of(*axis) * size
        return (at, size)

    def whole_base(self, number, step):
        at, size = self.base(number, step)
        start, half = self.starts[number], self.sizes[number] // 2
        return (at - start // 2 + start + bit_of(*CORE) * half, size)

    def part(self, number):
        return pl.ds(self.starts[number] // DEVICES, self.sizes[number] // DEVICES)


class Reduction:
    def __init__(self, sizes, source, part, held, landing, local_sems, sems, apart_first=False):
        self.layout = Layout(sizes)
        self.sizes = sizes
        self.source, self.part, self.held, self.landing = (source, part, held, landing)
        self.copies = Copies(sems)
        self.moves = Moves(local_sems)
        self.apart_first = apart_first

    def pieces(self, number, part):
        next_bit = bit_of(*ORDERS[number][1])
        piece = (1 - next_bit) if part == 0 else next_bit
        return (piece, self.sizes[number] // 4)

    def begin(self):
        for part in range(2):
            for number, size in enumerate(self.sizes):
                piece, quarter = self.pieces(number, part)
                at = self.layout.starts[number] + (1 - bit_of(*CORE)) * (size // 2)
                landing = self.layout.starts[number] // 2 + part * quarter
                self.copies.send(
                    (number, part),
                    self.source.at[aligned(at + piece * quarter, quarter)],
                    self.landing.at[pl.ds(landing, quarter)],
                    across(*CORE),
                )
        for number, size in enumerate(self.sizes):
            start = self.layout.starts[number]
            self.moves.start(
                number,
                self.source.at[aligned(start + bit_of(*CORE) * (size // 2), size // 2)],
                self.held.at[pl.ds(start // 2, size // 2)],
            )

    def first(self, number, part):
        piece, quarter = self.pieces(number, part)
        if part == 0:
            self.moves.wait(number)
        self.copies.arrive((number, part))
        start = self.layout.starts[number] // 2
        here = aligned(start + piece * quarter, quarter)
        self.held[here, :] = (
            self.held[here, :].astype(WIDE)
            + self.landing[pl.ds(start + part * quarter, quarter), :].astype(WIDE)
        ).astype(LOW)
        if part == 0:
            self.send(number, 1)

    def release(self):
        self.copies.sent([(number, part) for number in range(len(self.sizes)) for part in range(2)])

    def landed(self, number, step):
        start = sum(self.sizes) // 2
        for earlier in range(1, STEPS if self.apart_first and step == 1 else step):
            start += sum(self.sizes) >> (earlier + 1)
        return pl.ds(start + (self.layout.starts[number] >> (step + 1)), self.sizes[number] >> (step + 1))

    def send(self, number, step):
        axis = ORDERS[number][step]
        at, size = self.layout.base(number, step)
        size = size // 2
        self.copies.send(
            (number, "at", step),
            self.held.at[aligned(at + (1 - bit_of(*axis)) * size, size)],
            self.landing.at[self.landed(number, step)],
            across(*axis),
        )

    def add(self, number, step):
        at, size = self.layout.base(number, step + 1)
        self.copies.arrive((number, "at", step))
        summed = (
            self.held[aligned(at, size), :].astype(WIDE)
            + self.landing[self.landed(number, step), :].astype(WIDE)
        ).astype(LOW)
        if step + 1 < STEPS:
            self.held[aligned(at, size), :] = summed
            self.send(number, step + 1)
        else:
            self.part[self.layout.part(number), :] = summed
            if number == len(self.sizes) - 1:
                self.copies.close()

    def tasks(self):
        numbers = range(len(self.sizes))
        steps = [self.begin]
        steps += [functools.partial(self.first, number, part) for part in range(2) for number in numbers]
        steps += [
            functools.partial(self.add, number, step) for step in range(1, STEPS) for number in numbers
        ]
        return steps

    @staticmethod
    def scratch(sizes, apart_first):
        rows = sum(sizes)
        landing = sum(rows >> step for step in range(1, STEPS + 1))
        if apart_first:
            landing += rows >> 2
        return [
            pltpu.VMEM((rows // 2, 512), LOW),
            pltpu.VMEM((landing, 512), LOW),
            pltpu.SemaphoreType.DMA((len(sizes),)),
            pltpu.SemaphoreType.DMA((2, 6 * len(sizes))),
        ]


class Sharing:
    def __init__(self, sizes, part, total, local_sems, sems):
        self.layout = Layout(sizes)
        self.sizes = sizes
        self.part, self.total, self.local = (part, total, local_sems)
        self.met = False
        self.copies = Copies(sems)

    def rows(self, number, step):
        return aligned(*self.layout.whole_base(number, step))

    def stay(self, number):
        return pltpu.make_async_copy(
            self.part.at[self.layout.part(number)],
            self.total.at[self.rows(number, STEPS)],
            self.local.at[number],
        )

    def begin(self):
        for number in range(len(self.sizes)):
            self.stay(number).start()
        for number in range(len(self.sizes)):
            self.stay(number).wait()
            self.share(number, STEPS - 1)
            self.pass_on(number, STEPS)

    def share(self, number, step):
        rows = self.rows(number, step + 1)
        self.copies.send(
            (number, step),
            self.total.at[rows],
            self.total.at[rows],
            across(*ORDERS[number][step]),
        )

    def pass_on(self, number, step):
        if step == STEPS:
            rows = self.rows(number, STEPS)
        else:
            at, size = self.layout.whole_base(number, step)
            size = size // 2
            rows = aligned(at + (1 - bit_of(*ORDERS[number][step])) * size, size)
        self.copies.send(
            (number, "pass", step), self.total.at[rows], self.total.at[rows], across(*CORE)
        )

    def gather(self, number, step):
        self.copies.arrive((number, step))
        if step > 1:
            self.share(number, step - 1)
        self.pass_on(number, step)

    def core_began(self):
        if not self.met:
            self.met = True
            for number in range(len(self.sizes)):
                self.copies.arrive((number, "pass", STEPS))

    def end(self):
        self.core_began()
        for step in range(STEPS - 1, 0, -1):
            for number in range(len(self.sizes)):
                self.copies.arrive((number, "pass", step))
        self.copies.close()

    def tasks(self):
        steps = [self.begin]
        steps += [
            functools.partial(self.gather, number, step)
            for step in range(STEPS - 1, 0, -1)
            for number in range(len(self.sizes))
        ]
        return steps + [self.end]

    @staticmethod
    def scratch(sizes):
        return [
            pltpu.SemaphoreType.DMA((len(sizes),)),
            pltpu.SemaphoreType.DMA((2, 9 * len(sizes))),
        ]


class SmallSum:
    def __init__(self, total, landing, sems):
        self.total, self.landing = (total, landing)
        self.copies = Copies(sems)

    def send(self, step):
        self.copies.send(
            step, self.landing.at[STEPS + step], self.landing.at[step], across(*ORDERS[0][step])
        )

    def add(self, step):
        self.copies.arrive(step)
        summed = self.landing[STEPS + step] + self.landing[step]
        if step + 1 < STEPS:
            self.landing[STEPS + step + 1] = summed
            self.send(step + 1)
        else:
            self.total[...] = summed
            self.copies.close()

    def tasks(self):
        return [functools.partial(self.send, 0)] + [
            functools.partial(self.add, step) for step in range(STEPS)
        ]

    @staticmethod
    def scratch():
        return [
            pltpu.VMEM((2 * STEPS, 8, 512), WIDE),
            pltpu.SemaphoreType.DMA((2, STEPS)),
        ]


class Gathering:
    def __init__(self, whole_ref, rows, sems):
        self.whole, self.rows = (whole_ref, rows)
        self.copies = Copies(sems)
        self.band = band_here()
        self.x = self.band + 2 * (1 - 2 * bit_of(*EDGE_X))
        self.y = self.band + 1 - 2 * bit_of(*EDGE_Y)
        self.corner = self.x + self.y - self.band

    def send(self, key, band, axis, half=None):
        start, size = (band * self.rows, self.rows)
        if half is not None:
            size = size // 2
            start = start + half * size
        ref = self.whole.at[aligned(start, size)]
        self.copies.send(key, ref, ref, across(*axis))

    def begin(self):
        self.send("x", self.band, EDGE_X)
        self.send("y", self.band, EDGE_Y)
        self.send("core", self.band, CORE)

    def from_x(self):
        self.copies.arrive("x")
        self.send("corner 0", self.x, EDGE_Y, 0)
        self.send("core x", self.x, CORE)

    def from_y(self):
        self.copies.arrive("y")
        self.send("corner 1", self.y, EDGE_X, 1)
        self.send("core y", self.y, CORE)

    def from_corner(self, half):
        self.copies.arrive("corner %d" % half)
        self.send("core corner %d" % half, self.corner, CORE, half)

    def end(self):
        for key in ("core", "core x", "core y", "core corner 0", "core corner 1"):
            self.copies.arrive(key)
        self.copies.close()

    def tasks(self):
        corners = [functools.partial(self.from_corner, half) for half in range(2)]
        return [self.begin, self.from_x, self.from_y, *corners, self.end]

    @staticmethod
    def scratch():
        return [pltpu.SemaphoreType.DMA((2, 9))]


class Scattering:
    def __init__(self, source, held, landing, local_sems, sems, rows, finish):
        self.source, self.held, self.landing, self.rows, self.finish = (
            source,
            held,
            landing,
            rows,
            finish,
        )
        self.copies = Copies(sems)
        self.moves = Moves(local_sems)
        half = source.shape[1] // 2
        self.lanes = (slice(0, half), slice(half, 2 * half))

    def begin(self):
        size = 4 * self.rows
        self.copies.send(
            "core",
            self.source.at[aligned((1 - bit_of(*CORE)) * size, size)],
            self.landing.at[pl.ds(0, size)],
            across(*CORE),
        )
        self.moves.start("core", self.source.at[aligned(bit_of(*CORE) * size, size)], self.held)

    def first(self):
        rows = self.rows
        self.moves.wait("core")
        self.copies.arrive("core")
        self.held[...] = (
            self.held[...].astype(WIDE) + self.landing[pl.ds(0, 4 * rows), :].astype(WIDE)
        ).astype(LOW)
        x, y = (bit_of(*EDGE_X), bit_of(*EDGE_Y))
        self.copies.send(
            "x",
            self.held.at[aligned(2 * (1 - x) * rows, 2 * rows), self.lanes[0]],
            self.landing.at[pl.ds(4 * rows, 2 * rows), self.lanes[0]],
            across(*EDGE_X),
        )
        for other in range(2):
            self.copies.send(
                ("y", other),
                self.held.at[aligned((2 * other + 1 - y) * rows, rows), self.lanes[1]],
                self.landing.at[pl.ds((4 + other) * rows, rows), self.lanes[1]],
                across(*EDGE_Y),
            )

    def second(self):
        rows = self.rows
        x, y = (bit_of(*EDGE_X), bit_of(*EDGE_Y))
        self.copies.arrive("x")
        here = aligned(2 * x * rows, 2 * rows)
        self.held[here, self.lanes[0]] = (
            self.held[here, self.lanes[0]].astype(WIDE)
            + self.landing[pl.ds(4 * rows, 2 * rows), self.lanes[0]].astype(WIDE)
        ).astype(LOW)
        self.copies.send(
            "then y",
            self.held.at[aligned((2 * x + 1 - y) * rows, rows), self.lanes[0]],
            self.landing.at[pl.ds(6 * rows, rows), self.lanes[0]],
            across(*EDGE_Y),
        )
        for other in range(2):
            self.copies.arrive(("y", other))
            here = aligned((2 * other + y) * rows, rows)
            self.held[here, self.lanes[1]] = (
                self.held[here, self.lanes[1]].astype(WIDE)
                + self.landing[pl.ds((4 + other) * rows, rows), self.lanes[1]].astype(WIDE)
            ).astype(LOW)
        self.copies.send(
            "then x",
            self.held.at[aligned((2 * (1 - x) + y) * rows, rows), self.lanes[1]],
            self.landing.at[pl.ds(6 * rows, rows), self.lanes[1]],
            across(*EDGE_X),
        )

    def third(self):
        rows = self.rows
        self.copies.arrive("then y")
        self.copies.arrive("then x")
        here = aligned((2 * bit_of(*EDGE_X) + bit_of(*EDGE_Y)) * rows, rows)
        self.finish(
            self.held[here, :].astype(WIDE) + self.landing[pl.ds(6 * rows, rows), :].astype(WIDE)
        )
        self.copies.close()

    def tasks(self):
        return [self.begin, self.first, self.second, self.third]

    @staticmethod
    def scratch(rows):
        return [
            pltpu.VMEM((4 * rows, 512), LOW),
            pltpu.VMEM((7 * rows, 512), LOW),
            pltpu.SemaphoreType.DMA((2,)),
            pltpu.SemaphoreType.DMA((2, 7)),
        ]


class Homing:
    def __init__(self, source, target, sems):
        batch, seq = place()
        partner = home()
        self.here = (partner[0] == batch) & (partner[1] == seq)
        self.stay = pltpu.make_async_copy(source, target, sems.at[0])
        self.go = pltpu.make_async_remote_copy(
            src_ref=source,
            dst_ref=target,
            send_sem=sems.at[0],
            recv_sem=sems.at[1],
            device_id=partner,
            device_id_type=GRID,
        )

    def start(self):
        @pl.when(self.here)
        def _():
            self.stay.start()

        @pl.when(jnp.logical_not(self.here))
        def _():
            self.go.start()

    def wait(self):
        @pl.when(self.here)
        def _():
            self.stay.wait()

        @pl.when(jnp.logical_not(self.here))
        def _():
            self.go.wait()

    def tasks(self):
        return [self.start, self.wait]


def announce_home():
    batch, seq = place()
    partner = home()

    @pl.when((partner[0] != batch) | (partner[1] != seq))
    def _():
        announce([partner])


def meet_with_home(count):
    batch, seq = place()
    partner = home()
    here = (partner[0] == batch) & (partner[1] == seq)

    @pl.when(jnp.logical_not(here))
    def _():
        meet(count + 1)

    if count:

        @pl.when(here)
        def _():
            meet(count)


HOMING = [pltpu.SemaphoreType.DMA((2,))]


whole = pl.BlockSpec(memory_space=pltpu.VMEM)
scalars = pl.BlockSpec(memory_space=pltpu.SMEM)
apart = pl.BlockSpec(memory_space=pl.ANY)

def settings(number, limit=vmem_bytes):
    if number is None:
        return pltpu.CompilerParams(vmem_limit_bytes=limit)
    return pltpu.CompilerParams(
        vmem_limit_bytes=limit, collective_id=number, has_side_effects=True
    )


def cost(flops):
    return pl.CostEstimate(flops=int(flops), bytes_accessed=40 << 20, transcendentals=0)


class Names:
    def __init__(self, refs):
        self.refs = list(refs)

    def take(self, count):
        taken, self.refs = (self.refs[:count], self.refs[count:])
        return taken

    def share(self, lists):
        return [self.take(len(item)) for item in lists]


def flat(lists):
    return [item for items in lists for item in items]


GATHER_DUE = (
    (8.99000, 8.99002, 8.99004, 8.99006, 8.99008, 8.99010),
    (48.99020, 59.89032, 59.89034, 73.89050, 75.89052, 79.99056),
)
SCATTER_DUE = (
    (82.99076, 86.09084, 95.49106, 101.49118),
    (138.99196, 138.99406, 139.00138, 139.00552),
)
EARLY_REDUCE_DUE = (
    (54.49024, 57.89026, 57.89028, 57.89030, 59.89036, 59.89038, 59.89040, 71.89048, 69.89044, 69.89046, 79.99060, 76.49054, 79.99062, 86.09080, 82.99078, 86.09082, 92.79176, 90.64132, 92.79178),
    (110.49140, 113.89148, 113.89150, 113.89152, 113.89154, 113.89156, 115.89162, 129.89180, 125.89174, 129.89178, 138.99192, 138.99200, 138.99194, 138.99814, 138.99712, 138.99610, 139.00240, 139.00136, 139.00022),
)
EARLY_SHARE_DUE = (
    (92.79180, 99.79194, 101.49116, 101.49122, 104.99130, 106.99136, 106.99138, 111.99144, 121.89168, 115.89164, 123.89172, 132.49186, 135.99188, 138.99198),
    (139.00242, 139.00450, 139.00562, 139.00664, 139.00766, 139.01076, 139.00974, 139.01178, 139.01592, 139.01490, 139.01900, 139.02208, 139.02104, 139.02414),
)
LATE_REDUCE_DUE = (
    (79.99058, 82.99064, 82.99066, 82.99068, 82.99070, 82.99072, 82.99074, 88.49086, 88.49088, 88.49090, 95.49102, 92.79174, 95.49104, 99.79190, 97.64148, 99.79192, 103.49124, 103.49126, 104.99128),
    (138.99920, 139.00124, 139.00126, 139.00128, 139.00130, 139.00132, 139.00134, 139.00344, 139.00346, 139.00348, 139.00554, 139.00556, 139.00558, 139.00868, 139.00870, 139.00872, 139.01280, 139.01382, 139.01384),
)
LATE_SHARE_DUE = (
    (104.99132, 111.99146, 113.89158, 113.89160, 121.89170, 131.89182, 125.89176, 135.99190, 138.99302, 131.89184, 138.99404, 138.99816, 138.99508, 138.99918),
    (139.01386, 139.01694, 139.01796, 139.01798, 139.02206, 139.02002, 139.02310, 139.02516, 139.02312, 139.02618, 139.02822, 139.02720, 139.02924, 139.03026),
)
HOME_DUE = (
    (48.99022, 65.89042),
    (104.99134, 119.89166),
    (101.49120, 111.99142),
    (139.00560, 139.01388),
)


QUERY_LANES = 512


class Schedule:
    def __init__(self):
        self.waiting = []
        self.now = 0.0
        self.base = 0.0

    def add(self, due, tasks):
        self.waiting += zip(due, tasks, strict=True)
        self.waiting.sort(key=lambda task: task[0])

    def stage(self, base):
        self.base = base
        self.tick(0.0)

    def tick(self, now):
        self.now = self.base + now
        while self.waiting and self.waiting[0][0] <= self.now:
            self.waiting.pop(0)[1]()

    def require(self, last):
        while any(task == last for unused, task in self.waiting):
            self.waiting.pop(0)[1]()

    def drain(self):
        while self.waiting:
            self.waiting.pop(0)[1]()


def load_early(moves, block, hbm, target):
    unused, out_hbm, up_hbm, down_hbm = hbm
    width = target.shape[1]
    fan = up_hbm.shape[2]
    for number in range(fan // width):
        moves.start(
            ("up", block, number),
            up_hbm.at[block, :, pl.ds(number * width, width)],
            target.at[pl.ds(number * width, width)],
        )
    moves.start(("down", block), down_hbm.at[block], target.at[pl.ds(fan, fan)])
    moves.start(("out", block), out_hbm.at[block], target.at[pl.ds(2 * fan, width)])


def load_late(moves, block, hbm, target):
    width = target.shape[2]
    for number in range(3):
        moves.start(
            ("qkv", block, number),
            hbm[0].at[block, :, pl.ds(number * width, width)],
            target.at[block, pl.ds(number * width, width)],
        )


def forward_pass(block, schedule, moves, lengths, gains_ref, spill, r):
    tick = schedule.tick
    rows, width = r.moved.shape
    total = r.kv.shape[0]
    fan = r.hidden.shape[1]
    head_size = width // HEADS
    group_width = GROUP * head_size
    groups = width // group_width
    stacked = GROUP * rows
    band = band_here()
    lane_head = head_lanes(rows, head_size)
    chunks = key_chunks(total // rows, rows)
    image_query = segments(lengths, stacked_positions(band, rows))
    is_image = image_query == 1
    inputs_ref = r.moved if block == 0 else r.outputs.at[0]
    normed_all = r.normed.at[block]
    matrices = r.late_matrices.at[block]
    for number in range(3):
        moves.wait(("qkv", block, number))
    own = normed_all[aligned(band * rows, rows), :]
    query = product(own, matrices[:width], NN).astype(LOW)
    query = query * jnp.asarray(head_size ** (-0.5), LOW)
    for group in range(groups):
        lanes = slice(group * group_width, (group + 1) * group_width)
        r.query_stack[group] = stack_heads(query[:, lanes], lane_head)
    tick(1.0)
    for number, (start, size) in enumerate(chunks):
        at = slice(start, start + size)
        rows_here = normed_all[at]
        for part in range(2):
            r.kv[at, part * width : (part + 1) * width] = product(
                rows_here, matrices[(part + 1) * width : (part + 2) * width], NN
            ).astype(LOW)
    tick(3.1)
    for group in range(groups):
        base = 3.5 + 7.0 * group
        lanes = slice(group * group_width, (group + 1) * group_width)
        value_lanes = slice(width + group * group_width, width + (group + 1) * group_width)
        if group > 0:
            moves.wait(("spill", block, group - 1))
        attended, inverses = ([], [])
        for lane in range(0, stacked, QUERY_LANES):
            size_lanes = min(QUERY_LANES, stacked - lane)
            here = slice(lane, lane + size_lanes)
            stack = r.query_stack[group, here]
            edge_max = None
            middle_max = None
            for number, (start, size) in enumerate(chunks):
                scores = product(r.kv[start : start + size, lanes], stack, NT)
                edge = number in (0, len(chunks) - 1)
                if edge:
                    positions = start + lax.broadcasted_iota(jnp.int32, (size, 1), 0)
                    allowed = segments(lengths, positions) == image_query[:, here]
                    scores = jnp.where(allowed, scores, masked_score)
                r.scores[start : start + size, :size_lanes] = scores
                top = jnp.max(scores, axis=0, keepdims=True)
                if edge:
                    edge_max = top if edge_max is None else jnp.maximum(edge_max, top)
                else:
                    middle_max = top if middle_max is None else jnp.maximum(middle_max, top)
            image = is_image[:, here]
            row_max = jnp.maximum(edge_max, jnp.where(image, middle_max, masked_score))
            inner_max = jnp.where(image, row_max, -masked_score)
            totals = None
            gathered = None
            for number, (start, size) in enumerate(chunks):
                edge = number in (0, len(chunks) - 1)
                weights = jnp.exp(
                    r.scores[start : start + size, :size_lanes] - (row_max if edge else inner_max)
                )
                part = jnp.sum(weights, axis=0, keepdims=True)
                totals = part if totals is None else totals + part
                low = weights.astype(LOW)
                r.weights[start : start + size, here] = low
                piece = product(low, r.kv[start : start + size, value_lanes], TN)
                gathered = piece if gathered is None else gathered + piece
            attended.append(gathered)
            inverses.append(1.0 / totals)
            tick(base + lane * 0.0042 + 2.0)
        if group + 1 < groups:
            moves.start(("spill", block, group), r.weights, spill.at[group])
        columns = jnp.transpose(
            jnp.broadcast_to(jnp.concatenate(inverses, axis=1), (128, stacked))
        )
        inverse = unstack_heads(
            jnp.concatenate([columns] * (group_width // 128), axis=1), lane_head, rows
        )
        r.inverse[:, lanes] = inverse
        r.attended[:, lanes] = (
            unstack_heads(jnp.concatenate(attended, axis=0), lane_head, rows) * inverse
        )
    positions = band * rows + lax.broadcasted_iota(jnp.int32, (rows, 1), 0)
    keep_rows = (segments(lengths, positions) < 3).astype(WIDE)
    low = (r.attended[...] * keep_rows).astype(LOW)
    moves.wait(("out", block))
    middle = inputs_ref[...].astype(WIDE) + product(low, r.early_matrices[2 * fan :], NN)
    r.middle[...] = middle
    hat, unused = normalise(middle)
    second = (hat * gains_ref[block, 1:2, :]).astype(LOW)
    tick(18.5)
    for number in range(fan // width):
        moves.wait(("up", block, number))
        here = slice(number * width, (number + 1) * width)
        up_rows = product(second, r.early_matrices[here], NN)
        square = up_rows * up_rows
        bend = jnp.tanh(0.7978845608028654 * (up_rows + 0.044715 * square * up_rows))
        half = 0.5 * (1.0 + bend)
        r.hidden[:, here] = (up_rows * half).astype(LOW)
        r.slope[:, here] = (
            half
            + 0.5
            * up_rows
            * (1.0 - bend * bend)
            * (0.7978845608028654 * (1.0 + (3 * 0.044715) * square))
        ).astype(LOW)
    moves.wait(("down", block))
    tick(20.5)
    output = (middle + product(r.hidden[...], r.early_matrices[fan : 2 * fan], NN)).astype(LOW)
    r.outputs[block] = output
    if block == 0:
        hat, unused = normalise(output.astype(WIDE))
        r.normed[1, aligned(band * rows, rows), :] = (hat * gains_ref[1, 0:1, :]).astype(LOW)


def backward_pass(block, schedule, moves, lengths, gains_ref, spill, r, begin_early, begin_late):
    tick = schedule.tick
    rows, width = r.moved.shape
    total = r.kv.shape[0]
    fan = r.hidden.shape[1]
    head_size = width // HEADS
    group_width = GROUP * head_size
    groups = width // group_width
    band = band_here()
    lane_head = head_lanes(rows, head_size)
    chunks = key_chunks(total // rows, rows)
    normed_all = r.normed.at[block]
    matrices = r.late_matrices.at[block]
    early = r.early_matrices
    gain_terms = r.small.at[STEPS]

    def reload(group, number):
        at = pl.ds(*chunks[number])
        moves.start(("reload", block, group, number), spill.at[group, at], r.weights.at[at])

    order = tuple(reversed(range(groups)))
    grad = r.grads[block]
    grad_hidden = product(grad, early[fan : 2 * fan], NT)
    grad_up = (grad_hidden * r.slope[...].astype(WIDE)).astype(LOW)
    early[fan : 2 * fan] = product(r.hidden[...], grad, TN).astype(LOW)
    tick(2.0)
    hat, inverse = normalise(r.middle[...])
    second = (hat * gains_ref[block, 1:2, :]).astype(LOW)
    grad_second = None
    for number in range(fan // width):
        here = slice(number * width, (number + 1) * width)
        piece = product(grad_up[:, here], early[here], NT)
        grad_second = piece if grad_second is None else grad_second + piece
    for number in range(fan // width):
        here = slice(number * width, (number + 1) * width)
        early[here] = product(second, grad_up[:, here], TN).astype(LOW)
    tick(4.0)
    gain_terms[2 * block + 1 : 2 * block + 2, :] = jnp.sum(grad_second * hat, axis=0, keepdims=True)
    grad_middle = grad.astype(WIDE) + normalise_back(
        hat, inverse, gains_ref[block, 1:2, :], grad_second
    )
    r.middle_grad[...] = grad_middle
    grad_branch = grad_middle.astype(LOW)
    positions = band * rows + lax.broadcasted_iota(jnp.int32, (rows, 1), 0)
    keep_rows = (segments(lengths, positions) < 3).astype(WIDE)
    grad_attended = product(grad_branch, early[2 * fan :], NT) * keep_rows
    low = (r.attended[...] * keep_rows).astype(LOW)
    early[2 * fan :] = product(low, grad_branch, TN).astype(LOW)
    begin_early()
    tick(5.5)
    scaled = (grad_attended * r.inverse[...]).astype(LOW)
    ones = jnp.ones((8, group_width), LOW)
    deltas = []
    for group in range(groups):
        lanes = slice(group * group_width, (group + 1) * group_width)
        stack = stack_heads(scaled[:, lanes], lane_head)
        r.grad_stack[group] = stack
        dots = stack.astype(WIDE) * jnp.concatenate([r.attended[:, lanes]] * GROUP, axis=0)
        high = dots.astype(LOW)
        rest = (dots - high.astype(WIDE)).astype(LOW)
        deltas.append((product(ones, high, NT) + product(ones, rest, NT))[0:1])
    tick(7.0)
    query_grads = [None] * groups
    for turn, group in enumerate(order):
        lanes = slice(group * group_width, (group + 1) * group_width)
        value_lanes = slice(width + group * group_width, width + (group + 1) * group_width)
        collected = None
        for number, (start, size) in enumerate(chunks):
            base = 7.0 + 10.0 * turn + 2.0 * number
            at = slice(start, start + size)
            if turn > 0:
                moves.wait(("reload", block, group, number))
            low = r.weights[at]
            grad_weights = product(r.kv[at, value_lanes], r.grad_stack[group], NT)
            grad_scores = (low.astype(WIDE) * (grad_weights - deltas[group])).astype(LOW)
            r.kv[at, value_lanes] = product(low, r.grad_stack[group], NN).astype(LOW)
            piece = product(grad_scores, r.kv[at, lanes], TN)
            collected = piece if collected is None else collected + piece
            r.kv[at, lanes] = product(grad_scores, r.query_stack[group], NN).astype(LOW)
            if turn + 1 < groups:
                reload(order[turn + 1], number)
            tick(base + 1.9)
        query_grads[group] = unstack_heads(collected, lane_head, rows)
    query_grad = (jnp.concatenate(query_grads, axis=1) * head_size ** (-0.5)).astype(LOW)
    tick(27.5)
    here = aligned(band * rows, rows)
    own = normed_all[here, :]
    r.late_terms[:width] = product(own, query_grad, TN).astype(LOW)
    for part in range(2):
        r.late_terms[(part + 1) * width : (part + 2) * width] = product(
            normed_all[...], r.kv[:, part * width : (part + 1) * width], TN
        ).astype(LOW)
    begin_late()
    tick(31.0)
    query_part = product(query_grad, matrices[:width], NT)
    r.query_grad[...] = query_part
    gain_row = jnp.sum(query_part * own.astype(WIDE), axis=0, keepdims=True)
    for start, size in chunks:
        at = slice(start, start + size)
        normed_grad = product(r.kv[at, :width], matrices[width : 2 * width], NT) + product(
            r.kv[at, width:], matrices[2 * width :], NT
        )
        piece = normed_all[at].astype(WIDE)
        gain_row = gain_row + jnp.sum(normed_grad * piece, axis=0, keepdims=True)
        normed_all[at] = normed_grad.astype(LOW)
    gain_terms[2 * block : 2 * block + 1, :] = gain_row / gains_ref[block, 0:1, :]


def inputs_back(block, inputs_ref, gains_ref, r, summed):
    hat, inverse = normalise(inputs_ref[...].astype(WIDE))
    return (
        r.middle_grad[...]
        + normalise_back(hat, inverse, gains_ref[block, 0:1, :], summed + r.query_grad[...])
    ).astype(LOW)


LATE = (512, 512, 512)
EARLY = (1536, 1536, 1536)


class Holder:
    pass


def scratch_plan(rows, width, total, fan):
    groups = HEADS // GROUP
    gw = width // groups
    stacked = GROUP * rows
    plan = {
        "moved": pltpu.VMEM((rows, width), LOW),
        "grads": pltpu.VMEM((2, rows, width), LOW),
        "normed": pltpu.VMEM((2, total, width), LOW),
        "late_matrices": pltpu.VMEM((2, 3 * width, width), LOW),
        "early_matrices": pltpu.VMEM((2 * fan + width, width), LOW),
        "late_terms": pltpu.VMEM((3 * width, width), LOW),
        "query_stack": pltpu.VMEM((groups, stacked, gw), LOW),
        "grad_stack": pltpu.VMEM((groups, stacked, gw), LOW),
        "scores": pltpu.VMEM((total, QUERY_LANES), WIDE),
        "weights": pltpu.VMEM((total, stacked), LOW),
        "kv": pltpu.VMEM((total, 2 * width), LOW),
        "attended": pltpu.VMEM((rows, width), WIDE),
        "inverse": pltpu.VMEM((rows, width), WIDE),
        "middle": pltpu.VMEM((rows, width), WIDE),
        "hidden": pltpu.VMEM((rows, fan), LOW),
        "slope": pltpu.VMEM((rows, fan), LOW),
        "outputs": pltpu.VMEM((2, rows, width), LOW),
        "middle_grad": pltpu.VMEM((rows, width), WIDE),
        "query_grad": pltpu.VMEM((rows, width), WIDE),
        "inputs_grad": pltpu.VMEM((2, rows, width), LOW),
        "late_part": pltpu.VMEM((2, sum(LATE) // DEVICES, width), LOW),
        "early_part": pltpu.VMEM((2, sum(EARLY) // DEVICES, width), LOW),
        "small": pltpu.VMEM((2 * STEPS, 8, width), WIDE),
        "small_sems": pltpu.SemaphoreType.DMA((2, STEPS)),
        "home_sems": pltpu.SemaphoreType.DMA((7, 2)),
        "sems": pltpu.SemaphoreType.DMA((64,)),
    }
    return plan


def buffers(rows):
    return [
        Scattering.scratch(rows)[:2],
        Reduction.scratch(LATE, False)[:2],
        Reduction.scratch(EARLY, True)[:2],
    ]


def block_scratch(rows):
    return [
        Gathering.scratch(),
        Reduction.scratch(LATE, False)[2:],
        Reduction.scratch(EARLY, True)[2:],
        Sharing.scratch(LATE),
        Sharing.scratch(EARLY),
        Scattering.scratch(rows)[2:],
    ]


def blocks_kernel(
    lengths, gains_ref, tokens_ref, gen_grad_ref, disc_grad_ref, qkv_hbm, out_hbm, up_hbm, down_hbm,
    gen_out_ref, disc_out_ref, gen_in_ref, disc_in_ref, gen_late_ref, disc_late_ref, gen_early_ref,
    disc_early_ref, gain_total_ref, spill, *refs,
):
    rows, width = tokens_ref.shape
    total = 8 * rows
    fan = up_hbm.shape[2]
    plan = scratch_plan(rows, width, total, fan)
    r = Holder()
    for name, ref in zip(plan, refs):
        setattr(r, name, ref)
    refs = Names(refs[len(plan) :])
    scatter, late, early = refs.share(buffers(rows))
    passes = [refs.share(block_scratch(rows)) for unused in range(2)]
    hbm = (qkv_hbm, out_hbm, up_hbm, down_hbm)
    moves = Moves(r.sems)
    schedule = Schedule()

    announce_home()
    announce([across(*axis) for axis in ORDERS[0]])
    load_late(moves, 0, hbm, r.late_matrices)
    load_early(moves, 0, hbm, r.early_matrices)
    load_late(moves, 1, hbm, r.late_matrices)
    r.small[STEPS] = jnp.zeros((8, width), WIDE)
    meet_with_home(STEPS)
    homes = [
        Homing(source, target, r.home_sems.at[number])
        for number, (source, target) in enumerate(
            [
                (tokens_ref, r.moved),
                (gen_grad_ref, r.grads.at[0]),
                (disc_grad_ref, r.grads.at[1]),
                (r.outputs.at[0], gen_out_ref),
                (r.outputs.at[1], disc_out_ref),
                (r.inputs_grad.at[0], gen_in_ref),
                (r.inputs_grad.at[1], disc_in_ref),
            ]
        )
    ]
    homes[0].start()
    homes[0].wait()
    gatherings = [Gathering(r.normed.at[block], rows, *passes[block][0]) for block in range(2)]
    hat, unused = normalise(r.moved[...].astype(WIDE))
    r.normed[0, aligned(gatherings[0].band * rows, rows), :] = (
        hat * gains_ref[0, 0:1, :]
    ).astype(LOW)
    schedule.stage(9.0)
    schedule.add(GATHER_DUE[0], gatherings[0].tasks())
    homes[1].start()
    homes[2].start()
    schedule.require(gatherings[0].end)
    schedule.stage(27.0)
    forward_pass(0, schedule, moves, lengths, gains_ref, spill, r)

    scatterings = {}
    first_sharing = []

    def begin_after(ready, begin):
        ready()
        begin()

    totals = ((gen_late_ref, gen_early_ref), (disc_late_ref, disc_early_ref))

    def begin_early(block):
        reduction = Reduction(
            EARLY, r.early_matrices, r.early_part.at[block], *early, *passes[block][2], block == 1
        )
        sharing = Sharing(EARLY, r.early_part.at[block], totals[block][1], *passes[block][4])
        steps = reduction.tasks()
        if block == 0:
            first_sharing.append(sharing)
        else:
            steps[0] = functools.partial(begin_after, first_sharing[0].core_began, steps[0])
        schedule.add(EARLY_REDUCE_DUE[block], steps)
        schedule.add(EARLY_SHARE_DUE[block], sharing.tasks())
        if block == 0:

            def refill():
                reduction.release()
                load_early(moves, 1, hbm, r.early_matrices)

            schedule.add(EARLY_REDUCE_DUE[0][7:8], [refill])

    def begin_late(block):
        reduction = Reduction(LATE, r.late_terms, r.late_part.at[block], *late, *passes[block][1])
        sharing = Sharing(LATE, r.late_part.at[block], totals[block][0], *passes[block][3])
        schedule.add(LATE_REDUCE_DUE[block], reduction.tasks())
        schedule.add(LATE_SHARE_DUE[block], sharing.tasks())

    def begin_scatter(block):
        inputs_ref = r.moved if block == 0 else r.outputs.at[0]

        def finish(summed):
            r.inputs_grad[block] = inputs_back(block, inputs_ref, gains_ref, r, summed)

        scatterings[block] = Scattering(
            r.normed.at[block], *scatter, *passes[block][5], rows, finish
        )
        schedule.add(SCATTER_DUE[block], scatterings[block].tasks())
        schedule.add(HOME_DUE[2 + block], homes[5 + block].tasks())

    homes[1].wait()
    homes[2].wait()
    schedule.add(GATHER_DUE[1], gatherings[1].tasks())
    schedule.add(HOME_DUE[0], homes[3].tasks())
    schedule.stage(49.0)
    backward_pass(
        0, schedule, moves, lengths, gains_ref, spill, r,
        functools.partial(begin_early, 0), functools.partial(begin_late, 0),
    )
    begin_scatter(0)
    schedule.stage(83.0)
    schedule.require(gatherings[1].end)
    forward_pass(1, schedule, moves, lengths, gains_ref, spill, r)
    schedule.require(scatterings[0].third)
    schedule.add(HOME_DUE[1], homes[4].tasks())
    schedule.stage(105.0)
    backward_pass(
        1, schedule, moves, lengths, gains_ref, spill, r,
        functools.partial(begin_early, 1), functools.partial(begin_late, 1),
    )
    begin_scatter(1)
    small = SmallSum(gain_total_ref, r.small, r.small_sems)
    schedule.add([139.0 + 0.006 * step for step in range(1 + STEPS)], small.tasks())
    schedule.drain()


def run_blocks(lengths, gains, tokens, gen_grad, disc_grad, matrices):
    rows, width = tokens.shape
    total = 8 * rows
    fan = matrices[2].shape[2]
    shape = jax.ShapeDtypeStruct
    scratch = list(scratch_plan(rows, width, total, fan).values())
    scratch += flat(buffers(rows)) + flat(block_scratch(rows)) * 2
    return pl.pallas_call(
        blocks_kernel,
        out_shape=[shape((rows, width), LOW)] * 4
        + [shape((sum(LATE), width), LOW)] * 2
        + [shape((sum(EARLY), width), LOW)] * 2
        + [
            shape((8, width), WIDE),
            shape((HEADS // GROUP - 1, total, GROUP * rows), LOW),
        ],
        in_specs=[scalars, whole] + [apart] * 7,
        out_specs=[apart] * 8 + [whole, apart],
        scratch_shapes=scratch,
        compiler_params=settings(1),
        cost_estimate=cost(80e9),
        name="blocks",
    )(lengths, gains, tokens, gen_grad, disc_grad, *matrices)[:9]


def emit_kernel(
    late_refs, early_refs, small_refs, out_refs, small_out_refs, read, written, sems, *small_held
):
    width = read.shape[2]
    qkv_ref, out_ref, up_ref, down_ref = out_refs
    items = []
    for block, (late, early) in enumerate(zip(late_refs, early_refs, strict=True)):
        for target, source, at, count in (
            (qkv_ref, late, 0, qkv_ref.shape[2] // width),
            (up_ref, early, 0, up_ref.shape[2] // width),
            (out_ref, early, up_ref.shape[2] + down_ref.shape[1], 1),
        ):
            for number in range(count):
                items.append(
                    (
                        source.at[pl.ds(at + number * width, width)],
                        target.at[block, :, pl.ds(number * width, width)],
                    )
                )
        for number in range(down_ref.shape[1] // width):
            items.append(
                (
                    early.at[pl.ds(up_ref.shape[2] + number * width, width)],
                    down_ref.at[block, pl.ds(number * width, width)],
                )
            )
    slots = read.shape[0]
    small_loads, small_stores = (
        [
            pltpu.make_async_copy(source, target, sems.at[2, number])
            for number, (source, target) in enumerate(zip(sources, targets, strict=True))
        ]
        for sources, targets in ((small_refs, small_held), (small_held, small_out_refs))
    )
    for load in small_loads:
        load.start()
    loads = [
        pltpu.make_async_copy(source, read.at[number % slots], sems.at[0, number % slots])
        for number, (source, unused) in enumerate(items)
    ]
    stores = [
        pltpu.make_async_copy(written.at[number % slots], target, sems.at[1, number % slots])
        for number, (unused, target) in enumerate(items)
    ]
    for number in range(slots):
        loads[number].start()
    for load, store in zip(small_loads, small_stores, strict=True):
        load.wait()
        store.start()
    for number in range(len(items)):
        loads[number].wait()
        if number >= slots:
            stores[number - slots].wait()
        written[number % slots] = read[number % slots].astype(WIDE)
        stores[number].start()
        if number + slots < len(items):
            loads[number + slots].start()
    for store in stores[-slots:]:
        store.wait()
    for store in small_stores:
        store.wait()


def run_emit(lates, earlies, small, width, fan):
    shape = jax.ShapeDtypeStruct
    count = len(small)
    slots = 24

    def kernel(*refs):
        names = Names(refs)
        late_refs, early_refs, small_refs = names.share([lates, earlies, small])
        small_out, out_refs = (names.take(count), names.take(4))
        emit_kernel(late_refs, early_refs, small_refs, out_refs, small_out, *names.refs)

    return pl.pallas_call(
        kernel,
        out_shape=[shape(item.shape, item.dtype) for item in small]
        + [
            shape((2, width, 3 * width), WIDE),
            shape((2, width, width), WIDE),
            shape((2, width, fan), WIDE),
            shape((2, fan, width), WIDE),
        ],
        in_specs=[apart] * (4 + count),
        out_specs=[apart] * (4 + count),
        scratch_shapes=[
            pltpu.VMEM((slots, width, width), LOW),
            pltpu.VMEM((slots, width, width), WIDE),
            pltpu.SemaphoreType.DMA((3, max(slots, count))),
        ]
        + [pltpu.VMEM(item.shape, item.dtype) for item in small],
        compiler_params=settings(None),
        cost_estimate=cost(1e9),
        name="emit_part",
    )(*lates, *earlies, *small)


def local_kernels(
    tokens,
    norm_gains,
    qkv_weight,
    out_weight,
    up_weight,
    down_weight,
    gen_cotangent,
    disc_cotangent,
    seg_lengths,
):
    size = lax.axis_size("seq")
    swap = (0, 2, 1, 3)
    pairs = [
        (batch * size + seq, swap[seq // 2] * size + 2 * swap[batch] + seq % 2)
        for batch in range(lax.axis_size("batch"))
        for seq in range(size)
    ]
    lengths = lax.ppermute(seg_lengths, ("batch", "seq"), pairs)
    *outs, gen_late, disc_late, gen_early, disc_early, gain_sums = run_blocks(
        lengths,
        norm_gains,
        tokens[0],
        gen_cotangent[0],
        disc_cotangent[0],
        (qkv_weight, out_weight, up_weight, down_weight),
    )
    *outs, gain_sums, qkv_grad, out_grad, up_grad, down_grad = run_emit(
        (gen_late, disc_late),
        (gen_early, disc_early),
        (*outs, gain_sums),
        up_weight.shape[1],
        up_weight.shape[2],
    )
    return (
        *(out[None] for out in outs),
        gain_sums[:4].reshape(2, 2, -1),
        qkv_grad,
        out_grad,
        up_grad,
        down_grad,
    )


def solution(mesh):
    placed = (
        P("batch", "seq", None),
        P(),
        P(),
        P(),
        P(),
        P(),
        P("batch", "seq", None),
        P("batch", "seq", None),
        P("batch", None),
    )
    planes = dict(mesh.shape) == {"batch": 4, "seq": 8}
    return jax.shard_map(
        local_kernels if planes else local_scan,
        mesh=mesh,
        in_specs=placed,
        out_specs=(
            P("batch", "seq", None),
            P("batch", "seq", None),
            P("batch", "seq", None),
            P("batch", "seq", None),
            P(),
            P(),
            P(),
            P(),
            P(),
        ),
        check_vma=False,
    )
```
